32 devices in a mesh: seq: 4 (over y, x), dp: 8 (over z, core).
Axes of the slice: x: 2, y: 2, z: 4, core: 2. Of those that a mesh axis runs over, the one named last changes fastest.
Arguments:
- inputs: bfloat16 [32, 1024, 512], P('dp', 'seq'), may hold values from -6 to 6
- cotangent: bfloat16 [32, 1024, 512], P('dp', 'seq'), may hold values from -6 to 6
- timestep: int32 [32], P('dp'), may hold values from 0 to 1023
- unmask_order: int32 [32, 1024], P('dp', 'seq'), may hold values from 0 to 1023, each once within a row
- mask_embed: float32 [512], replicated, may hold values from -5 to 5
- ln1_gain: float32 [512], replicated, may hold values from 0.5 to 1.5
- weight_qkv: bfloat16 [512, 1536], P('dp'), may hold values from -0.25 to 0.25
- weight_out: bfloat16 [512, 512], P('dp'), may hold values from -6 to 6
- ln2_gain: float32 [512], replicated, may hold values from 0.5 to 1.5
- weight_up: bfloat16 [512, 2048], P('dp'), may hold values from -0.25 to 0.25
- weight_down: bfloat16 [2048, 512], P('dp'), may hold values from -0.125 to 0.125
Outputs:
- outputs: bfloat16 [32, 1024, 512], P('dp', 'seq')
- grad_inputs: bfloat16 [32, 1024, 512], P('dp', 'seq')
- grad_mask_embed: float32 [512], P('dp')
- grad_ln1_gain: float32 [512], P('dp')
- grad_weight_qkv: float32 [512, 1536], P('dp', 'seq')
- grad_weight_out: float32 [512, 512], P('dp', 'seq')
- grad_ln2_gain: float32 [512], P('dp')
- grad_weight_up: float32 [512, 2048], P('dp', 'seq')
- grad_weight_down: float32 [2048, 512], P('dp', 'seq')
The draws below stay inside these ranges and needn't reach their ends.
Inputs may be any that keep to these rules, and one draw needn't show every extreme that they name: Each row of unmask_order holds every number of 0 to 1023 once.
All inputs are finite; a program needn't handle non-finite values.
Results may differ from the reference program's by a relative error of at most 0.018.
Values may be sent and summed in bfloat16 or wider, within the bound.
No kernel may reach another device: no remote copies, remote signals or barrier semaphores. Data moves between devices by JAX's collectives and lax.ppermute only.
A program may use at most 128 MiB of HBM per device.

```python
import math
import jax
import jax.numpy as jnp
import numpy as np
from jax import lax

D = 512
HEADS = 8
FF = 2048
LEN = 1024
ROWS = 32


def with_ends(drawn, key, least, high):
    shape = drawn.shape
    place = [jax.random.randint(jax.random.fold_in(key, axis), (), 0, shape[axis]) for axis in range(len(shape))]
    drawn = drawn.at[tuple(place)].set(least)
    longest = shape.index(max(shape))
    place[longest] = (place[longest] + 1) % shape[longest]
    return drawn.at[tuple(place)].set(high)


def level_of(rng, dims, cuts, smallest, largest):
    loudness = 1.0
    for position, shards_of in cuts:
        steps = jax.random.uniform(jax.random.fold_in(jax.random.fold_in(rng, 6), position), (shards_of,), jnp.float32, smallest / len(cuts), largest / len(cuts))
        loudness = loudness * jnp.repeat(jnp.exp(steps), dims[position] // shards_of).reshape((-1,) + (1,) * (len(dims) - 1 - position))
    return loudness


def rank_bounds(amount, skew):
    portions = [(1 << 20) // math.isqrt(rank ** skew) + 1 for rank in range(1, amount + 1)]
    scale = 1 + sum(portions) // (1 << 30)
    return np.cumsum(np.array([max(1, weight // scale) for weight in portions]))


def skewed_ids(stream_key, dims, count, skew):
    grid = rank_bounds(count, skew)
    pick = jax.random.randint(jax.random.fold_in(stream_key, 1), dims, 0, int(grid[count - 1]))
    rank = jnp.searchsorted(jnp.asarray(grid, jnp.int32), pick, side="right")
    return jax.random.permutation(jax.random.fold_in(stream_key, 2), count)[rank].astype(jnp.int32)


def gaussian(stream_key, extent, scale, limit, shards=(), dtype=jnp.bfloat16):
    drawn = scale * jax.random.normal(stream_key, extent, jnp.float32)
    if shards:
        drawn = drawn * level_of(stream_key, extent, shards, -0.22, 0.18)
    return jnp.clip(drawn, -limit, limit).astype(dtype)


def setup_inputs(seed: int = 0) -> dict:
    arg_keys = jax.random.split(jax.random.key(seed), 12)
    inputs = gaussian(arg_keys[0], (ROWS, LEN, D), 1.0, 6.0, ((0, 8), (1, 4)))
    cotangent = gaussian(arg_keys[1], (ROWS, LEN, D), 1.0, 6.0, ((0, 8), (1, 4)))
    timestep = with_ends(skewed_ids(arg_keys[2], (ROWS,), LEN, 2), jax.random.fold_in(arg_keys[2], 3), 0, LEN - 1).astype(jnp.int32)
    unmask_order = jax.vmap(lambda own: jax.random.permutation(own, LEN))(jax.random.split(arg_keys[3], ROWS)).reshape((ROWS, LEN)).astype(jnp.int32)
    mask_embed = gaussian(arg_keys[4], (D,), 1.0, 5.0, (), jnp.float32)
    ln1_gain = jnp.clip(1.0 + 0.1 * jax.random.normal(arg_keys[5], (D,), jnp.float32), 0.5, 1.5)
    weight_qkv = gaussian(arg_keys[6], (D, 3 * D), D ** -0.5, 0.25, ((0, 8),))
    weight_out = gaussian(arg_keys[7], (D, D), (max(1, 3 * D // LEN)) ** -0.5, 6.0, ((0, 8),))
    ln2_gain = jnp.clip(1.0 + 0.1 * jax.random.normal(arg_keys[8], (D,), jnp.float32), 0.5, 1.5)
    weight_up = gaussian(arg_keys[9], (D, FF), D ** -0.5, 0.25, ((0, 8),))
    weight_down = gaussian(arg_keys[10], (FF, D), FF ** -0.5, 0.125, ((0, 8),))
    return {"inputs": inputs, "cotangent": cotangent, "timestep": timestep, "unmask_order": unmask_order, "mask_embed": mask_embed, "ln1_gain": ln1_gain, "weight_qkv": weight_qkv, "weight_out": weight_out, "ln2_gain": ln2_gain, "weight_up": weight_up, "weight_down": weight_down}


@jax.custom_vjp
def low(v):
    return lax.optimization_barrier(v.astype(jnp.bfloat16)).astype(jnp.float32)

@jax.custom_vjp
def low_back(v):
    return v

def low_keep(v):
    return (low(v), None)

def low_pass(kept, grad):
    return (grad,)

def back_keep(v):
    return (v, None)

def back_low(kept, grad):
    return (low(grad),)
low.defvjp(low_keep, low_pass)
low_back.defvjp(back_keep, back_low)
EPSILON = 1e-05

def layer_norm(tensor, gain_vec):
    center = tensor - lax.optimization_barrier(jnp.mean(tensor, axis=-1, keepdims=True))
    spread = lax.optimization_barrier(jnp.mean(center * center, axis=-1, keepdims=True))
    return center * lax.rsqrt(spread + EPSILON) * gain_vec

def smooth_gelu(tensor):
    return jax.nn.gelu(tensor, approximate=True)

def attend(queries, key_rows, value_rows):
    span_size, head_count, head_width = queries.shape
    block_len = min(span_size, 512)
    scaling = head_width ** (-0.5)

    @jax.checkpoint
    def single_block(query_block):
        logits = low_back(scaling * jnp.einsum('qhd,khd->hqk', query_block, key_rows, precision=lax.Precision.HIGHEST))
        weights = low(jnp.exp(logits))
        normalizer = lax.optimization_barrier(jnp.sum(weights, axis=-1))
        numerator = low_back(jnp.einsum('hqk,khd->qhd', weights, value_rows, precision=lax.Precision.HIGHEST))
        return numerator / jnp.transpose(normalizer)[:, :, None]
    query_blocks = queries.reshape(span_size // block_len, block_len, head_count, head_width)
    return lax.map(single_block, query_blocks).reshape(span_size, head_count * head_width)

def forward_row(row_input, row_mask, mask_embed, ln1_gain, weight_qkv, weight_out, ln2_gain, weight_up, weight_down):
    span_size, model_width = row_input.shape
    head_width = model_width // HEADS
    hidden = row_input + row_mask[:, None] * mask_embed
    normed_one = low(layer_norm(hidden, ln1_gain))
    projected = low_back(low(jnp.dot(normed_one, weight_qkv, precision=lax.Precision.HIGHEST)))
    queries = projected[:, :model_width].reshape(span_size, HEADS, head_width)
    key_rows = projected[:, model_width:2 * model_width].reshape(span_size, HEADS, head_width)
    value_rows = projected[:, 2 * model_width:].reshape(span_size, HEADS, head_width)
    attended = low(attend(queries, key_rows, value_rows))
    first = hidden + low_back(jnp.dot(attended, weight_out, precision=lax.Precision.HIGHEST))
    normed_two = low(layer_norm(first, ln2_gain))
    raised = low_back(jnp.dot(normed_two, weight_up, precision=lax.Precision.HIGHEST))
    activated = low(smooth_gelu(raised))
    return first + low_back(jnp.dot(activated, weight_down, precision=lax.Precision.HIGHEST))

def reference(inputs, cotangent, timestep, unmask_order, mask_embed, ln1_gain, weight_qkv, weight_out, ln2_gain, weight_up, weight_down):
    masking = (unmask_order <= timestep[:, None]).astype(jnp.float32)
    parameters = (mask_embed.astype(jnp.float32), ln1_gain.astype(jnp.float32), weight_qkv.astype(jnp.float32), weight_out.astype(jnp.float32), ln2_gain.astype(jnp.float32), weight_up.astype(jnp.float32), weight_down.astype(jnp.float32))

    def accumulate(totals, row_data):
        row_input, row_grad, row_mask = row_data

        def row_forward(values_in, embed_vec, gain_one, matrix_qkv, matrix_out, gain_two, matrix_up, matrix_down):
            return forward_row(values_in, row_mask, embed_vec, gain_one, matrix_qkv, matrix_out, gain_two, matrix_up, matrix_down)
        row_output, pullback = jax.vjp(row_forward, row_input.astype(jnp.float32), parameters[0], parameters[1], parameters[2], parameters[3], parameters[4], parameters[5], parameters[6])
        gradients = pullback(row_grad.astype(jnp.float32))
        totals = tuple((running_sum + increment for running_sum, increment in zip(totals, gradients[1:])))
        return (totals, (row_output.astype(jnp.bfloat16), gradients[0].astype(jnp.bfloat16)))
    start_totals = tuple((jnp.zeros_like(param_array) for param_array in parameters))
    totals, (row_outputs, row_grads) = lax.scan(accumulate, start_totals, (inputs, cotangent, masking))
    return (row_outputs, row_grads, totals[0], totals[1], totals[2], totals[3], totals[4], totals[5], totals[6])
```

```python
import functools

import jax
import jax.numpy as jnp
from jax import lax
from jax.experimental import pallas as pl
from jax.experimental.pallas import tpu as pltpu
from jax.sharding import PartitionSpec as P

EPSILON = 1e-05
HEADS = 8
F32 = jnp.float32
BF16 = jnp.bfloat16
VMEM_BYTES = 56 * 2**20


def nn(left, right):
    return jnp.dot(left, right, preferred_element_type=F32)


def nt(left, right):
    return lax.dot_general(left, right, (((1,), (1,)), ((), ())), preferred_element_type=F32)


def params(vmem=VMEM_BYTES):
    return pltpu.CompilerParams(vmem_limit_bytes=vmem)


def cost(flops, bytes_accessed):
    return pl.CostEstimate(
        flops=int(flops), bytes_accessed=int(bytes_accessed), transcendentals=0
    )


def attend_kernel(chunk, q_ref, k_ref, v_ref, out_ref, den_ref):
    count = q_ref.shape[0]
    low = lax.broadcasted_iota(jnp.int32, (1, 128), 1) < 64
    keys = k_ref[...]
    values = v_ref[...]
    one = jnp.ones_like(values)
    values_low = jnp.where(low, values, one)
    values_high = jnp.where(low, one, values)
    for start in range(0, count, chunk):
        q = q_ref[start : start + chunk, :] * jnp.asarray(0.125, BF16)
        zero = jnp.zeros_like(q)
        left = nn(jnp.exp(nt(jnp.where(low, q, zero), keys)).astype(BF16), values_low)
        right = nn(jnp.exp(nt(jnp.where(low, zero, q), keys)).astype(BF16), values_high)
        den = pltpu.roll(jnp.where(low, right, left), 64, 1)
        den_ref[start : start + chunk, :] = den
        out_ref[start : start + chunk, :] = jnp.where(low, left, right) / den


def attend(q_source, kv_source, kv_shift):
    count, span = q_source.shape[0], kv_source.shape[0]
    chunk = min(256, count)
    out = jax.ShapeDtypeStruct((count, 512), F32)
    return pl.pallas_call(
        functools.partial(attend_kernel, chunk),
        grid=(4,),
        in_specs=[
            pl.BlockSpec((count, 128), lambda p: (0, p)),
            pl.BlockSpec((span, 128), lambda p: (0, kv_shift + p)),
            pl.BlockSpec((span, 128), lambda p: (0, kv_shift + 4 + p)),
        ],
        out_specs=[pl.BlockSpec((count, 128), lambda p: (0, p))] * 2,
        out_shape=[out, out],
        compiler_params=params(),
        cost_estimate=cost(16 * count * span * 1024, 7 * 2**20),
        name="attend",
    )(q_source, kv_source, kv_source)


def attend_back_kernel(chunk, q_ref, k_ref, v_ref, s_ref, x_ref, dq_ref, dk_ref, dv_ref):
    count, span = q_ref.shape[0], k_ref.shape[0]
    lane = lax.broadcasted_iota(jnp.int32, (1, 128), 1)
    low = lane < 64
    q = q_ref[...] * jnp.asarray(0.125, BF16)
    scaled = s_ref[...]
    extra = x_ref[...]
    zero = jnp.zeros_like(q)
    q_own = (jnp.where(low, q, zero), jnp.where(low, zero, q))
    s_own = (jnp.where(low, scaled, zero), jnp.where(low, zero, scaled))
    s_with = (jnp.where(low, scaled, extra), jnp.where(low, extra, scaled))
    minus = (
        jnp.where((lane == 64) | (lane == 65), -1.0, 0.0).astype(BF16),
        jnp.where((lane == 0) | (lane == 1), -1.0, 0.0).astype(BF16),
    )
    total = jnp.zeros((128, count), F32)
    for start in range(0, span, chunk):
        keys = k_ref[start : start + chunk, :]
        values = v_ref[start : start + chunk, :]
        none = jnp.zeros_like(keys)
        k_own = (jnp.where(low, keys, none), jnp.where(low, none, keys))
        v_with = (jnp.where(low, values, minus[0]), jnp.where(low, minus[1], values))
        dk = dv = 0.0
        for head in range(2):
            weights = jnp.exp(nt(keys, q_own[head]))
            slopes = (weights * nt(v_with[head], s_with[head])).astype(BF16)
            dv = dv + nn(weights.astype(BF16), s_own[head])
            dk = dk + nn(slopes, q_own[head])
            total = total + nn(k_own[head].T, slopes)
        dk_ref[start : start + chunk, :] = dk.astype(BF16)
        dv_ref[start : start + chunk, :] = dv.astype(BF16)
    dq_ref[...] = (total.T * 0.125).astype(BF16)


def attend_back(q_source, kv_source, kv_shift, scaled, extra):
    count, span = q_source.shape[0], kv_source.shape[0]
    chunk = min(512, span)
    own = pl.BlockSpec((count, 128), lambda p: (0, p))
    far = pl.BlockSpec((span, 128), lambda p: (0, p))
    return pl.pallas_call(
        functools.partial(attend_back_kernel, chunk),
        grid=(4,),
        in_specs=[
            own,
            pl.BlockSpec((span, 128), lambda p: (0, kv_shift + p)),
            pl.BlockSpec((span, 128), lambda p: (0, kv_shift + 4 + p)),
            own,
            own,
        ],
        out_specs=[own, far, far],
        out_shape=[
            jax.ShapeDtypeStruct((count, 512), BF16),
            jax.ShapeDtypeStruct((span, 512), BF16),
            jax.ShapeDtypeStruct((span, 512), BF16),
        ],
        compiler_params=params(),
        cost_estimate=cost(32 * count * span * 1024, 8 * 2**20),
        name="attend_back",
    )(q_source, kv_source, kv_source, scaled, extra)


def norm_parts(tensor):
    center = tensor - jnp.mean(tensor, axis=-1, keepdims=True)
    scale = lax.rsqrt(jnp.mean(center * center, axis=-1, keepdims=True) + EPSILON)
    return center * scale, scale


def norm_back(q, normed, scale):
    return scale * (
        q - jnp.mean(q, axis=-1, keepdims=True) - normed * jnp.mean(q * normed, axis=-1, keepdims=True)
    )


def feed_kernel(
    hidden_ref,
    att_ref,
    den_ref,
    cot_ref,
    gain_ref,
    w_out_ref,
    w_up_ref,
    w_down_ref,
    out_ref,
    att_bf_ref,
    normed_ref,
    act_ref,
    raise_ref,
    first_ref,
    branch_ref,
    scaled_ref,
    extra_ref,
    gain_sum_ref,
):
    step = pl.program_id(0)
    att = att_ref[...]
    den = den_ref[...]
    cot = cot_ref[...]
    gain = gain_ref[...]
    att_bf = att.astype(BF16)
    att_bf_ref[...] = att_bf
    first = hidden_ref[...] + nn(att_bf, w_out_ref[...])
    normed, scale = norm_parts(first)
    normed_two = (normed * gain).astype(BF16)
    normed_ref[...] = normed_two
    total = first
    back = jnp.zeros_like(first)
    for start in range(0, w_up_ref.shape[1], 512):
        stop = start + 512
        up = w_up_ref[:, start:stop]
        down = w_down_ref[start:stop, :]
        v = nn(normed_two, up)
        square = v * v
        t = jnp.tanh(v * (0.7978845608028654 + 0.035677408136300125 * square))
        half = 0.5 + 0.5 * t
        act = (v * half).astype(BF16)
        slope = half + v * (0.5 - 0.5 * t * t) * (
            0.7978845608028654 + 0.10703222440890037 * square
        )
        act_ref[:, start:stop] = act
        total = total + nn(act, down)
        grad_raised = (nt(cot, down) * slope).astype(BF16)
        raise_ref[:, start:stop] = grad_raised
        back = back + nt(grad_raised, up)
    out_ref[...] = total.astype(BF16)

    @pl.when(step == 0)
    def _():
        gain_sum_ref[...] = jnp.zeros_like(gain_sum_ref)

    gain_sum_ref[...] += jnp.sum(back * normed, axis=0, keepdims=True)
    grad_first = cot.astype(F32) + norm_back(back * gain, normed, scale)
    first_ref[...] = grad_first
    branch = grad_first.astype(BF16)
    branch_ref[...] = branch
    ratio = nt(branch, w_out_ref[...]) / den
    scaled_ref[...] = ratio.astype(BF16)
    row = lax.broadcasted_iota(jnp.int32, (128, 128), 0)
    col = lax.broadcasted_iota(jnp.int32, (128, 128), 1)
    swap = jnp.where((row < 64) != (col < 64), 1.0, 0.0).astype(BF16)
    even = lax.broadcasted_iota(jnp.int32, (1, 128), 1) % 2 == 0
    product = ratio * att
    coarse = product.astype(BF16)
    fine = (product - coarse.astype(F32)).astype(BF16)
    for start in range(0, 512, 128):
        offset = nn(coarse[:, start : start + 128], swap) + nn(fine[:, start : start + 128], swap)
        upper = offset.astype(BF16)
        lower = (offset - upper.astype(F32)).astype(BF16)
        extra_ref[:, start : start + 128] = jnp.where(even, upper, lower)


def feed(hidden, att, den, cot, gain, w_out, w_up, w_down):
    count, width = hidden.shape
    raised = w_up.shape[1]
    chunk = min(256, count)
    blk = pl.BlockSpec((chunk, width), lambda i: (i, 0))
    wide = pl.BlockSpec((chunk, raised), lambda i: (i, 0))

    def whole(shape):
        return pl.BlockSpec(shape, lambda i: (0, 0), pipeline_mode=pl.Buffered(1))

    def sds(cols, dtype):
        return jax.ShapeDtypeStruct((count, cols), dtype)

    return pl.pallas_call(
        feed_kernel,
        grid=(count // chunk,),
        in_specs=[
            blk,
            blk,
            blk,
            blk,
            whole((1, width)),
            whole((width, width)),
            whole((width, raised)),
            whole((raised, width)),
        ],
        out_specs=[blk, blk, blk, wide, wide, blk, blk, blk, blk, whole((1, width))],
        out_shape=[
            sds(width, BF16),
            sds(width, BF16),
            sds(width, BF16),
            sds(raised, BF16),
            sds(raised, BF16),
            sds(width, F32),
            sds(width, BF16),
            sds(width, BF16),
            sds(width, BF16),
            jax.ShapeDtypeStruct((1, width), F32),
        ],
        compiler_params=params(),
        cost_estimate=cost(10 * 2**30, 30 * 2**20),
        name="feed",
    )(hidden, att, den, cot, gain, w_out, w_up, w_down)


def product_kernel(blocks, own_ref, left_ref, right_ref, out_ref, turned):
    @pl.when(pl.program_id(0) == 0)
    def _():
        turned[...] = left_ref[...].T

    result = nn(turned[...], right_ref[...]).astype(BF16)
    rows = result.shape[0] // blocks
    for block in range(blocks):
        piece = result[block * rows : (block + 1) * rows, :]
        if out_ref.shape[0] == 2:
            core = (block % 2) ^ own_ref[2]
            out_ref[core, 0, (block // 2) ^ own_ref[1]] = piece
        else:
            out_ref[0, block ^ own_ref[0], 0] = piece


def grad_pieces(own, left, right, seq_count, dp_count, flipped):
    count, left_cols = left.shape
    right_cols = right.shape[1]
    z_count = dp_count // 2
    left_blocks, right_blocks = (seq_count, dp_count) if flipped else (dp_count, seq_count)
    rows, cols = left_cols // left_blocks, right_cols // right_blocks
    if cols % 128 or rows % 16:
        whole = lax.dot_general(
            left, right, (((0,), (0,)), ((), ())), preferred_element_type=F32
        ).astype(BF16)
        whole = whole.reshape(left_blocks, rows, right_blocks, cols)
        whole = jnp.transpose(whole, (0, 2, 1, 3) if flipped else (2, 0, 1, 3))
        whole = whole.reshape(seq_count, z_count, 2, rows, cols)
        whole = jnp.take(whole, jnp.arange(seq_count) ^ own[0], axis=0)
        whole = jnp.take(whole, jnp.arange(z_count) ^ own[1], axis=1)
        whole = jnp.take(whole, jnp.arange(2) ^ own[2], axis=2)
        return jnp.transpose(whole, (2, 0, 1, 3, 4))
    if flipped:
        out_spec = pl.BlockSpec(
            (1, seq_count, 1, rows, cols),
            lambda i, own: ((i % 2) ^ own[2], 0, (i // 2) ^ own[1], 0, 0),
        )
    else:
        out_spec = pl.BlockSpec(
            (2, 1, z_count, rows, cols), lambda i, own: (0, i ^ own[0], 0, 0, 0)
        )
    return pl.pallas_call(
        functools.partial(product_kernel, left_blocks),
        grid_spec=pltpu.PrefetchScalarGridSpec(
            num_scalar_prefetch=1,
            grid=(right_blocks,),
            in_specs=[
                pl.BlockSpec((count, left_cols), lambda i, own: (0, 0)),
                pl.BlockSpec((count, cols), lambda i, own: (0, i)),
            ],
            out_specs=out_spec,
            scratch_shapes=[pltpu.VMEM((left_cols, count), BF16)],
        ),
        out_shape=jax.ShapeDtypeStruct((2, seq_count, z_count, rows, cols), BF16),
        compiler_params=params(),
        cost_estimate=cost(2 * count * left_cols * right_cols, 2 * count * (left_cols + right_cols)),
        name="grad_product",
    )(own, left, right)


def last_kernel(
    hidden_ref, first_ref, gain_ref, mask_ref, dq_ref, dk_ref, dv_ref, w_ref, out_ref, sums_ref
):
    width = hidden_ref.shape[1]
    back = nt(dq_ref[...], w_ref[:, :width])
    back = back + nt(dk_ref[...], w_ref[:, width : 2 * width])
    back = back + nt(dv_ref[...], w_ref[:, 2 * width :])
    normed, scale = norm_parts(hidden_ref[...])
    grad = first_ref[...] + norm_back(back * gain_ref[...], normed, scale)
    out_ref[...] = grad.astype(BF16)

    @pl.when(pl.program_id(0) == 0)
    def _():
        sums_ref[...] = jnp.zeros_like(sums_ref)

    mask = mask_ref[...].astype(BF16)
    coarse = grad.astype(BF16)
    fine = (grad - coarse.astype(F32)).astype(BF16)
    masked = nn(mask, coarse) + nn(mask, fine)
    sums_ref[0:1, :] += masked[0:1, :]
    sums_ref[1:2, :] += jnp.sum(back * normed, axis=0, keepdims=True)


def last(hidden, grad_first, gain, mask, dq, dk, dv, w_qkv):
    count, width = hidden.shape
    chunk = min(256, count)
    blk = pl.BlockSpec((chunk, width), lambda i: (i, 0))

    def whole(shape):
        return pl.BlockSpec(shape, lambda i: (0, 0), pipeline_mode=pl.Buffered(1))

    return pl.pallas_call(
        last_kernel,
        grid=(count // chunk,),
        in_specs=[
            blk,
            blk,
            whole((1, width)),
            pl.BlockSpec((8, chunk), lambda i: (0, i)),
            blk,
            blk,
            blk,
            whole(w_qkv.shape),
        ],
        out_specs=[blk, whole((8, width))],
        out_shape=[
            jax.ShapeDtypeStruct((count, width), BF16),
            jax.ShapeDtypeStruct((8, width), F32),
        ],
        compiler_params=params(),
        cost_estimate=cost(6 * count * width * width, 12 * 2**20),
        name="last",
    )(hidden, grad_first, gain, mask, dq, dk, dv, w_qkv)


def swap_along(value, axis, mask):
    count = lax.axis_size(axis)
    return lax.ppermute(value, axis, [(i, i ^ mask) for i in range(count)])


def add_up(values):
    total = values[0].astype(F32)
    for value in values[1:]:
        total = total + value.astype(F32)
    return total


def scatter_sum(pieces):
    seq_count, z_count = pieces.shape[1], pieces.shape[2]
    mine = add_up((pieces[0], swap_along(pieces[1], "dp", 1))).astype(BF16)
    plane = [mine[0]] + [swap_along(mine[j], "seq", j) for j in range(1, seq_count)]
    plane = add_up(plane).astype(BF16)
    line = [plane[0]] + [swap_along(plane[j], "dp", 2 * j) for j in range(1, z_count)]
    return add_up(line)


def vector_sum(vectors, own):
    seq_count, dp_count = lax.axis_size("seq"), lax.axis_size("dp")
    total = add_up([vectors] + [swap_along(vectors, "seq", j) for j in range(1, seq_count)])
    total = add_up([total] + [swap_along(total, "dp", 2 * j) for j in range(1, dp_count // 2)])
    total = total + swap_along(total, "dp", 1)
    width = vectors.shape[1] // dp_count
    return lax.dynamic_slice_in_dim(total, lax.axis_index("dp") * width, width, 1)


def per_device(
    inputs,
    cotangent,
    timestep,
    unmask_order,
    mask_embed,
    ln1_gain,
    weight_qkv,
    weight_out,
    ln2_gain,
    weight_up,
    weight_down,
):
    rows, segment, width = inputs.shape
    seq_count, dp_count = lax.axis_size("seq"), lax.axis_size("dp")
    outer = seq_count // rows
    place = lax.axis_index("seq")
    dp_place = lax.axis_index("dp")
    row = place % rows
    own = jnp.stack([place, dp_place // 2, dp_place % 2]).astype(jnp.int32)

    def to_rows(value):
        parts = [
            lax.dynamic_index_in_dim(value, row ^ j, 0, keepdims=False) for j in range(rows)
        ]
        return [parts[0]] + [swap_along(parts[j], "seq", j) for j in range(1, rows)]

    def from_rows(value):
        parts = [value[j * segment : (j + 1) * segment] for j in range(rows)]
        parts = [parts[0]] + [swap_along(parts[j], "seq", j) for j in range(1, rows)]
        bit = 1
        while bit < rows:
            odd = (row & bit) != 0
            parts = [jnp.where(odd, parts[j ^ bit], parts[j]) for j in range(rows)]
            bit *= 2
        return jnp.stack(parts)

    masked = (unmask_order <= timestep[:, None]).astype(F32)
    mask_row = jnp.concatenate(to_rows(masked))
    block = jnp.concatenate(to_rows(inputs)).astype(F32)
    cot = jnp.concatenate(to_rows(cotangent))
    whole_qkv = lax.all_gather(weight_qkv, "dp", axis=0, tiled=True)
    whole_up = lax.all_gather(
        jnp.concatenate((weight_out, weight_up), axis=1), "dp", axis=0, tiled=True
    )
    whole_down = lax.all_gather(weight_down, "dp", axis=0, tiled=True)
    whole_out, whole_up = whole_up[:, :width], whole_up[:, width:]

    hidden = block + mask_row[:, None] * mask_embed
    normed = norm_parts(hidden)[0]
    normed_one = (normed * ln1_gain).astype(BF16)
    projected = nn(normed_one, whole_qkv).astype(BF16)
    if outer > 1:
        groups = [[j * rows + i for j in range(outer)] for i in range(rows)]
        far = lax.all_gather(
            projected[:, width:], "seq", axis=0, tiled=True, axis_index_groups=groups
        )
        shift = 0
    else:
        far, shift = projected, 4
    attended, denominators = attend(projected, far, shift)
    (
        outputs,
        attended_bf,
        normed_two,
        activated,
        grad_raised,
        grad_first,
        grad_branch,
        scaled,
        extra,
        sum_gain_two,
    ) = feed(
        hidden,
        attended,
        denominators,
        cot,
        ln2_gain[None, :],
        whole_out,
        whole_up,
        whole_down,
    )
    result = from_rows(outputs)
    pieces = functools.partial(grad_pieces, own, seq_count=seq_count, dp_count=dp_count)
    pieces_down = pieces(cot, activated, flipped=True)
    pieces_up = pieces(normed_two, grad_raised, flipped=False)
    pieces_out = pieces(attended_bf, grad_branch, flipped=False)
    dq, dk, dv = attend_back(projected, far, shift, scaled, extra)
    if outer > 1:
        both = jnp.concatenate((dk, dv), axis=1)
        both = lax.psum_scatter(
            both, "seq", scatter_dimension=0, tiled=True, axis_index_groups=groups
        )
        dk, dv = both[:, :width], both[:, width:]
    pieces_qkv = pieces(normed_one, jnp.concatenate((dq, dk, dv), axis=1), flipped=False)
    mask_rows = jnp.broadcast_to(mask_row[None, :], (8, mask_row.shape[0]))
    grad_hidden, sums = last(
        hidden, grad_first, ln1_gain[None, :], mask_rows, dq, dk, dv, whole_qkv
    )
    grad_inputs = from_rows(grad_hidden)
    vectors = vector_sum(
        jnp.concatenate((sums[0:2], sum_gain_two, jnp.zeros((5, width), F32)), axis=0), own
    )
    return (
        result,
        grad_inputs,
        vectors[0],
        vectors[1],
        scatter_sum(pieces_qkv),
        scatter_sum(pieces_out),
        vectors[2],
        scatter_sum(pieces_up),
        scatter_sum(pieces_down).T,
    )


def solution(mesh):
    in_specs = (
        P("dp", "seq", None),
        P("dp", "seq", None),
        P("dp"),
        P("dp", "seq"),
        P(),
        P(),
        P("dp", None),
        P("dp", None),
        P(),
        P("dp", None),
        P("dp", None),
    )
    out_specs = (
        P("dp", "seq", None),
        P("dp", "seq", None),
        P("dp"),
        P("dp"),
        P("dp", "seq"),
        P("dp", "seq"),
        P("dp"),
        P("dp", "seq"),
        P("dp", "seq"),
    )
    return jax.shard_map(
        per_device, mesh=mesh, in_specs=in_specs, out_specs=out_specs, check_vma=False
    )
```

```python
import functools

import jax
import jax.numpy as jnp
from jax import lax
from jax.experimental import pallas as pl
from jax.experimental.pallas import tpu as pltpu
from jax.sharding import PartitionSpec as P

EPSILON = 1e-05
HEADS = 8
F32 = jnp.float32
BF16 = jnp.bfloat16
LIGHT = 2**20


def nn(left, right):
    return jnp.dot(left, right, preferred_element_type=F32)


def nt(left, right):
    return lax.dot_general(left, right, (((1,), (1,)), ((), ())), preferred_element_type=F32)


def params(vmem):
    return pltpu.CompilerParams(vmem_limit_bytes=vmem * 2**20)


def cost(flops, bytes_accessed):
    return pl.CostEstimate(
        flops=int(flops) // LIGHT, bytes_accessed=int(bytes_accessed) // LIGHT, transcendentals=0
    )


def attend_kernel(chunk, q_ref, k_ref, v_ref, out_ref, den_ref):
    count = q_ref.shape[0]
    pair = pl.program_id(0)
    lane = lax.broadcasted_iota(jnp.int32, (1, 128), 1)
    low = lane < 64
    keys = k_ref[...]
    values = v_ref[...]
    one = jnp.ones_like(values)
    values_low = jnp.where(low, values, one)
    values_high = jnp.where(low, one, values)
    for start in range(0, count, chunk):
        at = slice(start, start + chunk)
        q = q_ref[at, :] * jnp.asarray(0.125, BF16)
        zero = jnp.zeros_like(q)
        left = nn(jnp.exp(nt(jnp.where(low, q, zero), keys)).astype(BF16), values_low)
        right = nn(jnp.exp(nt(jnp.where(low, zero, q), keys)).astype(BF16), values_high)
        swapped = jnp.where(low, right, left)
        den = pltpu.roll(swapped, 64, 1)
        out_ref[at, :] = (jnp.where(low, left, right) / den).astype(BF16)
        first = lane // 16 == 2 * pair
        second = lane // 16 == 2 * pair + 1
        mine = jnp.where(
            first, jnp.where(low, den, swapped), jnp.where(low, swapped, den)
        )
        den_ref[at, :] = jnp.where(first | second, mine, den_ref[at, :])


def attend(q_source, kv_source, kv_shift):
    count, span = q_source.shape[0], kv_source.shape[0]
    chunk = min(256, count)
    return pl.pallas_call(
        functools.partial(attend_kernel, chunk),
        grid=(4,),
        in_specs=[
            pl.BlockSpec((count, 128), lambda p: (0, p)),
            pl.BlockSpec((span, 128), lambda p: (0, kv_shift + p)),
            pl.BlockSpec((span, 128), lambda p: (0, kv_shift + 4 + p)),
        ],
        out_specs=[
            pl.BlockSpec((count, 128), lambda p: (0, p)),
            pl.BlockSpec((count, 128), lambda p: (0, 0)),
        ],
        out_shape=[
            jax.ShapeDtypeStruct((count, 512), BF16),
            jax.ShapeDtypeStruct((count, 128), F32),
        ],
        compiler_params=params(20),
        cost_estimate=cost(16 * count * span * 1024, 5 * 2**20),
        name="attend",
    )(q_source, kv_source, kv_source)


def head_pair_back(chunk, q_ref, k_ref, v_ref, s_ref, x_ref, dk_ref, dv_ref):
    count, span = q_ref.shape[0], k_ref.shape[0]
    lane = lax.broadcasted_iota(jnp.int32, (1, 128), 1)
    low = lane < 64
    q = q_ref[...] * jnp.asarray(0.125, BF16)
    scaled = s_ref[...]
    extra = x_ref[...]
    zero = jnp.zeros_like(q)
    q_own = (jnp.where(low, q, zero), jnp.where(low, zero, q))
    s_own = (jnp.where(low, scaled, zero), jnp.where(low, zero, scaled))
    s_with = (jnp.where(low, scaled, extra), jnp.where(low, extra, scaled))
    minus = (
        jnp.where((lane == 64) | (lane == 65), -1.0, 0.0).astype(BF16),
        jnp.where((lane == 0) | (lane == 1), -1.0, 0.0).astype(BF16),
    )
    total = jnp.zeros((128, count), F32)
    for start in range(0, span, chunk):
        keys = k_ref[start : start + chunk, :]
        values = v_ref[start : start + chunk, :]
        none = jnp.zeros_like(keys)
        k_own = (jnp.where(low, keys, none), jnp.where(low, none, keys))
        v_with = (jnp.where(low, values, minus[0]), jnp.where(low, minus[1], values))
        dk = dv = 0.0
        for head in range(2):
            weights = jnp.exp(nt(keys, q_own[head]))
            slopes = (weights * nt(v_with[head], s_with[head])).astype(BF16)
            dv = dv + nn(weights.astype(BF16), s_own[head])
            dk = dk + nn(slopes, q_own[head])
            total = total + nn(k_own[head].T, slopes)
        dk_ref[start : start + chunk, :] = dk.astype(BF16)
        dv_ref[start : start + chunk, :] = dv.astype(BF16)
    return (total.T * 0.125).astype(BF16)


def attend_back_kernel(chunk, q_ref, k_ref, v_ref, s_ref, x_ref, dq_ref, dk_ref, dv_ref):
    dq_ref[...] = head_pair_back(chunk, q_ref, k_ref, v_ref, s_ref, x_ref, dk_ref, dv_ref)


def attend_back_half(projected, scaled, extra):
    count, width = scaled.shape

    def at(shift):
        return pl.BlockSpec((count, 128), lambda p: (0, shift + p))

    return pl.pallas_call(
        functools.partial(attend_back_kernel, min(512, count)),
        grid=(2,),
        in_specs=[at(0), at(4), at(8), at(0), at(0)],
        out_specs=[at(0)] * 3,
        out_shape=[jax.ShapeDtypeStruct((count, width // 2), BF16)] * 3,
        compiler_params=params(20),
        cost_estimate=cost(16 * count * count * 1024, 6 * 2**20),
        name="attend_back_half",
    )(projected, projected, projected, scaled, extra)


def attend_back_sum_kernel(
    chunk,
    dp_count,
    own_ref,
    q_ref,
    k_ref,
    v_ref,
    s_ref,
    x_ref,
    normed_ref,
    dq_first,
    dk_first,
    dv_first,
    dq_ref,
    dk_ref,
    dv_ref,
    mine_out,
    other_out,
    normed_t,
    joined,
    grad_ref,
    sem,
):
    step = pl.program_id(0)
    grad_outs = (mine_out, other_out)

    @pl.when(step == 0)
    def _():
        normed_t[...] = normed_ref[...].T

    def weight_part(pair):
        result = nn(normed_t[...], joined[...]).astype(BF16)
        rows = result.shape[0] // dp_count
        per = grad_ref.shape[3]
        for kind in range(3):
            block = pair + 4 * kind
            col, part = (block // per) ^ own_ref[0], block % per
            for d in range(dp_count):
                grad_ref[(d % 2) ^ own_ref[2], col, (d // 2) ^ own_ref[1], part] = result[
                    d * rows : (d + 1) * rows, kind * 128 : (kind + 1) * 128
                ]

    for kind, ref in enumerate((dq_first, dk_first, dv_first)):
        joined[:, kind * 128 : (kind + 1) * 128] = ref[...]
    weight_part(step)
    dq = head_pair_back(chunk, q_ref, k_ref, v_ref, s_ref, x_ref, dk_ref, dv_ref)
    dq_ref[...] = dq
    joined[:, :128] = dq
    joined[:, 128:256] = dk_ref[...]
    joined[:, 256:] = dv_ref[...]
    weight_part(step + 2)

    @pl.when(step == 1)
    def _():
        hand_out(grad_ref, grad_outs, sem)


def attend_back_sum(own, projected, scaled, extra, normed, first_half, seq_count, dp_count):
    count, width = scaled.shape
    pieces = (2, seq_count, dp_count // 2, 12 // seq_count, width // dp_count, 128)

    def at(shift):
        return pl.BlockSpec((count, 128), lambda p, own: (0, shift + p))

    return pl.pallas_call(
        functools.partial(attend_back_sum_kernel, min(512, count), dp_count),
        grid_spec=pltpu.PrefetchScalarGridSpec(
            num_scalar_prefetch=1,
            grid=(2,),
            in_specs=[
                at(2),
                at(6),
                at(10),
                at(2),
                at(2),
                pl.BlockSpec((count, width), lambda p, own: (0, 0)),
                at(0),
                at(0),
                at(0),
            ],
            out_specs=[at(0)] * 3 + [pl.BlockSpec(memory_space=pl.ANY)] * 2,
            scratch_shapes=[
                pltpu.VMEM((width, count), BF16),
                pltpu.VMEM((count, 384), BF16),
                pltpu.VMEM(pieces, BF16),
                pltpu.SemaphoreType.DMA((2,)),
            ],
        ),
        out_shape=[jax.ShapeDtypeStruct((count, width // 2), BF16)] * 3
        + outs_of(pieces, True),
        compiler_params=params(24),
        cost_estimate=cost(20 * count * count * 1024, 10 * 2**20),
        name="attend_back_sum",
    )(own, projected, projected, projected, scaled, extra, normed, *first_half)


def attend_back(q_source, kv_source, scaled, extra):
    count, span = q_source.shape[0], kv_source.shape[0]
    chunk = min(512, span)
    own = pl.BlockSpec((count, 128), lambda p: (0, p))
    far = pl.BlockSpec((span, 128), lambda p: (0, p))
    return pl.pallas_call(
        functools.partial(attend_back_kernel, chunk),
        grid=(4,),
        in_specs=[
            own,
            pl.BlockSpec((span, 128), lambda p: (0, p)),
            pl.BlockSpec((span, 128), lambda p: (0, 4 + p)),
            own,
            own,
        ],
        out_specs=[own, far, far],
        out_shape=[
            jax.ShapeDtypeStruct((count, 512), BF16),
            jax.ShapeDtypeStruct((span, 512), BF16),
            jax.ShapeDtypeStruct((span, 512), BF16),
        ],
        compiler_params=params(40),
        cost_estimate=cost(32 * count * span * 1024, 8 * 2**20),
        name="attend_back",
    )(q_source, kv_source, kv_source, scaled, extra)


def norm_parts(tensor):
    center = tensor - jnp.mean(tensor, axis=-1, keepdims=True)
    scale = lax.rsqrt(jnp.mean(center * center, axis=-1, keepdims=True) + EPSILON)
    return center * scale, scale


def norm_back(q, normed, scale):
    return scale * (
        q - jnp.mean(q, axis=-1, keepdims=True) - normed * jnp.mean(q * normed, axis=-1, keepdims=True)
    )


def place_blocks(own_ref, sources, target, sems):
    copies = []
    for core in range(2):
        source = sources[core]
        by_seq = len(source.shape) == 4
        seq_count = source.shape[0] if by_seq else 1
        z_count, rows, cols = source.shape[-3:]
        by_rows = by_seq and cols == target.shape[1]
        for j in range(seq_count):
            for i in range(z_count):
                block = 2 * (own_ref[1] ^ i) + (own_ref[2] ^ core)
                across = slice(None)
                if by_rows:
                    block = block * seq_count + (own_ref[0] ^ j)
                elif by_seq:
                    across = pl.ds(pl.multiple_of((own_ref[0] ^ j) * cols, cols), cols)
                down = pl.ds(pl.multiple_of(block * rows, rows), rows)
                piece = source.at[j, i] if by_seq else source.at[i]
                copy = pltpu.make_async_copy(piece, target.at[down, across], sems.at[len(copies)])
                copies.append(copy)
    return copies


def fetches(own_ref, refs, target, sems):
    if len(refs) == 2:
        return place_blocks(own_ref, refs, target, sems)
    return [pltpu.make_async_copy(refs[0], target, sems.at[0])]


def launch(copies):
    for copy in copies:
        copy.start()


def finish(copies):
    for copy in copies:
        copy.wait()


def hand_out(held, outs, sems):
    sources = [held] if len(outs) == 1 else [held.at[0], held.at[1]]
    copies = [
        pltpu.make_async_copy(source, out, sems.at[i])
        for i, (source, out) in enumerate(zip(sources, outs))
    ]
    launch(copies)
    finish(copies)


def outs_of(shape, split):
    if split:
        return [jax.ShapeDtypeStruct(shape[1:], BF16)] * 2
    return [jax.ShapeDtypeStruct(shape, BF16)]


def copies_of(parts):
    count = 1
    for size in parts[0].shape[:-2]:
        count *= size
    return max(1, count * len(parts))


def project_kernel(parts, own_ref, hidden_ref, gain_ref, *refs):
    sources, (normed_ref, out_ref, whole_ref, sems) = refs[:parts], refs[parts:]

    @pl.when(pl.program_id(0) == 0)
    def _():
        launch(fetches(own_ref, sources, whole_ref, sems))

    normed = (norm_parts(hidden_ref[...])[0] * gain_ref[...]).astype(BF16)
    normed_ref[...] = normed

    @pl.when(pl.program_id(0) == 0)
    def _():
        finish(fetches(own_ref, sources, whole_ref, sems))

    out_ref[...] = nn(normed, whole_ref[...]).astype(BF16)


def project(own, hidden, gain, parts, cols):
    count, width = hidden.shape
    chunk = min(512, count)

    def rows(cols):
        return pl.BlockSpec((chunk, cols), lambda i, own: (i, 0))

    return pl.pallas_call(
        functools.partial(project_kernel, len(parts)),
        grid_spec=pltpu.PrefetchScalarGridSpec(
            num_scalar_prefetch=1,
            grid=(count // chunk,),
            in_specs=[rows(width), pl.BlockSpec((1, width), lambda i, own: (0, 0))]
            + [pl.BlockSpec(memory_space=pl.ANY)] * len(parts),
            out_specs=[
                rows(width),
                rows(cols),
                pl.BlockSpec((width, cols), lambda i, own: (0, 0)),
            ],
            scratch_shapes=[pltpu.SemaphoreType.DMA((copies_of(parts),))],
        ),
        out_shape=[
            jax.ShapeDtypeStruct((count, width), BF16),
            jax.ShapeDtypeStruct((count, cols), BF16),
            jax.ShapeDtypeStruct((width, cols), BF16),
        ],
        compiler_params=params(16),
        cost_estimate=cost(2 * count * width * cols, 8 * 2**20),
        name="project",
    )(own, hidden, gain, *parts)


def rise_kernel(cfg, own_ref, hidden_ref, att_ref, cot_ref, gain_ref, *refs):
    seq_count, dp_count, split, up_parts, down_parts = cfg
    up_sources, refs = refs[:up_parts], refs[up_parts:]
    down_sources, refs = refs[:down_parts], refs[down_parts:]
    outs = 2 if split else 1
    out_ref, normed_ref, scale_ref, slope_ref, w_up, w_down, *refs = refs
    grad_outs, refs = refs[:outs], refs[outs:]
    (
        act_ref,
        cot_t,
        grad_ref,
        up_sems,
        down_sems,
        out_sem,
    ) = refs
    step = pl.program_id(0)
    chunk, width = hidden_ref.shape
    count, raised = act_ref.shape
    steps = count // chunk

    def tokens():
        at = pl.ds(pl.multiple_of(step * chunk, chunk), chunk)
        first = hidden_ref[...] + nn(att_ref[...], w_up[:, :width])
        normed, scale = norm_parts(first)
        normed_ref[...] = normed
        scale_ref[...] = jnp.broadcast_to(scale, scale_ref.shape)
        normed_two = (normed * gain_ref[...]).astype(BF16)
        cot_t[:, at] = cot_ref[...].T
        total = first
        for start in range(0, raised, 512):
            stop = start + 512
            v = nn(normed_two, w_up[:, width + start : width + stop])
            square = v * v
            t = jnp.tanh(v * (0.7978845608028654 + 0.035677408136300125 * square))
            half = 0.5 + 0.5 * t
            act = (v * half).astype(BF16)
            slope = half + v * (0.5 - 0.5 * t * t) * (
                0.7978845608028654 + 0.10703222440890037 * square
            )
            act_ref[at, start:stop] = act
            slope_ref[:, start:stop] = slope.astype(BF16)
            total = total + nn(act, w_down[start:stop, :])
        out_ref[...] = total.astype(BF16)

    @pl.when(step == 0)
    def _():
        copies = fetches(own_ref, up_sources, w_up, up_sems)
        copies += fetches(own_ref, down_sources, w_down, down_sems)
        launch(copies)
        finish(copies)

    pl.when(step < steps)(tokens)

    @pl.when(step == steps)
    def _():
        if split:
            cols = width // seq_count
            rows = raised // dp_count
            for d in range(dp_count):
                result = nn(cot_t[...], act_ref[:, d * rows : (d + 1) * rows]).astype(BF16)
                for s in range(seq_count):
                    piece = result[s * cols : (s + 1) * cols, :]
                    for part in range(rows // 128):
                        grad_ref[
                            (d % 2) ^ own_ref[2], (d // 2) ^ own_ref[1], s ^ own_ref[0], part
                        ] = piece[:, part * 128 : (part + 1) * 128]
        else:
            for start in range(0, raised, 512):
                grad_ref[:, start : start + 512] = nn(
                    cot_t[...], act_ref[:, start : start + 512]
                ).astype(BF16)
        hand_out(grad_ref, grad_outs, out_sem)


def rise(own, hidden, att, cot, gain, up_parts, down_parts, raised, seq_count, dp_count, split):
    count, width = hidden.shape
    chunk = min(256, count)
    steps = count // chunk

    def rows(cols):
        return pl.BlockSpec((chunk, cols), lambda i, own: (jnp.minimum(i, steps - 1), 0))

    def whole(shape):
        return pl.BlockSpec(shape, lambda i, own: (0, 0), pipeline_mode=pl.Buffered(1))

    anywhere = pl.BlockSpec(memory_space=pl.ANY)
    if split:
        parts = raised // dp_count // 128
        grad_shape = (2, dp_count // 2, seq_count, parts, width // seq_count, 128)
    else:
        grad_shape = (width, raised)
    cfg = (seq_count, dp_count, split, len(up_parts), len(down_parts))
    grads = outs_of(grad_shape, split)
    up_shape, down_shape = (width, width + raised), (raised, width)
    return pl.pallas_call(
        functools.partial(rise_kernel, cfg),
        grid_spec=pltpu.PrefetchScalarGridSpec(
            num_scalar_prefetch=1,
            grid=(steps + 1,),
            in_specs=[rows(width), rows(width), rows(width), whole((1, width))]
            + [anywhere] * (len(up_parts) + len(down_parts)),
            out_specs=[
                rows(width),
                rows(width),
                rows(128),
                rows(raised),
                whole(up_shape),
                whole(down_shape),
            ]
            + [anywhere] * len(grads),
            scratch_shapes=[
                pltpu.VMEM((count, raised), BF16),
                pltpu.VMEM((width, count), BF16),
                pltpu.VMEM(grad_shape, BF16),
                pltpu.SemaphoreType.DMA((copies_of(up_parts),)),
                pltpu.SemaphoreType.DMA((copies_of(down_parts),)),
                pltpu.SemaphoreType.DMA((2,)),
            ],
        ),
        out_shape=[
            jax.ShapeDtypeStruct((count, width), BF16),
            jax.ShapeDtypeStruct((count, width), F32),
            jax.ShapeDtypeStruct((count, 128), F32),
            jax.ShapeDtypeStruct((count, raised), BF16),
            jax.ShapeDtypeStruct(up_shape, BF16),
            jax.ShapeDtypeStruct(down_shape, BF16),
        ]
        + grads,
        compiler_params=params(32),
        cost_estimate=cost(7 * 2**30, 24 * 2**20),
        name="rise",
    )(own, hidden, att, cot, gain, *up_parts, *down_parts)


def fall_kernel(
    cfg,
    own_ref,
    cot_ref,
    slope_ref,
    normed_ref,
    scale_ref,
    att_ref,
    den_ref,
    gain_ref,
    w_up,
    w_down,
    first_ref,
    scaled_ref,
    extra_ref,
    gain_sum_ref,
    *refs,
):
    seq_count, dp_count, split = cfg
    outs = 2 if split else 1
    grad_outs, (raise_ref, normed_t, att_t, branch_ref, grad_ref, out_sem) = refs[:outs], refs[outs:]
    step = pl.program_id(0)
    chunk, width = cot_ref.shape
    count, raised = raise_ref.shape
    steps = count // chunk

    def tokens():
        at = pl.ds(pl.multiple_of(step * chunk, chunk), chunk)
        att = att_ref[...]
        cot = cot_ref[...]
        normed = normed_ref[...]
        gain = gain_ref[...]
        normed_t[:, at] = (normed * gain).astype(BF16).T
        att_t[:, at] = att.T
        back = jnp.zeros((chunk, width), F32)
        for start in range(0, raised, 512):
            stop = start + 512
            grad_raised = (nt(cot, w_down[start:stop, :]) * slope_ref[:, start:stop]).astype(BF16)
            raise_ref[at, start:stop] = grad_raised
            back = back + nt(grad_raised, w_up[:, width + start : width + stop])
        gain_sum_ref[...] += jnp.sum(back * normed, axis=0, keepdims=True)
        grad_first = cot.astype(F32) + norm_back(back * gain, normed, scale_ref[:, :1])
        first_ref[...] = grad_first
        branch = grad_first.astype(BF16)
        branch_ref[at, :] = branch
        inverse = 1.0 / den_ref[...]
        row = lax.broadcasted_iota(jnp.int32, (128, width), 0)
        col = lax.broadcasted_iota(jnp.int32, (128, width), 1)
        spread = jnp.where(row == 16 * (col // 64), 1.0, 0.0).astype(BF16)
        coarse = inverse.astype(BF16)
        fine = (inverse - coarse.astype(F32)).astype(BF16)
        ratio = nt(branch, w_up[:, :width]) * (nn(coarse, spread) + nn(fine, spread))
        scaled_ref[...] = ratio.astype(BF16)
        row = lax.broadcasted_iota(jnp.int32, (128, 128), 0)
        col = lax.broadcasted_iota(jnp.int32, (128, 128), 1)
        swap = jnp.where((row < 64) != (col < 64), 1.0, 0.0).astype(BF16)
        even = lax.broadcasted_iota(jnp.int32, (1, 128), 1) % 2 == 0
        product = ratio * att
        coarse = product.astype(BF16)
        fine = (product - coarse.astype(F32)).astype(BF16)
        for start in range(0, width, 128):
            stop = start + 128
            offset = nn(coarse[:, start:stop], swap) + nn(fine[:, start:stop], swap)
            upper = offset.astype(BF16)
            lower = (offset - upper.astype(F32)).astype(BF16)
            extra_ref[:, start:stop] = jnp.where(even, upper, lower)

    @pl.when(step == 0)
    def _():
        gain_sum_ref[...] = jnp.zeros_like(gain_sum_ref)

    pl.when(step < steps)(tokens)

    @pl.when(step == steps)
    def _():
        if split:
            cols = raised // seq_count
            wide = width // seq_count
            rows = width // dp_count
            for s in range(seq_count):
                result = nn(normed_t[...], raise_ref[:, s * cols : (s + 1) * cols]).astype(BF16)
                for d in range(dp_count):
                    grad_ref[
                        (d % 2) ^ own_ref[2], s ^ own_ref[0], (d // 2) ^ own_ref[1], :, wide:
                    ] = result[d * rows : (d + 1) * rows, :]
            result = nn(att_t[...], branch_ref[...]).astype(BF16)
            for s in range(seq_count):
                for d in range(dp_count):
                    grad_ref[
                        (d % 2) ^ own_ref[2], s ^ own_ref[0], (d // 2) ^ own_ref[1], :, :wide
                    ] = result[d * rows : (d + 1) * rows, s * wide : (s + 1) * wide]
        else:
            grad_ref[:, :width] = nn(att_t[...], branch_ref[...]).astype(BF16)
            for start in range(0, raised, 512):
                grad_ref[:, width + start : width + start + 512] = nn(
                    normed_t[...], raise_ref[:, start : start + 512]
                ).astype(BF16)
        hand_out(grad_ref, grad_outs, out_sem)


def fall(own, cot, slope, normed, scale, att, den, gain, w_up, w_down, seq_count, dp_count, split):
    count, width = cot.shape
    raised = w_down.shape[0]
    chunk = min(256, count)
    steps = count // chunk

    def rows(cols):
        return pl.BlockSpec((chunk, cols), lambda i, own: (jnp.minimum(i, steps - 1), 0))

    def whole(shape):
        return pl.BlockSpec(shape, lambda i, own: (0, 0), pipeline_mode=pl.Buffered(1))

    if split:
        grad_shape = (2, seq_count, dp_count // 2, width // dp_count, (width + raised) // seq_count)
    else:
        grad_shape = (width, width + raised)
    block = rows(width)
    grads = outs_of(grad_shape, split)

    def sds(dtype):
        return jax.ShapeDtypeStruct((count, width), dtype)

    return pl.pallas_call(
        functools.partial(fall_kernel, (seq_count, dp_count, split)),
        grid_spec=pltpu.PrefetchScalarGridSpec(
            num_scalar_prefetch=1,
            grid=(steps + 1,),
            in_specs=[
                block,
                rows(raised),
                block,
                rows(128),
                block,
                rows(128),
                whole((1, width)),
                whole(w_up.shape),
                whole(w_down.shape),
            ],
            out_specs=[
                block,
                block,
                block,
                whole((1, width)),
            ]
            + [pl.BlockSpec(memory_space=pl.ANY)] * len(grads),
            scratch_shapes=[
                pltpu.VMEM((count, raised), BF16),
                pltpu.VMEM((width, count), BF16),
                pltpu.VMEM((width, count), BF16),
                pltpu.VMEM((count, width), BF16),
                pltpu.VMEM(grad_shape, BF16),
                pltpu.SemaphoreType.DMA((2,)),
            ],
        ),
        out_shape=[
            sds(F32),
            sds(BF16),
            sds(BF16),
            jax.ShapeDtypeStruct((1, width), F32),
        ]
        + grads,
        compiler_params=params(32),
        cost_estimate=cost(8 * 2**30, 24 * 2**20),
        name="fall",
    )(own, cot, slope, normed, scale, att, den, gain, w_up, w_down)


def last_kernel(parts, hidden_ref, first_ref, gain_ref, mask_ref, w_ref, *refs):
    grads, (out_ref, sums_ref) = refs[:parts], refs[parts:]
    back = 0.0
    start = 0
    for ref in grads:
        stop = start + ref.shape[1]
        back = back + nt(ref[...], w_ref[:, start:stop])
        start = stop
    normed, scale = norm_parts(hidden_ref[...])
    grad = first_ref[...] + norm_back(back * gain_ref[...], normed, scale)
    out_ref[...] = grad.astype(BF16)

    @pl.when(pl.program_id(0) == 0)
    def _():
        sums_ref[...] = jnp.zeros_like(sums_ref)

    mask = mask_ref[...].astype(BF16)
    coarse = grad.astype(BF16)
    fine = (grad - coarse.astype(F32)).astype(BF16)
    masked = nn(mask, coarse) + nn(mask, fine)
    sums_ref[0:1, :] += masked[0:1, :]
    sums_ref[1:2, :] += jnp.sum(back * normed, axis=0, keepdims=True)


def last(hidden, grad_first, gain, mask, w_qkv, grads):
    count, width = hidden.shape
    chunk = min(256, count)
    blk = pl.BlockSpec((chunk, width), lambda i: (i, 0))

    def whole(shape):
        return pl.BlockSpec(shape, lambda i: (0, 0), pipeline_mode=pl.Buffered(1))

    return pl.pallas_call(
        functools.partial(last_kernel, len(grads)),
        grid=(count // chunk,),
        in_specs=[
            blk,
            blk,
            whole((1, width)),
            pl.BlockSpec((8, chunk), lambda i: (0, i)),
            whole(w_qkv.shape),
        ]
        + [pl.BlockSpec((chunk, g.shape[1]), lambda i: (i, 0)) for g in grads],
        out_specs=[blk, whole((8, width))],
        out_shape=[
            jax.ShapeDtypeStruct((count, width), BF16),
            jax.ShapeDtypeStruct((8, width), F32),
        ],
        compiler_params=params(16),
        cost_estimate=cost(6 * count * width * width, 12 * 2**20),
        name="last",
    )(hidden, grad_first, gain, mask, w_qkv, *grads)


def swap_along(value, axis, mask):
    count = lax.axis_size(axis)
    return lax.ppermute(value, axis, [(i, i ^ mask) for i in range(count)])


def add_up(values):
    total = values[0].astype(F32)
    for value in values[1:]:
        total = total + value.astype(F32)
    return total


def together(*values):
    return lax.optimization_barrier(values)


def from_plane(values):
    return [values[0]] + [swap_along(values[j], "seq", j) for j in range(1, len(values))]


def from_line(values):
    return [values[0]] + [swap_along(values[j], "dp", 2 * j) for j in range(1, len(values))]


def other_core(value):
    return swap_along(value, "dp", 1)


def add_split(left, right):
    return [add_up((left[j], right[j])).astype(BF16) for j in range(left.shape[0])]


def split_first(value):
    return [value[j] for j in range(value.shape[0])]


def halve_line(value):
    half = value.shape[0] // 2
    while half:
        came = swap_along(value[half:], "dp", 2 * half)
        value = add_up((value[:half], came))
        half //= 2
        if half:
            value = value.astype(BF16)
    return value[0]


def gather_line(value):
    return jnp.stack(from_line([value] * (lax.axis_size("dp") // 2)))


def gather_plane(value):
    return jnp.stack(from_plane([value] * lax.axis_size("seq")))


def own_columns(weight):
    cols = weight.shape[1] // lax.axis_size("seq")
    return lax.dynamic_slice_in_dim(weight, lax.axis_index("seq") * cols, cols, 1)


def pieces_of(whole, own, seq_count, dp_count, flipped):
    row_blocks, col_blocks = (seq_count, dp_count) if flipped else (dp_count, seq_count)
    rows, cols = whole.shape[0] // row_blocks, whole.shape[1] // col_blocks
    whole = whole.reshape(row_blocks, rows, col_blocks, cols)
    whole = jnp.transpose(whole, (0, 2, 1, 3) if flipped else (2, 0, 1, 3))
    whole = whole.reshape(seq_count, dp_count // 2, 2, rows, cols)
    whole = jnp.take(whole, jnp.arange(seq_count) ^ own[0], axis=0)
    whole = jnp.take(whole, jnp.arange(dp_count // 2) ^ own[1], axis=1)
    whole = jnp.take(whole, jnp.arange(2) ^ own[2], axis=2)
    return jnp.transpose(whole, (2, 0, 1, 3, 4))


def per_device(
    inputs,
    cotangent,
    timestep,
    unmask_order,
    mask_embed,
    ln1_gain,
    weight_qkv,
    weight_out,
    ln2_gain,
    weight_up,
    weight_down,
):
    rows, segment, width = inputs.shape
    raised = weight_up.shape[1]
    seq_count, dp_count = lax.axis_size("seq"), lax.axis_size("dp")
    outer = seq_count // rows
    split = outer == 1 and (width // seq_count) % 128 == 0 and (width // dp_count) % 16 == 0
    place = lax.axis_index("seq")
    dp_place = lax.axis_index("dp")
    row = place % rows
    own = jnp.stack([place, dp_place // 2, dp_place % 2]).astype(jnp.int32)

    def by_partner(value):
        return [lax.dynamic_index_in_dim(value, row ^ j, 0, keepdims=False) for j in range(rows)]

    def to_rows(value):
        return jnp.concatenate(from_plane(by_partner(value)))

    def to_partners(value):
        return from_plane([value[j * segment : (j + 1) * segment] for j in range(rows)])

    def by_row(parts):
        bit = 1
        while bit < rows:
            odd = (row & bit) != 0
            parts = [jnp.where(odd, parts[j ^ bit], parts[j]) for j in range(rows)]
            bit *= 2
        return jnp.stack(parts)

    masked = (unmask_order <= timestep[:, None]).astype(BF16)
    masked = jnp.pad(masked[:, None, :], ((0, 0), (0, 15), (0, width - segment)))
    came = from_plane(by_partner(jnp.concatenate((inputs, masked), axis=1)))
    block = jnp.concatenate([part[:segment] for part in came]).astype(F32)
    mask_row = jnp.concatenate([part[segment, :segment] for part in came])
    up_and_out = jnp.concatenate((weight_out, weight_up), axis=1)
    if split:
        down_rows = weight_down.shape[0] // seq_count
        own_down = lax.dynamic_slice_in_dim(weight_down, place * down_rows, down_rows, 0)
        own_parts = jnp.concatenate((own_columns(weight_qkv), own_down), axis=1)
        line = gather_line(own_parts)
        line, up_and_out = together(line, up_and_out)
        line_up = from_line([up_and_out] * (dp_count // 2))
        plane_qkv = gather_plane(line[..., : -width])
        line_down = line[..., -width:].reshape(-1, width)
        plane_qkv, line_down, cot = together(plane_qkv, line_down, cotangent)
        parts_qkv = [plane_qkv, other_core(plane_qkv)]
        cot = by_partner(cot)
        cot = from_plane([jnp.concatenate((part, line_down)) for part in cot])
    else:
        cot = from_plane(by_partner(cotangent))
        parts_qkv, parts_up, parts_down = (
            [lax.all_gather(weight, "dp", axis=0, tiled=True)]
            for weight in (weight_qkv, up_and_out, weight_down)
        )

    hidden = block + mask_row.astype(F32)[:, None] * mask_embed
    normed_one, projected, whole_qkv = project(
        own, hidden, ln1_gain[None, :], parts_qkv, 3 * width
    )
    if outer > 1:
        groups = [[j * rows + i for j in range(outer)] for i in range(rows)]
        far = lax.all_gather(
            projected[:, width:], "seq", axis=0, tiled=True, axis_index_groups=groups
        )
        shift = 0
    else:
        far, shift = projected, 4
    attended, denominators = attend(projected, far, shift)
    if split:
        cot, line_up, attended = together(cot, line_up, attended)
        plane_down = jnp.stack([part[segment:] for part in cot])
        plane_down = plane_down.reshape(seq_count, dp_count // 2, -1, width)
        line_up = jnp.stack(line_up)
        parts_up = [line_up, other_core(line_up)]
        parts_down = [plane_down, other_core(plane_down)]
    cot = jnp.concatenate([part[:segment] for part in cot])
    outputs, normed, scale, slope, whole_up, whole_down, *grad_down = rise(
        own,
        hidden,
        attended,
        cot,
        ln2_gain[None, :],
        parts_up,
        parts_down,
        raised,
        seq_count,
        dp_count,
        split,
    )
    result = to_partners(outputs)
    grad_first, scaled, extra, sum_gain_two, *grad_up = fall(
        own,
        cot,
        slope,
        normed,
        scale,
        attended,
        denominators,
        ln2_gain[None, :],
        whole_up,
        whole_down,
        seq_count,
        dp_count,
        split,
    )
    mask_rows = jnp.broadcast_to(mask_row[None, :], (8, mask_row.shape[0]))
    if split:
        grad_down[1] = other_core(grad_down[1])
        grad_down, scaled, grad_up, result = together(grad_down, scaled, grad_up, result)
        line_down = from_line(add_split(*grad_down))
        grad_up[1] = other_core(grad_up[1])
        half = attend_back_half(projected, scaled, extra)
        grad_up, half, line_down[1] = together(grad_up, half, line_down[1])
        plane_up = from_plane(add_split(*grad_up))
        *rest, mine_qkv, other_qkv = attend_back_sum(
            own, projected, scaled, extra, normed_one, half, seq_count, dp_count
        )
        plane_up, line_down, rest, mine_qkv, other_qkv = together(
            plane_up, line_down, rest, mine_qkv, other_qkv
        )
        grads = [part for pair in zip(half, rest) for part in pair]
        both_qkv = (mine_qkv, other_core(other_qkv))
        line_up = add_up(plane_up).astype(BF16)
        z_half = line_up.shape[0] // 2
        line_came = swap_along(line_up[z_half:], "dp", 2 * z_half)
        both_qkv, mask_rows = together(both_qkv, mask_rows)
        tall = width // dp_count
        down = add_up(line_down).astype(BF16).reshape(seq_count, -1, tall, 128)
        mine_qkv = [part.reshape(-1, tall, 128) for part in add_split(*both_qkv)]
        plane_last = from_plane([jnp.concatenate((mine_qkv[j], down[j])) for j in range(seq_count)])
    else:
        dq, dk, dv = attend_back(projected, far, scaled, extra)
        both = jnp.concatenate((dk, dv), axis=1)
        both = lax.psum_scatter(
            both, "seq", scatter_dimension=0, tiled=True, axis_index_groups=groups
        )
        grads = [dq, both]
        grad_qkv = lax.dot_general(
            normed_one,
            jnp.concatenate(grads, axis=1),
            (((0,), (0,)), ((), ())),
            preferred_element_type=F32,
        ).astype(BF16)
        cut = functools.partial(pieces_of, own=own, seq_count=seq_count, dp_count=dp_count)
        (grad_up,), (grad_down,) = grad_up, grad_down
        grad_out, grad_up = (
            cut(part, flipped=False) for part in (grad_up[:, :width], grad_up[:, width:])
        )
        grad_up = jnp.concatenate((grad_out, grad_up), axis=-1)
        grad_qkv = cut(grad_qkv, flipped=False)
        grad_down = cut(grad_down, flipped=True)
        sums = []
        for pieces in (grad_qkv, grad_up, grad_down):
            mine = add_up((pieces[0], other_core(pieces[1]))).astype(BF16)
            plane = add_up(from_plane(split_first(mine))).astype(BF16)
            sums.append(add_up(from_line(split_first(plane))))
        sum_qkv, sum_up, sum_down = sums
        sum_down = sum_down.T
    grad_hidden, sums = last(
        hidden, grad_first, ln1_gain[None, :], mask_rows, whole_qkv, grads
    )
    vectors = jnp.concatenate((sums[0:2], sum_gain_two, jnp.zeros((13, width), F32)), axis=0)
    vectors = vectors + other_core(vectors)
    bit = 1
    while bit < seq_count:
        vectors = vectors + swap_along(vectors, "seq", bit)
        bit *= 2
    if split:
        grad_hidden, vectors, line_came, plane_last = together(
            grad_hidden, vectors, line_came, plane_last
        )
        grad_inputs = to_partners(grad_hidden)
        sum_up = halve_line(add_up((line_up[:z_half], line_came)).astype(BF16))
        plane = add_up(plane_last)
        kinds = mine_qkv[0].shape[0]
        sum_down = plane[kinds:].reshape(-1, width // seq_count, 128)
        sum_down = jnp.transpose(sum_down, (0, 2, 1)).reshape(-1, width // seq_count)
        z_count = dp_count // 2
        plane = plane[:kinds].astype(BF16).reshape((z_count, -1) + plane.shape[1:])
        flat = jnp.transpose(vectors.reshape(16, -1, 128), (1, 0, 2)).astype(BF16)
        flat = jnp.broadcast_to(flat.reshape(1, -1, tall, 128), (z_count, 1, tall, 128))
        line = halve_line(jnp.concatenate((plane, flat), axis=1))
        sum_qkv = jnp.transpose(line[:-1], (1, 0, 2)).reshape(tall, -1)
        vectors = jnp.transpose(line[-1].reshape(-1, 16, 128), (1, 0, 2)).reshape(16, -1)
    else:
        grad_inputs = to_partners(grad_hidden)
        vectors = add_up(from_line([vectors] * (dp_count // 2)))
    block_width = width // dp_count
    vectors = lax.dynamic_slice_in_dim(vectors, dp_place * block_width, block_width, 1)
    out_cols = width // seq_count
    return (
        by_row(result),
        by_row(grad_inputs),
        vectors[0],
        vectors[1],
        sum_qkv,
        sum_up[:, :out_cols],
        vectors[2],
        sum_up[:, out_cols:],
        sum_down,
    )


def solution(mesh):
    in_specs = (
        P("dp", "seq", None),
        P("dp", "seq", None),
        P("dp"),
        P("dp", "seq"),
        P(),
        P(),
        P("dp", None),
        P("dp", None),
        P(),
        P("dp", None),
        P("dp", None),
    )
    out_specs = (
        P("dp", "seq", None),
        P("dp", "seq", None),
        P("dp"),
        P("dp"),
        P("dp", "seq"),
        P("dp", "seq"),
        P("dp"),
        P("dp", "seq"),
        P("dp", "seq"),
    )
    return jax.shard_map(
        per_device, mesh=mesh, in_specs=in_specs, out_specs=out_specs, check_vma=False
    )
```

```python
import functools

import jax
import jax.numpy as jnp
from jax import lax
from jax.experimental import pallas as pl
from jax.experimental.pallas import tpu as pltpu
from jax.sharding import PartitionSpec as P

EPSILON = 1e-05
HEADS = 8
F32 = jnp.float32
BF16 = jnp.bfloat16
IN_VMEM = pl.BlockSpec(memory_space=pltpu.VMEM)


def nn(left, right):
    return jnp.dot(left, right, preferred_element_type=F32)


def nt(left, right):
    return lax.dot_general(left, right, (((1,), (1,)), ((), ())), preferred_element_type=F32)


def params(vmem):
    return pltpu.CompilerParams(vmem_limit_bytes=vmem * 2**20)


def cost(flops, bytes_accessed):
    return pl.CostEstimate(
        flops=int(flops), bytes_accessed=int(bytes_accessed), transcendentals=0
    )


def attend_kernel(chunk, q_ref, k_ref, v_ref, out_ref, den_ref):
    count = q_ref.shape[0]
    pair = pl.program_id(0)
    lane = lax.broadcasted_iota(jnp.int32, (1, 128), 1)
    low = lane < 64
    keys = k_ref[...]
    values = v_ref[...]
    one = jnp.ones_like(values)
    values_low = jnp.where(low, values, one)
    values_high = jnp.where(low, one, values)
    for start in range(0, count, chunk):
        at = slice(start, start + chunk)
        q = q_ref[at, :] * jnp.asarray(0.125, BF16)
        zero = jnp.zeros_like(q)
        left = nn(jnp.exp(nt(jnp.where(low, q, zero), keys)).astype(BF16), values_low)
        right = nn(jnp.exp(nt(jnp.where(low, zero, q), keys)).astype(BF16), values_high)
        swapped = jnp.where(low, right, left)
        den = pltpu.roll(swapped, 64, 1)
        out_ref[at, :] = (jnp.where(low, left, right) / den).astype(BF16)
        first = lane // 16 == 2 * pair
        second = lane // 16 == 2 * pair + 1
        mine = jnp.where(
            first, jnp.where(low, den, swapped), jnp.where(low, swapped, den)
        )
        den_ref[at, :] = jnp.where(first | second, mine, den_ref[at, :])


def attend(q_source, kv_source, kv_shift):
    count, span = q_source.shape[0], kv_source.shape[0]
    chunk = min(256, count)
    return pl.pallas_call(
        functools.partial(attend_kernel, chunk),
        grid=(4,),
        in_specs=[
            pl.BlockSpec((count, 128), lambda p: (0, p)),
            pl.BlockSpec((span, 128), lambda p: (0, kv_shift + p)),
            pl.BlockSpec((span, 128), lambda p: (0, kv_shift + 4 + p)),
        ],
        out_specs=[
            pl.BlockSpec((count, 128), lambda p: (0, p)),
            pl.BlockSpec((count, 128), lambda p: (0, 0)),
        ],
        out_shape=[
            jax.ShapeDtypeStruct((count, 512), BF16),
            jax.ShapeDtypeStruct((count, 128), F32),
        ],
        compiler_params=params(12),
        cost_estimate=cost(16 * count * span * 1024, 5 * 2**20),
        name="attend",
    )(q_source, kv_source, kv_source)


def attend_row_kernel(chunk, own_ref, out_ref, den_ref):
    count, width = out_ref.shape
    lane = lax.broadcasted_iota(jnp.int32, (1, 128), 1)
    low = lane < 64
    for start in range(0, count, chunk):
        at = slice(start, start + chunk)
        sums = jnp.zeros((chunk, 128), F32)
        for pair in range(width // 128):
            col = pair * 128
            keys = own_ref[:, width + col : width + col + 128]
            values = own_ref[:, 2 * width + col : 2 * width + col + 128]
            one = jnp.ones_like(values)
            q = own_ref[at, col : col + 128] * jnp.asarray(0.125, BF16)
            zero = jnp.zeros_like(q)
            left = nn(
                jnp.exp(nt(jnp.where(low, q, zero), keys)).astype(BF16),
                jnp.where(low, values, one),
            )
            right = nn(
                jnp.exp(nt(jnp.where(low, zero, q), keys)).astype(BF16),
                jnp.where(low, one, values),
            )
            swapped = jnp.where(low, right, left)
            den = pltpu.roll(swapped, 64, 1)
            out_ref[at, col : col + 128] = (jnp.where(low, left, right) / den).astype(BF16)
            first, second = lane // 16 == 2 * pair, lane // 16 == 2 * pair + 1
            sums = jnp.where(first, jnp.where(low, den, swapped), sums)
            sums = jnp.where(second, jnp.where(low, swapped, den), sums)
        den_ref[at, :] = sums


def attend_row(projected):
    count, width = projected.shape[0], projected.shape[1] // 3
    return pl.pallas_call(
        functools.partial(attend_row_kernel, min(256, count)),
        in_specs=[IN_VMEM],
        out_specs=[IN_VMEM] * 2,
        out_shape=[
            jax.ShapeDtypeStruct((count, width), BF16),
            jax.ShapeDtypeStruct((count, 128), F32),
        ],
        compiler_params=params(12),
        cost_estimate=cost(16 * count * count * 1024, 5 * 2**20),
        name="attend_row",
    )(projected)


def head_pair_back(chunk, q_ref, k_ref, v_ref, s_ref, x_ref, dk_ref, dv_ref):
    count, span = q_ref.shape[0], k_ref.shape[0]
    lane = lax.broadcasted_iota(jnp.int32, (1, 128), 1)
    low = lane < 64
    q = q_ref[...] * jnp.asarray(0.125, BF16)
    scaled = s_ref[...]
    extra = x_ref[...]
    zero = jnp.zeros_like(q)
    q_own = (jnp.where(low, q, zero), jnp.where(low, zero, q))
    s_own = (jnp.where(low, scaled, zero), jnp.where(low, zero, scaled))
    s_with = (jnp.where(low, scaled, extra), jnp.where(low, extra, scaled))
    minus = (
        jnp.where((lane == 64) | (lane == 65), -1.0, 0.0).astype(BF16),
        jnp.where((lane == 0) | (lane == 1), -1.0, 0.0).astype(BF16),
    )
    total = jnp.zeros((128, count), F32)
    for start in range(0, span, chunk):
        keys = k_ref[start : start + chunk, :]
        values = v_ref[start : start + chunk, :]
        none = jnp.zeros_like(keys)
        k_own = (jnp.where(low, keys, none), jnp.where(low, none, keys))
        v_with = (jnp.where(low, values, minus[0]), jnp.where(low, minus[1], values))
        dk = dv = 0.0
        for head in range(2):
            weights = jnp.exp(nt(keys, q_own[head]))
            slopes = (weights * nt(v_with[head], s_with[head])).astype(BF16)
            dv = dv + nn(weights.astype(BF16), s_own[head])
            dk = dk + nn(slopes, q_own[head])
            total = total + nn(k_own[head].T, slopes)
        dk_ref[start : start + chunk, :] = dk.astype(BF16)
        dv_ref[start : start + chunk, :] = dv.astype(BF16)
    return (total.T * 0.125).astype(BF16)


def attend_back_kernel(chunk, q_ref, k_ref, v_ref, s_ref, x_ref, dq_ref, dk_ref, dv_ref):
    dq_ref[...] = head_pair_back(chunk, q_ref, k_ref, v_ref, s_ref, x_ref, dk_ref, dv_ref)


def pair_views(col, width, proj_ref, s_ref, x_ref):
    at = [slice(shift + col, shift + col + 128) for shift in (0, width, 2 * width)]
    return [proj_ref.at[:, cols] for cols in at] + [s_ref.at[:, at[0]], x_ref.at[:, at[0]]]


def attend_back_half_kernel(chunk, proj_ref, s_ref, x_ref, dq_ref, dk_ref, dv_ref):
    width = s_ref.shape[1]
    for pair in range(2):
        col = pair * 128
        at = slice(col, col + 128)
        dq_ref[:, at] = head_pair_back(
            chunk,
            *pair_views(col, width, proj_ref, s_ref, x_ref),
            dk_ref.at[:, at],
            dv_ref.at[:, at],
        )


def attend_back_half(projected, scaled, extra):
    count, width = scaled.shape
    return pl.pallas_call(
        functools.partial(attend_back_half_kernel, min(512, count)),
        in_specs=[IN_VMEM] * 3,
        out_specs=[IN_VMEM] * 3,
        out_shape=[jax.ShapeDtypeStruct((count, width // 2), BF16)] * 3,
        compiler_params=params(14),
        cost_estimate=cost(16 * count * count * 1024, 6 * 2**20),
        name="attend_back_half",
    )(projected, scaled, extra)


def attend_back_sum_kernel(
    chunk,
    dp_count,
    own_ref,
    proj_ref,
    s_ref,
    x_ref,
    normed_ref,
    dq_first,
    dk_first,
    dv_first,
    dq_ref,
    dk_ref,
    dv_ref,
    mine_out,
    other_out,
    normed_t,
    joined,
    grad_ref,
    sems,
):
    width = s_ref.shape[1]
    normed_t[...] = normed_ref[...].T

    def weight_part(pair, refs):
        cols = slice((pair % 2) * 128, (pair % 2) * 128 + 128)
        for kind, ref in enumerate(refs):
            joined[:, kind * 128 : (kind + 1) * 128] = ref[:, cols]
        result = nn(normed_t[...], joined[...]).astype(BF16)
        rows = result.shape[0] // dp_count
        per = grad_ref.shape[3]
        for kind in range(3):
            block = pair + 4 * kind
            col, part = (block // per) ^ own_ref[0], block % per
            for d in range(dp_count):
                grad_ref[(d % 2) ^ own_ref[2], col, (d // 2) ^ own_ref[1], part] = result[
                    d * rows : (d + 1) * rows, kind * 128 : (kind + 1) * 128
                ]

    for pair in range(2):
        weight_part(pair, (dq_first, dk_first, dv_first))
    for pair in range(2, 4):
        at = slice((pair - 2) * 128, (pair - 1) * 128)
        dq_ref[:, at] = head_pair_back(
            chunk,
            *pair_views(pair * 128, width, proj_ref, s_ref, x_ref),
            dk_ref.at[:, at],
            dv_ref.at[:, at],
        )
        weight_part(pair, (dq_ref, dk_ref, dv_ref))
    hand_out(grad_ref, (mine_out, other_out), sems)


def attend_back_sum(own, projected, scaled, extra, normed, first_half, seq_count, dp_count):
    count, width = scaled.shape
    pieces = (2, seq_count, dp_count // 2, 12 // seq_count, width // dp_count, 128)
    return pl.pallas_call(
        functools.partial(attend_back_sum_kernel, min(512, count), dp_count),
        in_specs=[pl.BlockSpec(memory_space=pltpu.SMEM)] + [IN_VMEM] * 7,
        out_specs=[IN_VMEM] * 3 + [pl.BlockSpec(memory_space=pl.ANY)] * 2,
        scratch_shapes=[
            pltpu.VMEM((width, count), BF16),
            pltpu.VMEM((count, 384), BF16),
            pltpu.VMEM(pieces, BF16),
            pltpu.SemaphoreType.DMA((2,)),
        ],
        out_shape=[jax.ShapeDtypeStruct((count, width // 2), BF16)] * 3 + outs_of(pieces, True),
        compiler_params=params(18),
        cost_estimate=cost(20 * count * count * 1024, 10 * 2**20),
        name="attend_back_sum",
    )(own, projected, scaled, extra, normed, *first_half)


def attend_back(q_source, kv_source, scaled, extra):
    count, span = q_source.shape[0], kv_source.shape[0]
    chunk = min(512, span)
    own = pl.BlockSpec((count, 128), lambda p: (0, p))
    far = pl.BlockSpec((span, 128), lambda p: (0, p))
    return pl.pallas_call(
        functools.partial(attend_back_kernel, chunk),
        grid=(4,),
        in_specs=[
            own,
            pl.BlockSpec((span, 128), lambda p: (0, p)),
            pl.BlockSpec((span, 128), lambda p: (0, 4 + p)),
            own,
            own,
        ],
        out_specs=[own, far, far],
        out_shape=[
            jax.ShapeDtypeStruct((count, 512), BF16),
            jax.ShapeDtypeStruct((span, 512), BF16),
            jax.ShapeDtypeStruct((span, 512), BF16),
        ],
        compiler_params=params(40),
        cost_estimate=cost(32 * count * span * 1024, 8 * 2**20),
        name="attend_back",
    )(q_source, kv_source, kv_source, scaled, extra)


def norm_parts(tensor):
    center = tensor - jnp.mean(tensor, axis=-1, keepdims=True)
    scale = lax.rsqrt(jnp.mean(center * center, axis=-1, keepdims=True) + EPSILON)
    return center * scale, scale


def norm_back(q, normed, scale):
    return scale * (
        q - jnp.mean(q, axis=-1, keepdims=True) - normed * jnp.mean(q * normed, axis=-1, keepdims=True)
    )


def place_blocks(own_ref, sources, target, sems):
    copies = []
    for core in range(2):
        source = sources[core]
        by_seq = len(source.shape) == 4
        seq_count = source.shape[0] if by_seq else 1
        z_count, rows, cols = source.shape[-3:]
        by_rows = by_seq and cols == target.shape[1]
        for j in range(seq_count):
            for i in range(z_count):
                block = 2 * (own_ref[1] ^ i) + (own_ref[2] ^ core)
                across = slice(None)
                if by_rows:
                    block = block * seq_count + (own_ref[0] ^ j)
                elif by_seq:
                    across = pl.ds(pl.multiple_of((own_ref[0] ^ j) * cols, cols), cols)
                down = pl.ds(pl.multiple_of(block * rows, rows), rows)
                piece = source.at[j, i] if by_seq else source.at[i]
                copy = pltpu.make_async_copy(piece, target.at[down, across], sems.at[len(copies)])
                copies.append(copy)
    return copies


def fetches(own_ref, refs, target, sems):
    if len(refs) == 2:
        return place_blocks(own_ref, refs, target, sems)
    return [pltpu.make_async_copy(refs[0], target, sems.at[0])]


def launch(copies):
    for copy in copies:
        copy.start()


def finish(copies):
    for copy in copies:
        copy.wait()


def hand_out(held, outs, sems):
    sources = [held] if len(outs) == 1 else [held.at[0], held.at[1]]
    copies = [
        pltpu.make_async_copy(source, out, sems.at[i])
        for i, (source, out) in enumerate(zip(sources, outs))
    ]
    launch(copies)
    finish(copies)


def outs_of(shape, split):
    if split:
        return [jax.ShapeDtypeStruct(shape[1:], BF16)] * 2
    return [jax.ShapeDtypeStruct(shape, BF16)]


def copies_of(parts):
    count = 1
    for size in parts[0].shape[:-2]:
        count *= size
    return max(1, count * len(parts))


def project_kernel(parts, own_ref, hidden_ref, gain_ref, *refs):
    sources, (normed_ref, out_ref, whole_ref, sems) = refs[:parts], refs[parts:]

    @pl.when(pl.program_id(0) == 0)
    def _():
        launch(fetches(own_ref, sources, whole_ref, sems))

    normed = (norm_parts(hidden_ref[...])[0] * gain_ref[...]).astype(BF16)
    normed_ref[...] = normed

    @pl.when(pl.program_id(0) == 0)
    def _():
        finish(fetches(own_ref, sources, whole_ref, sems))

    out_ref[...] = nn(normed, whole_ref[...]).astype(BF16)


def project(own, hidden, gain, parts, cols):
    count, width = hidden.shape
    chunk = min(512, count)

    def rows(cols):
        return pl.BlockSpec((chunk, cols), lambda i, own: (i, 0))

    return pl.pallas_call(
        functools.partial(project_kernel, len(parts)),
        grid_spec=pltpu.PrefetchScalarGridSpec(
            num_scalar_prefetch=1,
            grid=(count // chunk,),
            in_specs=[rows(width), pl.BlockSpec((1, width), lambda i, own: (0, 0))]
            + [pl.BlockSpec(memory_space=pl.ANY)] * len(parts),
            out_specs=[
                rows(width),
                rows(cols),
                pl.BlockSpec((width, cols), lambda i, own: (0, 0)),
            ],
            scratch_shapes=[pltpu.SemaphoreType.DMA((copies_of(parts),))],
        ),
        out_shape=[
            jax.ShapeDtypeStruct((count, width), BF16),
            jax.ShapeDtypeStruct((count, cols), BF16),
            jax.ShapeDtypeStruct((width, cols), BF16),
        ],
        compiler_params=params(12),
        cost_estimate=cost(2 * count * width * cols, 8 * 2**20),
        name="project",
    )(own, hidden, gain, *parts)


def rise_kernel(cfg, own_ref, hidden_ref, att_ref, cot_ref, gain_ref, *refs):
    seq_count, dp_count, split, chunk, up_parts, down_parts = cfg
    up_sources, refs = refs[:up_parts], refs[up_parts:]
    down_sources, refs = refs[:down_parts], refs[down_parts:]
    outs = 2 if split else 1
    out_ref, normed_ref, scale_ref, slope_ref, w_up, w_down, *refs = refs
    grad_outs, refs = refs[:outs], refs[outs:]
    act_ref, cot_t, grad_ref, up_sems, down_sems, out_sems = refs
    count, width = hidden_ref.shape
    raised = act_ref.shape[1]
    up_copies = fetches(own_ref, up_sources, w_up, up_sems)
    down_copies = fetches(own_ref, down_sources, w_down, down_sems)
    launch(up_copies)
    launch(down_copies)
    cot_t[...] = cot_ref[...].T
    finish(up_copies)
    for row in range(0, count, chunk):
        at = slice(row, row + chunk)
        first = hidden_ref[at, :] + nn(att_ref[at, :], w_up[:, :width])
        normed, scale = norm_parts(first)
        normed_ref[at, :] = normed
        scale_ref[at, :] = jnp.broadcast_to(scale, (chunk, scale_ref.shape[1]))
        normed_two = (normed * gain_ref[...]).astype(BF16)
        if row == 0:
            finish(down_copies)
        total = first
        for start in range(0, raised, 512):
            stop = start + 512
            v = nn(normed_two, w_up[:, width + start : width + stop])
            square = v * v
            t = jnp.tanh(v * (0.7978845608028654 + 0.035677408136300125 * square))
            half = 0.5 + 0.5 * t
            act = (v * half).astype(BF16)
            slope = half + v * (0.5 - 0.5 * t * t) * (
                0.7978845608028654 + 0.10703222440890037 * square
            )
            act_ref[at, start:stop] = act
            slope_ref[at, start:stop] = slope.astype(BF16)
            total = total + nn(act, w_down[start:stop, :])
        out_ref[at, :] = total.astype(BF16)
    if not split:
        for start in range(0, raised, 512):
            grad_ref[:, start : start + 512] = nn(
                cot_t[...], act_ref[:, start : start + 512]
            ).astype(BF16)
        hand_out(grad_ref, grad_outs, out_sems)
        return
    cols = width // seq_count
    rows = raised // dp_count
    copies = []
    for i in range(dp_count // 2):
        result = nn(cot_t[...], act_ref[:, 2 * i * rows : 2 * (i + 1) * rows]).astype(BF16)
        z = i ^ own_ref[1]
        for s in range(seq_count):
            piece = result[s * cols : (s + 1) * cols, :]
            for core in range(2):
                for part in range(rows // 128):
                    col = core * rows + part * 128
                    grad_ref[core ^ own_ref[2], z, s ^ own_ref[0], part] = piece[:, col : col + 128]
        for core in range(2):
            copy = pltpu.make_async_copy(
                grad_ref.at[core, z], grad_outs[core].at[z], out_sems.at[len(copies)]
            )
            copies.append(copy)
            copy.start()
    finish(copies)


def rise(own, hidden, att, cot, gain, up_parts, down_parts, raised, seq_count, dp_count, split):
    count, width = hidden.shape
    if split:
        parts = raised // dp_count // 128
        grad_shape = (2, dp_count // 2, seq_count, parts, width // seq_count, 128)
    else:
        grad_shape = (width, raised)
    chunk = min(512, count)
    cfg = (seq_count, dp_count, split, chunk, len(up_parts), len(down_parts))
    grads = outs_of(grad_shape, split)
    up_shape, down_shape = (width, width + raised), (raised, width)
    anywhere = pl.BlockSpec(memory_space=pl.ANY)
    return pl.pallas_call(
        functools.partial(rise_kernel, cfg),
        in_specs=[pl.BlockSpec(memory_space=pltpu.SMEM)]
        + [IN_VMEM] * 4
        + [anywhere] * (len(up_parts) + len(down_parts)),
        out_specs=[IN_VMEM] * 6 + [anywhere] * len(grads),
        scratch_shapes=[
            pltpu.VMEM((count, raised), BF16),
            pltpu.VMEM((width, count), BF16),
            pltpu.VMEM(grad_shape, BF16),
            pltpu.SemaphoreType.DMA((copies_of(up_parts),)),
            pltpu.SemaphoreType.DMA((copies_of(down_parts),)),
            pltpu.SemaphoreType.DMA((dp_count,)),
        ],
        out_shape=[
            jax.ShapeDtypeStruct((count, width), BF16),
            jax.ShapeDtypeStruct((count, width), F32),
            jax.ShapeDtypeStruct((count, 128), F32),
            jax.ShapeDtypeStruct((count, raised), BF16),
            jax.ShapeDtypeStruct(up_shape, BF16),
            jax.ShapeDtypeStruct(down_shape, BF16),
        ]
        + grads,
        compiler_params=params(22),
        cost_estimate=cost(7 * 2**30, 24 * 2**20),
        name="rise",
    )(own, hidden, att, cot, gain, *up_parts, *down_parts)


def fall_kernel(
    cfg,
    own_ref,
    cot_ref,
    slope_ref,
    normed_ref,
    scale_ref,
    att_ref,
    den_ref,
    gain_ref,
    w_up,
    w_down,
    first_ref,
    scaled_ref,
    extra_ref,
    gain_sum_ref,
    *refs,
):
    seq_count, dp_count, split, chunk = cfg
    outs = 2 if split else 1
    grad_outs, (raise_ref, normed_t, att_t, branch_ref, grad_ref, out_sems) = (
        refs[:outs],
        refs[outs:],
    )
    count, width = cot_ref.shape
    raised = raise_ref.shape[1]
    gain = gain_ref[...]
    lane = lax.broadcasted_iota(jnp.int32, (128, width), 1)
    spread = lax.broadcasted_iota(jnp.int32, (128, width), 0) == 16 * (lane // 64)
    spread = jnp.where(spread, 1.0, 0.0).astype(BF16)
    row = lax.broadcasted_iota(jnp.int32, (128, 128), 0)
    col = lax.broadcasted_iota(jnp.int32, (128, 128), 1)
    swap = jnp.where((row < 64) != (col < 64), 1.0, 0.0).astype(BF16)
    even = lax.broadcasted_iota(jnp.int32, (1, 128), 1) % 2 == 0
    gain_sum = jnp.zeros((1, width), F32)
    att_t[...] = att_ref[...].T
    for top in range(0, count, chunk):
        at = slice(top, top + chunk)
        cot = cot_ref[at, :]
        normed = normed_ref[at, :]
        normed_t[:, at] = (normed * gain).astype(BF16).T
        back = jnp.zeros((chunk, width), F32)
        for start in range(0, raised, 512):
            stop = start + 512
            grad_raised = (nt(cot, w_down[start:stop, :]) * slope_ref[at, start:stop]).astype(BF16)
            raise_ref[at, start:stop] = grad_raised
            back = back + nt(grad_raised, w_up[:, width + start : width + stop])
        gain_sum = gain_sum + jnp.sum(back * normed, axis=0, keepdims=True)
        grad_first = cot.astype(F32) + norm_back(back * gain, normed, scale_ref[at, :1])
        first_ref[at, :] = grad_first
        branch = grad_first.astype(BF16)
        branch_ref[at, :] = branch
        inverse = 1.0 / den_ref[at, :]
        coarse = inverse.astype(BF16)
        fine = (inverse - coarse.astype(F32)).astype(BF16)
        ratio = nt(branch, w_up[:, :width]) * (nn(coarse, spread) + nn(fine, spread))
        scaled_ref[at, :] = ratio.astype(BF16)
        product = ratio * att_ref[at, :]
        coarse = product.astype(BF16)
        fine = (product - coarse.astype(F32)).astype(BF16)
        for start in range(0, width, 128):
            stop = start + 128
            offset = nn(coarse[:, start:stop], swap) + nn(fine[:, start:stop], swap)
            upper = offset.astype(BF16)
            lower = (offset - upper.astype(F32)).astype(BF16)
            extra_ref[at, start:stop] = jnp.where(even, upper, lower)
    gain_sum_ref[...] = gain_sum
    if not split:
        grad_ref[:, :width] = nn(att_t[...], branch_ref[...]).astype(BF16)
        for start in range(0, raised, 512):
            grad_ref[:, width + start : width + start + 512] = nn(
                normed_t[...], raise_ref[:, start : start + 512]
            ).astype(BF16)
        hand_out(grad_ref, grad_outs, out_sems)
        return
    cols = raised // seq_count
    wide = width // seq_count
    rows = width // dp_count
    copies = []

    def keep(result, s, at):
        for d in range(dp_count):
            grad_ref[(d % 2) ^ own_ref[2], s ^ own_ref[0], (d // 2) ^ own_ref[1], :, at] = result[
                d * rows : (d + 1) * rows, :
            ]

    result = nn(att_t[...], branch_ref[...]).astype(BF16)
    for s in range(seq_count):
        keep(result[:, s * wide : (s + 1) * wide], s, slice(0, wide))
    for s in range(seq_count):
        result = nn(normed_t[...], raise_ref[:, s * cols : (s + 1) * cols]).astype(BF16)
        keep(result, s, slice(wide, wide + cols))
        for core in range(2):
            copy = pltpu.make_async_copy(
                grad_ref.at[core, s ^ own_ref[0]],
                grad_outs[core].at[s ^ own_ref[0]],
                out_sems.at[len(copies)],
            )
            copies.append(copy)
            copy.start()
    finish(copies)


def fall(own, cot, slope, normed, scale, att, den, gain, w_up, w_down, seq_count, dp_count, split):
    count, width = cot.shape
    raised = w_down.shape[0]
    if split:
        grad_shape = (2, seq_count, dp_count // 2, width // dp_count, (width + raised) // seq_count)
    else:
        grad_shape = (width, width + raised)
    grads = outs_of(grad_shape, split)
    cfg = (seq_count, dp_count, split, min(512, count))

    def sds(dtype):
        return jax.ShapeDtypeStruct((count, width), dtype)

    return pl.pallas_call(
        functools.partial(fall_kernel, cfg),
        in_specs=[pl.BlockSpec(memory_space=pltpu.SMEM)] + [IN_VMEM] * 9,
        out_specs=[IN_VMEM] * 4 + [pl.BlockSpec(memory_space=pl.ANY)] * len(grads),
        scratch_shapes=[
            pltpu.VMEM((count, raised), BF16),
            pltpu.VMEM((width, count), BF16),
            pltpu.VMEM((width, count), BF16),
            pltpu.VMEM((count, width), BF16),
            pltpu.VMEM(grad_shape, BF16),
            pltpu.SemaphoreType.DMA((2 * seq_count,)),
        ],
        out_shape=[
            sds(F32),
            sds(BF16),
            sds(BF16),
            jax.ShapeDtypeStruct((1, width), F32),
        ]
        + grads,
        compiler_params=params(24),
        cost_estimate=cost(8 * 2**30, 24 * 2**20),
        name="fall",
    )(own, cot, slope, normed, scale, att, den, gain, w_up, w_down)


def last_kernel(chunk, hidden_ref, first_ref, gain_ref, mask_ref, w_ref, *refs):
    *grads, out_ref, sums_ref = refs
    masked = gain_sum = 0.0
    for top in range(0, hidden_ref.shape[0], chunk):
        at = slice(top, top + chunk)
        back = 0.0
        start = 0
        for ref in grads:
            stop = start + ref.shape[1]
            back = back + nt(ref[at, :], w_ref[:, start:stop])
            start = stop
        normed, scale = norm_parts(hidden_ref[at, :])
        grad = first_ref[at, :] + norm_back(back * gain_ref[...], normed, scale)
        coarse = grad.astype(BF16)
        out_ref[at, :] = coarse
        fine = (grad - coarse.astype(F32)).astype(BF16)
        mask = mask_ref[:, at]
        masked = masked + nn(mask, coarse) + nn(mask, fine)
        gain_sum = gain_sum + jnp.sum(back * normed, axis=0, keepdims=True)
    sums_ref[...] = masked
    sums_ref[1:2, :] = gain_sum


def last(hidden, grad_first, gain, mask, w_qkv, grads):
    count, width = hidden.shape
    return pl.pallas_call(
        functools.partial(last_kernel, min(512, count)),
        in_specs=[IN_VMEM] * (5 + len(grads)),
        out_specs=[IN_VMEM] * 2,
        out_shape=[
            jax.ShapeDtypeStruct((count, width), BF16),
            jax.ShapeDtypeStruct((8, width), F32),
        ],
        compiler_params=params(14),
        cost_estimate=cost(6 * count * width * width, 12 * 2**20),
        name="last",
    )(hidden, grad_first, gain, mask, w_qkv, *grads)


def swap_along(value, axis, mask):
    count = lax.axis_size(axis)
    return lax.ppermute(value, axis, [(i, i ^ mask) for i in range(count)])


def add_up(values):
    total = values[0].astype(F32)
    for value in values[1:]:
        total = total + value.astype(F32)
    return total


def together(*values):
    return lax.optimization_barrier(values)


def from_plane(values):
    return [values[0]] + [swap_along(values[j], "seq", j) for j in range(1, len(values))]


def from_line(values):
    return [values[0]] + [swap_along(values[j], "dp", 2 * j) for j in range(1, len(values))]


def other_core(value):
    return swap_along(value, "dp", 1)


def add_split(left, right):
    return [add_up((left[j], right[j])).astype(BF16) for j in range(left.shape[0])]


def split_first(value):
    return [value[j] for j in range(value.shape[0])]


def halve_line(value):
    half = value.shape[0] // 2
    while half:
        came = swap_along(value[half:], "dp", 2 * half)
        value = add_up((value[:half], came))
        half //= 2
        if half:
            value = value.astype(BF16)
    return value[0]


def gather_line(value):
    return jnp.stack(from_line([value] * (lax.axis_size("dp") // 2)))


def gather_plane(value):
    return jnp.stack(from_plane([value] * lax.axis_size("seq")))


def own_columns(weight):
    cols = weight.shape[1] // lax.axis_size("seq")
    return lax.dynamic_slice_in_dim(weight, lax.axis_index("seq") * cols, cols, 1)


def pieces_of(whole, own, seq_count, dp_count, flipped):
    row_blocks, col_blocks = (seq_count, dp_count) if flipped else (dp_count, seq_count)
    rows, cols = whole.shape[0] // row_blocks, whole.shape[1] // col_blocks
    whole = whole.reshape(row_blocks, rows, col_blocks, cols)
    whole = jnp.transpose(whole, (0, 2, 1, 3) if flipped else (2, 0, 1, 3))
    whole = whole.reshape(seq_count, dp_count // 2, 2, rows, cols)
    whole = jnp.take(whole, jnp.arange(seq_count) ^ own[0], axis=0)
    whole = jnp.take(whole, jnp.arange(dp_count // 2) ^ own[1], axis=1)
    whole = jnp.take(whole, jnp.arange(2) ^ own[2], axis=2)
    return jnp.transpose(whole, (2, 0, 1, 3, 4))


def per_device(
    inputs,
    cotangent,
    timestep,
    unmask_order,
    mask_embed,
    ln1_gain,
    weight_qkv,
    weight_out,
    ln2_gain,
    weight_up,
    weight_down,
):
    rows, segment, width = inputs.shape
    raised = weight_up.shape[1]
    seq_count, dp_count = lax.axis_size("seq"), lax.axis_size("dp")
    outer = seq_count // rows
    split = outer == 1 and (width // seq_count) % 128 == 0 and (width // dp_count) % 16 == 0
    place = lax.axis_index("seq")
    dp_place = lax.axis_index("dp")
    row = place % rows
    own = jnp.stack([place, dp_place // 2, dp_place % 2]).astype(jnp.int32)

    def by_partner(value):
        return [lax.dynamic_index_in_dim(value, row ^ j, 0, keepdims=False) for j in range(rows)]

    def to_rows(value):
        return jnp.concatenate(from_plane(by_partner(value)))

    def to_partners(value):
        return from_plane([value[j * segment : (j + 1) * segment] for j in range(rows)])

    def by_row(parts):
        bit = 1
        while bit < rows:
            odd = (row & bit) != 0
            parts = [jnp.where(odd, parts[j ^ bit], parts[j]) for j in range(rows)]
            bit *= 2
        return jnp.stack(parts)

    masked = (unmask_order <= timestep[:, None]).astype(BF16)
    masked = jnp.pad(masked[:, None, :], ((0, 0), (0, 15), (0, width - segment)))
    came = from_plane(by_partner(jnp.concatenate((inputs, masked), axis=1)))
    block = jnp.concatenate([part[:segment] for part in came]).astype(F32)
    mask_row = jnp.concatenate([part[segment, :segment] for part in came])
    up_and_out = jnp.concatenate((weight_out, weight_up), axis=1)
    if split:
        down_rows = weight_down.shape[0] // seq_count
        own_down = lax.dynamic_slice_in_dim(weight_down, place * down_rows, down_rows, 0)
        own_parts = jnp.concatenate((own_columns(weight_qkv), own_down), axis=1)
        line = gather_line(own_parts)
        line, up_and_out = together(line, up_and_out)
        line_up = from_line([up_and_out] * (dp_count // 2))
        plane_qkv = gather_plane(line[..., : -width])
        line_down = line[..., -width:].reshape(-1, width)
        plane_qkv, line_down, cot = together(plane_qkv, line_down, cotangent)
        parts_qkv = [plane_qkv, other_core(plane_qkv)]
        cot = by_partner(cot)
        cot = from_plane([jnp.concatenate((part, line_down)) for part in cot])
    else:
        cot = from_plane(by_partner(cotangent))
        parts_qkv, parts_up, parts_down = (
            [lax.all_gather(weight, "dp", axis=0, tiled=True)]
            for weight in (weight_qkv, up_and_out, weight_down)
        )

    hidden = block + mask_row.astype(F32)[:, None] * mask_embed
    normed_one, projected, whole_qkv = project(
        own, hidden, ln1_gain[None, :], parts_qkv, 3 * width
    )
    if outer > 1:
        groups = [[j * rows + i for j in range(outer)] for i in range(rows)]
        far = lax.all_gather(
            projected[:, width:], "seq", axis=0, tiled=True, axis_index_groups=groups
        )
        attended, denominators = attend(projected, far, 0)
    else:
        attended, denominators = attend_row(projected)
    if split:
        cot, line_up, attended = together(cot, line_up, attended)
        plane_down = jnp.stack([part[segment:] for part in cot])
        plane_down = plane_down.reshape(seq_count, dp_count // 2, -1, width)
        line_up = jnp.stack(line_up)
        parts_up = [line_up, other_core(line_up)]
        parts_down = [plane_down, other_core(plane_down)]
    cot = jnp.concatenate([part[:segment] for part in cot])
    outputs, normed, scale, slope, whole_up, whole_down, *grad_down = rise(
        own,
        hidden,
        attended,
        cot,
        ln2_gain[None, :],
        parts_up,
        parts_down,
        raised,
        seq_count,
        dp_count,
        split,
    )
    result = to_partners(outputs)
    grad_first, scaled, extra, sum_gain_two, *grad_up = fall(
        own,
        cot,
        slope,
        normed,
        scale,
        attended,
        denominators,
        ln2_gain[None, :],
        whole_up,
        whole_down,
        seq_count,
        dp_count,
        split,
    )
    mask_rows = jnp.broadcast_to(mask_row[None, :], (8, mask_row.shape[0]))
    if split:
        grad_down[1] = other_core(grad_down[1])
        grad_down, scaled, grad_up, result = together(grad_down, scaled, grad_up, result)
        line_down = from_line(add_split(*grad_down))
        grad_up[1] = other_core(grad_up[1])
        half = attend_back_half(projected, scaled, extra)
        grad_up, half, line_down[1] = together(grad_up, half, line_down[1])
        plane_up = from_plane(add_split(*grad_up))
        *rest, mine_qkv, other_qkv = attend_back_sum(
            own, projected, scaled, extra, normed_one, half, seq_count, dp_count
        )
        plane_up, line_down, rest, mine_qkv, other_qkv = together(
            plane_up, line_down, rest, mine_qkv, other_qkv
        )
        grads = [part for pair in zip(half, rest) for part in pair]
        both_qkv = (mine_qkv, other_core(other_qkv))
        line_up = add_up(plane_up).astype(BF16)
        z_half = line_up.shape[0] // 2
        line_came = swap_along(line_up[z_half:], "dp", 2 * z_half)
        both_qkv, mask_rows = together(both_qkv, mask_rows)
        tall = width // dp_count
        down = add_up(line_down).astype(BF16).reshape(seq_count, -1, tall, 128)
        mine_qkv = [part.reshape(-1, tall, 128) for part in add_split(*both_qkv)]
        plane_last = from_plane([jnp.concatenate((mine_qkv[j], down[j])) for j in range(seq_count)])
    else:
        dq, dk, dv = attend_back(projected, far, scaled, extra)
        both = jnp.concatenate((dk, dv), axis=1)
        both = lax.psum_scatter(
            both, "seq", scatter_dimension=0, tiled=True, axis_index_groups=groups
        )
        grads = [dq, both]
        grad_qkv = lax.dot_general(
            normed_one,
            jnp.concatenate(grads, axis=1),
            (((0,), (0,)), ((), ())),
            preferred_element_type=F32,
        ).astype(BF16)
        cut = functools.partial(pieces_of, own=own, seq_count=seq_count, dp_count=dp_count)
        (grad_up,), (grad_down,) = grad_up, grad_down
        grad_out, grad_up = (
            cut(part, flipped=False) for part in (grad_up[:, :width], grad_up[:, width:])
        )
        grad_up = jnp.concatenate((grad_out, grad_up), axis=-1)
        grad_qkv = cut(grad_qkv, flipped=False)
        grad_down = cut(grad_down, flipped=True)
        sums = []
        for pieces in (grad_qkv, grad_up, grad_down):
            mine = add_up((pieces[0], other_core(pieces[1]))).astype(BF16)
            plane = add_up(from_plane(split_first(mine))).astype(BF16)
            sums.append(add_up(from_line(split_first(plane))))
        sum_qkv, sum_up, sum_down = sums
        sum_down = sum_down.T
    grad_hidden, sums = last(
        hidden, grad_first, ln1_gain[None, :], mask_rows, whole_qkv, grads
    )
    vectors = jnp.concatenate((sums[0:2], sum_gain_two, jnp.zeros((13, width), F32)), axis=0)
    vectors = vectors + other_core(vectors)
    bit = 1
    while bit < seq_count:
        vectors = vectors + swap_along(vectors, "seq", bit)
        bit *= 2
    if split:
        grad_hidden, vectors, line_came, plane_last = together(
            grad_hidden, vectors, line_came, plane_last
        )
        grad_inputs = to_partners(grad_hidden)
        sum_up = halve_line(add_up((line_up[:z_half], line_came)).astype(BF16))
        plane = add_up(plane_last)
        kinds = mine_qkv[0].shape[0]
        sum_down = plane[kinds:].reshape(-1, width // seq_count, 128)
        sum_down = jnp.transpose(sum_down, (0, 2, 1)).reshape(-1, width // seq_count)
        z_count = dp_count // 2
        plane = plane[:kinds].astype(BF16).reshape((z_count, -1) + plane.shape[1:])
        flat = jnp.transpose(vectors.reshape(16, -1, 128), (1, 0, 2)).astype(BF16)
        flat = jnp.broadcast_to(flat.reshape(1, -1, tall, 128), (z_count, 1, tall, 128))
        line = halve_line(jnp.concatenate((plane, flat), axis=1))
        sum_qkv = jnp.transpose(line[:-1], (1, 0, 2)).reshape(tall, -1)
        vectors = jnp.transpose(line[-1].reshape(-1, 16, 128), (1, 0, 2)).reshape(16, -1)
    else:
        grad_inputs = to_partners(grad_hidden)
        vectors = add_up(from_line([vectors] * (dp_count // 2)))
    block_width = width // dp_count
    vectors = lax.dynamic_slice_in_dim(vectors, dp_place * block_width, block_width, 1)
    out_cols = width // seq_count
    return (
        by_row(result),
        by_row(grad_inputs),
        vectors[0],
        vectors[1],
        sum_qkv,
        sum_up[:, :out_cols],
        vectors[2],
        sum_up[:, out_cols:],
        sum_down,
    )


def solution(mesh):
    in_specs = (
        P("dp", "seq", None),
        P("dp", "seq", None),
        P("dp"),
        P("dp", "seq"),
        P(),
        P(),
        P("dp", None),
        P("dp", None),
        P(),
        P("dp", None),
        P("dp", None),
    )
    out_specs = (
        P("dp", "seq", None),
        P("dp", "seq", None),
        P("dp"),
        P("dp"),
        P("dp", "seq"),
        P("dp", "seq"),
        P("dp"),
        P("dp", "seq"),
        P("dp", "seq"),
    )
    return jax.shard_map(
        per_device, mesh=mesh, in_specs=in_specs, out_specs=out_specs, check_vma=False
    )
```

```python
import functools

import jax
import jax.numpy as jnp
from jax import lax
from jax.experimental import pallas as pl
from jax.experimental.pallas import tpu as pltpu
from jax.sharding import PartitionSpec as P

EPSILON = 1e-05
HEADS = 8
F32 = jnp.float32
BF16 = jnp.bfloat16
IN_VMEM = pl.BlockSpec(memory_space=pltpu.VMEM)


def nn(left, right):
    return jnp.dot(left, right, preferred_element_type=F32)


def nt(left, right):
    return lax.dot_general(left, right, (((1,), (1,)), ((), ())), preferred_element_type=F32)


def params(vmem):
    return pltpu.CompilerParams(vmem_limit_bytes=vmem * 2**20)


def cost(flops, bytes_accessed):
    return pl.CostEstimate(
        flops=int(flops), bytes_accessed=int(bytes_accessed), transcendentals=0
    )


def attend_kernel(chunk, q_ref, k_ref, v_ref, out_ref, den_ref):
    count = q_ref.shape[0]
    pair = pl.program_id(0)
    lane = lax.broadcasted_iota(jnp.int32, (1, 128), 1)
    low = lane < 64
    keys = k_ref[...]
    values = v_ref[...]
    one = jnp.ones_like(values)
    values_low = jnp.where(low, values, one)
    values_high = jnp.where(low, one, values)
    for start in range(0, count, chunk):
        at = slice(start, start + chunk)
        q = q_ref[at, :] * jnp.asarray(0.125, BF16)
        zero = jnp.zeros_like(q)
        left = nn(jnp.exp(nt(jnp.where(low, q, zero), keys)).astype(BF16), values_low)
        right = nn(jnp.exp(nt(jnp.where(low, zero, q), keys)).astype(BF16), values_high)
        swapped = jnp.where(low, right, left)
        den = pltpu.roll(swapped, 64, 1)
        out_ref[at, :] = (jnp.where(low, left, right) / den).astype(BF16)
        first = lane // 16 == 2 * pair
        second = lane // 16 == 2 * pair + 1
        mine = jnp.where(
            first, jnp.where(low, den, swapped), jnp.where(low, swapped, den)
        )
        den_ref[at, :] = jnp.where(first | second, mine, den_ref[at, :])


def attend(q_source, kv_source, kv_shift):
    count, span = q_source.shape[0], kv_source.shape[0]
    chunk = min(256, count)
    return pl.pallas_call(
        functools.partial(attend_kernel, chunk),
        grid=(4,),
        in_specs=[
            pl.BlockSpec((count, 128), lambda p: (0, p)),
            pl.BlockSpec((span, 128), lambda p: (0, kv_shift + p)),
            pl.BlockSpec((span, 128), lambda p: (0, kv_shift + 4 + p)),
        ],
        out_specs=[
            pl.BlockSpec((count, 128), lambda p: (0, p)),
            pl.BlockSpec((count, 128), lambda p: (0, 0)),
        ],
        out_shape=[
            jax.ShapeDtypeStruct((count, 512), BF16),
            jax.ShapeDtypeStruct((count, 128), F32),
        ],
        compiler_params=params(12),
        cost_estimate=cost(16 * count * span * 1024, 5 * 2**20),
        name="attend",
    )(q_source, kv_source, kv_source)


def attend_row_kernel(chunk, own_ref, out_ref, den_ref):
    count, width = out_ref.shape
    lane = lax.broadcasted_iota(jnp.int32, (1, 128), 1)
    low = lane < 64
    for start in range(0, count, chunk):
        at = slice(start, start + chunk)
        sums = jnp.zeros((chunk, 128), F32)
        for pair in range(width // 128):
            col = pair * 128
            keys = own_ref[:, width + col : width + col + 128]
            values = own_ref[:, 2 * width + col : 2 * width + col + 128]
            one = jnp.ones_like(values)
            q = own_ref[at, col : col + 128] * jnp.asarray(0.125, BF16)
            zero = jnp.zeros_like(q)
            left = nn(
                jnp.exp(nt(jnp.where(low, q, zero), keys)).astype(BF16),
                jnp.where(low, values, one),
            )
            right = nn(
                jnp.exp(nt(jnp.where(low, zero, q), keys)).astype(BF16),
                jnp.where(low, one, values),
            )
            swapped = jnp.where(low, right, left)
            den = pltpu.roll(swapped, 64, 1)
            out_ref[at, col : col + 128] = (jnp.where(low, left, right) / den).astype(BF16)
            first, second = lane // 16 == 2 * pair, lane // 16 == 2 * pair + 1
            sums = jnp.where(first, jnp.where(low, den, swapped), sums)
            sums = jnp.where(second, jnp.where(low, swapped, den), sums)
        den_ref[at, :] = sums


def attend_row(projected):
    count, width = projected.shape[0], projected.shape[1] // 3
    return pl.pallas_call(
        functools.partial(attend_row_kernel, min(256, count)),
        in_specs=[IN_VMEM],
        out_specs=[IN_VMEM] * 2,
        out_shape=[
            jax.ShapeDtypeStruct((count, width), BF16),
            jax.ShapeDtypeStruct((count, 128), F32),
        ],
        compiler_params=params(8),
        cost_estimate=cost(16 * count * count * 1024, 5 * 2**20),
        name="attend_row",
    )(projected)


def head_pair_back(chunk, q_ref, k_ref, v_ref, s_ref, x_ref, dk_ref, dv_ref):
    count, span = q_ref.shape[0], k_ref.shape[0]
    lane = lax.broadcasted_iota(jnp.int32, (1, 128), 1)
    low = lane < 64
    q = q_ref[...] * jnp.asarray(0.125, BF16)
    scaled = s_ref[...]
    extra = x_ref[...]
    zero = jnp.zeros_like(q)
    q_own = (jnp.where(low, q, zero), jnp.where(low, zero, q))
    s_own = (jnp.where(low, scaled, zero), jnp.where(low, zero, scaled))
    s_with = (jnp.where(low, scaled, extra), jnp.where(low, extra, scaled))
    minus = (
        jnp.where((lane == 64) | (lane == 65), -1.0, 0.0).astype(BF16),
        jnp.where((lane == 0) | (lane == 1), -1.0, 0.0).astype(BF16),
    )
    total = jnp.zeros((128, count), F32)
    for start in range(0, span, chunk):
        keys = k_ref[start : start + chunk, :]
        values = v_ref[start : start + chunk, :]
        none = jnp.zeros_like(keys)
        k_own = (jnp.where(low, keys, none), jnp.where(low, none, keys))
        v_with = (jnp.where(low, values, minus[0]), jnp.where(low, minus[1], values))
        dk = dv = 0.0
        for head in range(2):
            weights = jnp.exp(nt(keys, q_own[head]))
            slopes = (weights * nt(v_with[head], s_with[head])).astype(BF16)
            dv = dv + nn(weights.astype(BF16), s_own[head])
            dk = dk + nn(slopes, q_own[head])
            total = total + nn(k_own[head].T, slopes)
        dk_ref[start : start + chunk, :] = dk.astype(BF16)
        dv_ref[start : start + chunk, :] = dv.astype(BF16)
    return (total.T * 0.125).astype(BF16)


def attend_back_kernel(chunk, q_ref, k_ref, v_ref, s_ref, x_ref, dq_ref, dk_ref, dv_ref):
    dq_ref[...] = head_pair_back(chunk, q_ref, k_ref, v_ref, s_ref, x_ref, dk_ref, dv_ref)


def pair_views(col, width, proj_ref, s_ref, x_ref):
    at = [slice(shift + col, shift + col + 128) for shift in (0, width, 2 * width)]
    return [proj_ref.at[:, cols] for cols in at] + [s_ref.at[:, at[0]], x_ref.at[:, at[0]]]


def attend_back_half_kernel(chunk, proj_ref, s_ref, x_ref, dq_ref, dk_ref, dv_ref):
    width = s_ref.shape[1]
    for pair in range(2):
        col = pair * 128
        at = slice(col, col + 128)
        dq_ref[:, at] = head_pair_back(
            chunk,
            *pair_views(col, width, proj_ref, s_ref, x_ref),
            dk_ref.at[:, at],
            dv_ref.at[:, at],
        )


def attend_back_half(projected, scaled, extra):
    count, width = scaled.shape
    return pl.pallas_call(
        functools.partial(attend_back_half_kernel, min(512, count)),
        in_specs=[IN_VMEM] * 3,
        out_specs=[IN_VMEM] * 3,
        out_shape=[jax.ShapeDtypeStruct((count, width // 2), BF16)] * 3,
        compiler_params=params(10),
        cost_estimate=cost(16 * count * count * 1024, 6 * 2**20),
        name="attend_back_half",
    )(projected, scaled, extra)


def attend_back_sum_kernel(
    chunk,
    dp_count,
    own_ref,
    proj_ref,
    s_ref,
    x_ref,
    normed_ref,
    dq_first,
    dk_first,
    dv_first,
    dq_ref,
    dk_ref,
    dv_ref,
    mine_out,
    other_out,
    normed_t,
    joined,
    grad_ref,
    sems,
):
    width = s_ref.shape[1]
    normed_t[...] = normed_ref[...].T

    def weight_part(pair, refs):
        cols = slice((pair % 2) * 128, (pair % 2) * 128 + 128)
        for kind, ref in enumerate(refs):
            joined[:, kind * 128 : (kind + 1) * 128] = ref[:, cols]
        result = nn(normed_t[...], joined[...]).astype(BF16)
        rows = result.shape[0] // dp_count
        per = grad_ref.shape[3]
        for kind in range(3):
            block = pair + 4 * kind
            col, part = (block // per) ^ own_ref[0], block % per
            for d in range(dp_count):
                grad_ref[(d % 2) ^ own_ref[2], col, (d // 2) ^ own_ref[1], part] = result[
                    d * rows : (d + 1) * rows, kind * 128 : (kind + 1) * 128
                ]

    for pair in range(2):
        weight_part(pair, (dq_first, dk_first, dv_first))
    for pair in range(2, 4):
        at = slice((pair - 2) * 128, (pair - 1) * 128)
        dq_ref[:, at] = head_pair_back(
            chunk,
            *pair_views(pair * 128, width, proj_ref, s_ref, x_ref),
            dk_ref.at[:, at],
            dv_ref.at[:, at],
        )
        weight_part(pair, (dq_ref, dk_ref, dv_ref))
    hand_out(grad_ref, (mine_out, other_out), sems)


def attend_back_sum(own, projected, scaled, extra, normed, first_half, seq_count, dp_count):
    count, width = scaled.shape
    pieces = (2, seq_count, dp_count // 2, 12 // seq_count, width // dp_count, 128)
    return pl.pallas_call(
        functools.partial(attend_back_sum_kernel, min(512, count), dp_count),
        in_specs=[pl.BlockSpec(memory_space=pltpu.SMEM)] + [IN_VMEM] * 7,
        out_specs=[IN_VMEM] * 3 + [pl.BlockSpec(memory_space=pl.ANY)] * 2,
        scratch_shapes=[
            pltpu.VMEM((width, count), BF16),
            pltpu.VMEM((count, 384), BF16),
            pltpu.VMEM(pieces, BF16),
            pltpu.SemaphoreType.DMA((2,)),
        ],
        out_shape=[jax.ShapeDtypeStruct((count, width // 2), BF16)] * 3 + outs_of(pieces, True),
        compiler_params=params(12),
        cost_estimate=cost(20 * count * count * 1024, 10 * 2**20),
        name="attend_back_sum",
    )(own, projected, scaled, extra, normed, *first_half)


def attend_back(q_source, kv_source, scaled, extra):
    count, span = q_source.shape[0], kv_source.shape[0]
    chunk = min(512, span)
    own = pl.BlockSpec((count, 128), lambda p: (0, p))
    far = pl.BlockSpec((span, 128), lambda p: (0, p))
    return pl.pallas_call(
        functools.partial(attend_back_kernel, chunk),
        grid=(4,),
        in_specs=[
            own,
            pl.BlockSpec((span, 128), lambda p: (0, p)),
            pl.BlockSpec((span, 128), lambda p: (0, 4 + p)),
            own,
            own,
        ],
        out_specs=[own, far, far],
        out_shape=[
            jax.ShapeDtypeStruct((count, 512), BF16),
            jax.ShapeDtypeStruct((span, 512), BF16),
            jax.ShapeDtypeStruct((span, 512), BF16),
        ],
        compiler_params=params(40),
        cost_estimate=cost(32 * count * span * 1024, 8 * 2**20),
        name="attend_back",
    )(q_source, kv_source, kv_source, scaled, extra)


def norm_parts(tensor):
    center = tensor - jnp.mean(tensor, axis=-1, keepdims=True)
    scale = lax.rsqrt(jnp.mean(center * center, axis=-1, keepdims=True) + EPSILON)
    return center * scale, scale


def norm_back(q, normed, scale):
    return scale * (
        q - jnp.mean(q, axis=-1, keepdims=True) - normed * jnp.mean(q * normed, axis=-1, keepdims=True)
    )


def place_blocks(own_ref, sources, target, sems):
    copies = []
    for core in range(2):
        source = sources[core]
        by_seq = len(source.shape) == 4
        seq_count = source.shape[0] if by_seq else 1
        z_count, rows, cols = source.shape[-3:]
        by_rows = by_seq and cols == target.shape[1]
        for j in range(seq_count):
            for i in range(z_count):
                block = 2 * (own_ref[1] ^ i) + (own_ref[2] ^ core)
                across = slice(None)
                if by_rows:
                    block = block * seq_count + (own_ref[0] ^ j)
                elif by_seq:
                    across = pl.ds(pl.multiple_of((own_ref[0] ^ j) * cols, cols), cols)
                down = pl.ds(pl.multiple_of(block * rows, rows), rows)
                piece = source.at[j, i] if by_seq else source.at[i]
                copy = pltpu.make_async_copy(piece, target.at[down, across], sems.at[len(copies)])
                copies.append(copy)
    return copies


def fetches(own_ref, refs, target, sems, cols=None):
    if cols is not None:
        axes = len(refs[0].shape) - 1
        refs = [ref.at[(slice(None),) * axes + (cols,)] for ref in refs]
        target = target.at[:, cols]
    if len(refs) == 2:
        return place_blocks(own_ref, refs, target, sems)
    return [pltpu.make_async_copy(refs[0], target, sems.at[0])]


def launch(copies):
    for copy in copies:
        copy.start()


def finish(copies):
    for copy in copies:
        copy.wait()


def hand_out(held, outs, sems):
    sources = [held] if len(outs) == 1 else [held.at[0], held.at[1]]
    copies = [
        pltpu.make_async_copy(source, out, sems.at[i])
        for i, (source, out) in enumerate(zip(sources, outs))
    ]
    launch(copies)
    finish(copies)


def outs_of(shape, split):
    if split:
        return [jax.ShapeDtypeStruct(shape[1:], BF16)] * 2
    return [jax.ShapeDtypeStruct(shape, BF16)]


def copies_of(parts):
    count = 1
    for size in parts[0].shape[:-2]:
        count *= size
    return max(1, count * len(parts))


def project_kernel(chunk, parts, own_ref, hidden_ref, gain_ref, *refs):
    sources, (normed_out, out_ref, whole_out, normed_ref, whole_ref, sems, out_sems) = (
        refs[:parts],
        refs[parts:],
    )
    copies = fetches(own_ref, sources, whole_ref, sems)
    launch(copies)
    count = hidden_ref.shape[0]
    for row in range(0, count, chunk):
        at = slice(row, row + chunk)
        normed_ref[at, :] = (norm_parts(hidden_ref[at, :])[0] * gain_ref[...]).astype(BF16)
    finish(copies)
    copies = [
        pltpu.make_async_copy(normed_ref, normed_out, out_sems.at[0]),
        pltpu.make_async_copy(whole_ref, whole_out, out_sems.at[1]),
    ]
    launch(copies)
    for row in range(0, count, chunk):
        at = slice(row, row + chunk)
        out_ref[at, :] = nn(normed_ref[at, :], whole_ref[...]).astype(BF16)
    finish(copies)


def project(own, hidden, gain, parts, cols):
    count, width = hidden.shape
    in_hbm = pl.BlockSpec(memory_space=pltpu.HBM)
    return pl.pallas_call(
        functools.partial(project_kernel, min(512, count), len(parts)),
        in_specs=[pl.BlockSpec(memory_space=pltpu.SMEM)]
        + [IN_VMEM] * 2
        + [pl.BlockSpec(memory_space=pl.ANY)] * len(parts),
        out_specs=[in_hbm, IN_VMEM, in_hbm],
        scratch_shapes=[
            pltpu.VMEM((count, width), BF16),
            pltpu.VMEM((width, cols), BF16),
            pltpu.SemaphoreType.DMA((copies_of(parts),)),
            pltpu.SemaphoreType.DMA((2,)),
        ],
        out_shape=[
            jax.ShapeDtypeStruct((count, width), BF16),
            jax.ShapeDtypeStruct((count, cols), BF16),
            jax.ShapeDtypeStruct((width, cols), BF16),
        ],
        compiler_params=params(10),
        cost_estimate=cost(2 * count * width * cols, 8 * 2**20),
        name="project",
    )(own, hidden, gain, *parts)


def rise_kernel(cfg, own_ref, hidden_ref, att_ref, cot_ref, gain_ref, *refs):
    seq_count, dp_count, split, chunk, up_parts, down_parts = cfg
    up_sources, refs = refs[:up_parts], refs[up_parts:]
    down_sources, refs = refs[:down_parts], refs[down_parts:]
    outs = 2 if split else 1
    out_ref, normed_ref, scale_ref, slope_ref, w_up, w_down, *refs = refs
    grad_outs, refs = refs[:outs], refs[outs:]
    act_ref, cot_t, grad_ref, up_sems, down_sems, out_sems = refs
    count, width = hidden_ref.shape
    raised = act_ref.shape[1]
    up_copies = [
        fetches(own_ref, up_sources, w_up, up_sems.at[i], slice(start, start + 512))
        for i, start in enumerate(range(0, width + raised, 512))
    ]
    down_copies = fetches(own_ref, down_sources, w_down, down_sems)
    for copies in up_copies[:2] + [down_copies] + up_copies[2:]:
        launch(copies)
    cot_t[...] = cot_ref[...].T
    finish(up_copies[0])
    for row in range(0, count, chunk):
        at = slice(row, row + chunk)
        first = hidden_ref[at, :] + nn(att_ref[at, :], w_up[:, :width])
        normed, scale = norm_parts(first)
        normed_ref[at, :] = normed
        scale_ref[at, :] = jnp.broadcast_to(scale, (chunk, scale_ref.shape[1]))
        normed_two = (normed * gain_ref[...]).astype(BF16)
        total = first
        for start in range(0, raised, 512):
            stop = start + 512
            if row == 0:
                finish(up_copies[1 + start // 512])
            v = nn(normed_two, w_up[:, width + start : width + stop])
            square = v * v
            t = jnp.tanh(v * (0.7978845608028654 + 0.035677408136300125 * square))
            half = 0.5 + 0.5 * t
            act = (v * half).astype(BF16)
            slope = half + v * (0.5 - 0.5 * t * t) * (
                0.7978845608028654 + 0.10703222440890037 * square
            )
            act_ref[at, start:stop] = act
            slope_ref[at, start:stop] = slope.astype(BF16)
            if row == 0 and start == 0:
                finish(down_copies)
            total = total + nn(act, w_down[start:stop, :])
        out_ref[at, :] = total.astype(BF16)
    if not split:
        for start in range(0, raised, 512):
            grad_ref[:, start : start + 512] = nn(
                cot_t[...], act_ref[:, start : start + 512]
            ).astype(BF16)
        hand_out(grad_ref, grad_outs, out_sems)
        return
    cols = width // seq_count
    rows = raised // dp_count
    copies = []
    for i in range(dp_count // 2):
        result = nn(cot_t[...], act_ref[:, 2 * i * rows : 2 * (i + 1) * rows]).astype(BF16)
        z = i ^ own_ref[1]
        for s in range(seq_count):
            piece = result[s * cols : (s + 1) * cols, :]
            for core in range(2):
                for part in range(rows // 128):
                    col = core * rows + part * 128
                    grad_ref[core ^ own_ref[2], z, s ^ own_ref[0], part] = piece[:, col : col + 128]
        for core in range(2):
            copy = pltpu.make_async_copy(
                grad_ref.at[core, z], grad_outs[core].at[z], out_sems.at[len(copies)]
            )
            copies.append(copy)
            copy.start()
    finish(copies)


def rise(own, hidden, att, cot, gain, up_parts, down_parts, raised, seq_count, dp_count, split):
    count, width = hidden.shape
    if split:
        parts = raised // dp_count // 128
        grad_shape = (2, dp_count // 2, seq_count, parts, width // seq_count, 128)
    else:
        grad_shape = (width, raised)
    chunk = min(512, count)
    cfg = (seq_count, dp_count, split, chunk, len(up_parts), len(down_parts))
    grads = outs_of(grad_shape, split)
    up_shape, down_shape = (width, width + raised), (raised, width)
    anywhere = pl.BlockSpec(memory_space=pl.ANY)
    return pl.pallas_call(
        functools.partial(rise_kernel, cfg),
        in_specs=[pl.BlockSpec(memory_space=pltpu.SMEM)]
        + [IN_VMEM] * 4
        + [anywhere] * (len(up_parts) + len(down_parts)),
        out_specs=[IN_VMEM] * 6 + [anywhere] * len(grads),
        scratch_shapes=[
            pltpu.VMEM((count, raised), BF16),
            pltpu.VMEM((width, count), BF16),
            pltpu.VMEM(grad_shape, BF16),
            pltpu.SemaphoreType.DMA(((width + raised) // 512, copies_of(up_parts))),
            pltpu.SemaphoreType.DMA((copies_of(down_parts),)),
            pltpu.SemaphoreType.DMA((dp_count,)),
        ],
        out_shape=[
            jax.ShapeDtypeStruct((count, width), BF16),
            jax.ShapeDtypeStruct((count, width), F32),
            jax.ShapeDtypeStruct((count, 128), F32),
            jax.ShapeDtypeStruct((count, raised), BF16),
            jax.ShapeDtypeStruct(up_shape, BF16),
            jax.ShapeDtypeStruct(down_shape, BF16),
        ]
        + grads,
        compiler_params=params(15),
        cost_estimate=cost(7 * 2**30, 24 * 2**20),
        name="rise",
    )(own, hidden, att, cot, gain, *up_parts, *down_parts)


def fall_kernel(
    cfg,
    own_ref,
    cot_ref,
    slope_ref,
    normed_ref,
    scale_ref,
    att_ref,
    den_ref,
    gain_ref,
    w_up,
    w_down,
    first_ref,
    scaled_ref,
    extra_ref,
    gain_sum_ref,
    *refs,
):
    seq_count, dp_count, split, chunk = cfg
    outs = 2 if split else 1
    grad_outs, (raise_ref, normed_t, att_t, branch_ref, grad_ref, out_sems) = (
        refs[:outs],
        refs[outs:],
    )
    count, width = cot_ref.shape
    raised = raise_ref.shape[1]
    gain = gain_ref[...]
    lane = lax.broadcasted_iota(jnp.int32, (128, width), 1)
    spread = lax.broadcasted_iota(jnp.int32, (128, width), 0) == 16 * (lane // 64)
    spread = jnp.where(spread, 1.0, 0.0).astype(BF16)
    row = lax.broadcasted_iota(jnp.int32, (128, 128), 0)
    col = lax.broadcasted_iota(jnp.int32, (128, 128), 1)
    swap = jnp.where((row < 64) != (col < 64), 1.0, 0.0).astype(BF16)
    even = lax.broadcasted_iota(jnp.int32, (1, 128), 1) % 2 == 0
    gain_sum = jnp.zeros((1, width), F32)
    att_t[...] = att_ref[...].T
    for top in range(0, count, chunk):
        at = slice(top, top + chunk)
        cot = cot_ref[at, :]
        normed = normed_ref[at, :]
        normed_t[:, at] = (normed * gain).astype(BF16).T
        back = jnp.zeros((chunk, width), F32)
        for start in range(0, raised, 512):
            stop = start + 512
            grad_raised = (nt(cot, w_down[start:stop, :]) * slope_ref[at, start:stop]).astype(BF16)
            raise_ref[at, start:stop] = grad_raised
            back = back + nt(grad_raised, w_up[:, width + start : width + stop])
        gain_sum = gain_sum + jnp.sum(back * normed, axis=0, keepdims=True)
        grad_first = cot.astype(F32) + norm_back(back * gain, normed, scale_ref[at, :1])
        first_ref[at, :] = grad_first
        branch = grad_first.astype(BF16)
        branch_ref[at, :] = branch
        inverse = 1.0 / den_ref[at, :]
        coarse = inverse.astype(BF16)
        fine = (inverse - coarse.astype(F32)).astype(BF16)
        ratio = nt(branch, w_up[:, :width]) * (nn(coarse, spread) + nn(fine, spread))
        scaled_ref[at, :] = ratio.astype(BF16)
        product = ratio * att_ref[at, :]
        coarse = product.astype(BF16)
        fine = (product - coarse.astype(F32)).astype(BF16)
        for start in range(0, width, 128):
            stop = start + 128
            offset = nn(coarse[:, start:stop], swap) + nn(fine[:, start:stop], swap)
            upper = offset.astype(BF16)
            lower = (offset - upper.astype(F32)).astype(BF16)
            extra_ref[at, start:stop] = jnp.where(even, upper, lower)
    gain_sum_ref[...] = gain_sum
    if not split:
        grad_ref[:, :width] = nn(att_t[...], branch_ref[...]).astype(BF16)
        for start in range(0, raised, 512):
            grad_ref[:, width + start : width + start + 512] = nn(
                normed_t[...], raise_ref[:, start : start + 512]
            ).astype(BF16)
        hand_out(grad_ref, grad_outs, out_sems)
        return
    cols = raised // seq_count
    wide = width // seq_count
    rows = width // dp_count
    copies = []

    def keep(result, s, at):
        for d in range(dp_count):
            grad_ref[(d % 2) ^ own_ref[2], s ^ own_ref[0], (d // 2) ^ own_ref[1], :, at] = result[
                d * rows : (d + 1) * rows, :
            ]

    result = nn(att_t[...], branch_ref[...]).astype(BF16)
    for s in range(seq_count):
        keep(result[:, s * wide : (s + 1) * wide], s, slice(0, wide))
    for s in range(seq_count):
        result = nn(normed_t[...], raise_ref[:, s * cols : (s + 1) * cols]).astype(BF16)
        keep(result, s, slice(wide, wide + cols))
        for core in range(2):
            copy = pltpu.make_async_copy(
                grad_ref.at[core, s ^ own_ref[0]],
                grad_outs[core].at[s ^ own_ref[0]],
                out_sems.at[len(copies)],
            )
            copies.append(copy)
            copy.start()
    finish(copies)


def fall(own, cot, slope, normed, scale, att, den, gain, w_up, w_down, seq_count, dp_count, split):
    count, width = cot.shape
    raised = w_down.shape[0]
    if split:
        grad_shape = (2, seq_count, dp_count // 2, width // dp_count, (width + raised) // seq_count)
    else:
        grad_shape = (width, width + raised)
    grads = outs_of(grad_shape, split)
    cfg = (seq_count, dp_count, split, min(512, count))

    def sds(dtype):
        return jax.ShapeDtypeStruct((count, width), dtype)

    return pl.pallas_call(
        functools.partial(fall_kernel, cfg),
        in_specs=[pl.BlockSpec(memory_space=pltpu.SMEM)] + [IN_VMEM] * 9,
        out_specs=[IN_VMEM] * 4 + [pl.BlockSpec(memory_space=pl.ANY)] * len(grads),
        scratch_shapes=[
            pltpu.VMEM((count, raised), BF16),
            pltpu.VMEM((width, count), BF16),
            pltpu.VMEM((width, count), BF16),
            pltpu.VMEM((count, width), BF16),
            pltpu.VMEM(grad_shape, BF16),
            pltpu.SemaphoreType.DMA((2 * seq_count,)),
        ],
        out_shape=[
            sds(F32),
            sds(BF16),
            sds(BF16),
            jax.ShapeDtypeStruct((1, width), F32),
        ]
        + grads,
        compiler_params=params(17),
        cost_estimate=cost(8 * 2**30, 24 * 2**20),
        name="fall",
    )(own, cot, slope, normed, scale, att, den, gain, w_up, w_down)


def last_kernel(chunk, hidden_ref, first_ref, gain_ref, mask_ref, w_ref, *refs):
    *grads, out_ref, sums_ref = refs
    masked = gain_sum = 0.0
    for top in range(0, hidden_ref.shape[0], chunk):
        at = slice(top, top + chunk)
        back = 0.0
        start = 0
        for ref in grads:
            stop = start + ref.shape[1]
            back = back + nt(ref[at, :], w_ref[:, start:stop])
            start = stop
        normed, scale = norm_parts(hidden_ref[at, :])
        grad = first_ref[at, :] + norm_back(back * gain_ref[...], normed, scale)
        coarse = grad.astype(BF16)
        out_ref[at, :] = coarse
        fine = (grad - coarse.astype(F32)).astype(BF16)
        mask = mask_ref[:, at]
        masked = masked + nn(mask, coarse) + nn(mask, fine)
        gain_sum = gain_sum + jnp.sum(back * normed, axis=0, keepdims=True)
    sums_ref[...] = masked
    sums_ref[1:2, :] = gain_sum


def last(hidden, grad_first, gain, mask, w_qkv, grads):
    count, width = hidden.shape
    return pl.pallas_call(
        functools.partial(last_kernel, min(512, count)),
        in_specs=[IN_VMEM] * (5 + len(grads)),
        out_specs=[IN_VMEM] * 2,
        out_shape=[
            jax.ShapeDtypeStruct((count, width), BF16),
            jax.ShapeDtypeStruct((8, width), F32),
        ],
        compiler_params=params(8),
        cost_estimate=cost(6 * count * width * width, 12 * 2**20),
        name="last",
    )(hidden, grad_first, gain, mask, w_qkv, *grads)


def swap_along(value, axis, mask):
    count = lax.axis_size(axis)
    return lax.ppermute(value, axis, [(i, i ^ mask) for i in range(count)])


def add_up(values):
    total = values[0].astype(F32)
    for value in values[1:]:
        total = total + value.astype(F32)
    return total


def together(*values):
    return lax.optimization_barrier(values)


def from_plane(values):
    return [values[0]] + [swap_along(values[j], "seq", j) for j in range(1, len(values))]


def from_line(values):
    return [values[0]] + [swap_along(values[j], "dp", 2 * j) for j in range(1, len(values))]


def other_core(value):
    return swap_along(value, "dp", 1)


def add_split(left, right):
    return [add_up((left[j], right[j])).astype(BF16) for j in range(left.shape[0])]


def both_cores(value):
    return [value, other_core(value)]


def split_first(value):
    return [value[j] for j in range(value.shape[0])]


def halve_line(value):
    half = value.shape[0] // 2
    while half:
        came = swap_along(value[half:], "dp", 2 * half)
        value = add_up((value[:half], came))
        half //= 2
        if half:
            value = value.astype(BF16)
    return value[0]


def gather_line(value):
    return jnp.stack(from_line([value] * (lax.axis_size("dp") // 2)))


def gather_plane(value):
    return jnp.stack(from_plane([value] * lax.axis_size("seq")))


def own_columns(weight):
    cols = weight.shape[1] // lax.axis_size("seq")
    return lax.dynamic_slice_in_dim(weight, lax.axis_index("seq") * cols, cols, 1)


def pieces_of(whole, own, seq_count, dp_count, flipped):
    row_blocks, col_blocks = (seq_count, dp_count) if flipped else (dp_count, seq_count)
    rows, cols = whole.shape[0] // row_blocks, whole.shape[1] // col_blocks
    whole = whole.reshape(row_blocks, rows, col_blocks, cols)
    whole = jnp.transpose(whole, (0, 2, 1, 3) if flipped else (2, 0, 1, 3))
    whole = whole.reshape(seq_count, dp_count // 2, 2, rows, cols)
    whole = jnp.take(whole, jnp.arange(seq_count) ^ own[0], axis=0)
    whole = jnp.take(whole, jnp.arange(dp_count // 2) ^ own[1], axis=1)
    whole = jnp.take(whole, jnp.arange(2) ^ own[2], axis=2)
    return jnp.transpose(whole, (2, 0, 1, 3, 4))


def per_device(
    inputs,
    cotangent,
    timestep,
    unmask_order,
    mask_embed,
    ln1_gain,
    weight_qkv,
    weight_out,
    ln2_gain,
    weight_up,
    weight_down,
):
    rows, segment, width = inputs.shape
    raised = weight_up.shape[1]
    seq_count, dp_count = lax.axis_size("seq"), lax.axis_size("dp")
    outer = seq_count // rows
    split = outer == 1 and (seq_count, dp_count) == (4, 8)
    place = lax.axis_index("seq")
    dp_place = lax.axis_index("dp")
    row = place % rows
    own = jnp.stack([place, dp_place // 2, dp_place % 2]).astype(jnp.int32)

    def by_partner(value):
        return [lax.dynamic_index_in_dim(value, row ^ j, 0, keepdims=False) for j in range(rows)]

    def to_rows(value):
        return jnp.concatenate(from_plane(by_partner(value)))

    def to_partners(value):
        return from_plane([value[j * segment : (j + 1) * segment] for j in range(rows)])

    def by_row(parts):
        bit = 1
        while bit < rows:
            odd = (row & bit) != 0
            parts = [jnp.where(odd, parts[j ^ bit], parts[j]) for j in range(rows)]
            bit *= 2
        return jnp.stack(parts)

    masked = (unmask_order <= timestep[:, None]).astype(BF16)
    masked = jnp.pad(masked[:, None, :], ((0, 0), (0, 15), (0, width - segment)))
    came = by_partner(jnp.concatenate((inputs, masked), axis=1))
    up_and_out = jnp.concatenate((weight_out, weight_up), axis=1)
    if split:
        down_rows = weight_down.shape[0] // seq_count
        own_down = lax.dynamic_slice_in_dim(weight_down, place * down_rows, down_rows, 0)
        line = gather_line(jnp.concatenate((own_columns(weight_qkv), own_down), axis=1))
        came = from_plane(came)
        line, up_and_out = together(line, up_and_out)
        line_up = from_line([up_and_out] * (dp_count // 2))
        plane_qkv = gather_plane(line[..., :-width])
        line_down = line[..., -width:].reshape(-1, width)
        plane_qkv, line_down, cot = together(plane_qkv, line_down, cotangent)
        parts_qkv = both_cores(plane_qkv)
        cot = from_plane([jnp.concatenate((part, line_down)) for part in by_partner(cot)])
    else:
        came, cot = from_plane(came), from_plane(by_partner(cotangent))
        parts_qkv, parts_up, parts_down = (
            [lax.all_gather(weight, "dp", axis=0, tiled=True)]
            for weight in (weight_qkv, up_and_out, weight_down)
        )

    block = jnp.concatenate([part[:segment] for part in came]).astype(F32)
    mask_row = jnp.concatenate([part[segment, :segment] for part in came])
    hidden = block + mask_row.astype(F32)[:, None] * mask_embed
    normed_one, projected, whole_qkv = project(
        own, hidden, ln1_gain[None, :], parts_qkv, 3 * width
    )
    if outer > 1:
        groups = [[j * rows + i for j in range(outer)] for i in range(rows)]
        far = lax.all_gather(
            projected[:, width:], "seq", axis=0, tiled=True, axis_index_groups=groups
        )
        attended, denominators = attend(projected, far, 0)
    else:
        attended, denominators = attend_row(projected)
    if split:
        line_up, attended = together(line_up, attended)
        parts_up = both_cores(jnp.stack(line_up))
        cot, parts_up[0] = together(cot, parts_up[0])
        plane_down = jnp.stack([part[segment:] for part in cot])
        plane_down = plane_down.reshape(seq_count, dp_count // 2, -1, width)
        parts_down = both_cores(plane_down)
    cot = jnp.concatenate([part[:segment] for part in cot])
    outputs, normed, scale, slope, whole_up, whole_down, *grad_down = rise(
        own,
        hidden,
        attended,
        cot,
        ln2_gain[None, :],
        parts_up,
        parts_down,
        raised,
        seq_count,
        dp_count,
        split,
    )
    result = to_partners(outputs)
    grad_first, scaled, extra, sum_gain_two, *grad_up = fall(
        own,
        cot,
        slope,
        normed,
        scale,
        attended,
        denominators,
        ln2_gain[None, :],
        whole_up,
        whole_down,
        seq_count,
        dp_count,
        split,
    )
    mask_rows = jnp.broadcast_to(mask_row[None, :], (8, mask_row.shape[0]))
    if split:
        grad_down[1] = other_core(grad_down[1])
        grad_down, scaled, grad_up, result = together(grad_down, scaled, grad_up, result)
        line_down = from_line(add_split(*grad_down))
        grad_up[1] = other_core(grad_up[1])
        half = attend_back_half(projected, scaled, extra)
        grad_up, half, line_down[1] = together(grad_up, half, line_down[1])
        plane_up = from_plane(add_split(*grad_up))
        *rest, mine_qkv, other_qkv = attend_back_sum(
            own, projected, scaled, extra, normed_one, half, seq_count, dp_count
        )
        plane_up, line_down, rest, mine_qkv, other_qkv = together(
            plane_up, line_down, rest, mine_qkv, other_qkv
        )
        grads = [part for pair in zip(half, rest) for part in pair]
        both_qkv = (mine_qkv, other_core(other_qkv))
        line_up = add_up(plane_up).astype(BF16)
        z_half = line_up.shape[0] // 2
        line_came = swap_along(line_up[z_half:], "dp", 2 * z_half)
        tall = width // dp_count
        down = add_up(line_down).astype(BF16).reshape(seq_count, -1, tall, 128)
        both_qkv, mask_rows = together(both_qkv, mask_rows)
        mine_qkv = [part.reshape(-1, tall, 128) for part in add_split(*both_qkv)]
        plane_last = from_plane([jnp.concatenate((mine_qkv[j], down[j])) for j in range(seq_count)])
    else:
        dq, dk, dv = attend_back(projected, far, scaled, extra)
        both = jnp.concatenate((dk, dv), axis=1)
        both = lax.psum_scatter(
            both, "seq", scatter_dimension=0, tiled=True, axis_index_groups=groups
        )
        grads = [dq, both]
        grad_qkv = lax.dot_general(
            normed_one,
            jnp.concatenate(grads, axis=1),
            (((0,), (0,)), ((), ())),
            preferred_element_type=F32,
        ).astype(BF16)
        cut = functools.partial(pieces_of, own=own, seq_count=seq_count, dp_count=dp_count)
        (grad_up,), (grad_down,) = grad_up, grad_down
        grad_out, grad_up = (
            cut(part, flipped=False) for part in (grad_up[:, :width], grad_up[:, width:])
        )
        grad_up = jnp.concatenate((grad_out, grad_up), axis=-1)
        grad_qkv = cut(grad_qkv, flipped=False)
        grad_down = cut(grad_down, flipped=True)
        sums = []
        for pieces in (grad_qkv, grad_up, grad_down):
            mine = add_up((pieces[0], other_core(pieces[1]))).astype(BF16)
            plane = add_up(from_plane(split_first(mine))).astype(BF16)
            sums.append(add_up(from_line(split_first(plane))))
        sum_qkv, sum_up, sum_down = sums
        sum_down = sum_down.T
    grad_hidden, sums = last(
        hidden, grad_first, ln1_gain[None, :], mask_rows, whole_qkv, grads
    )
    vectors = jnp.concatenate((sums[0:2], sum_gain_two, jnp.zeros((5, width), F32)), axis=0)
    vectors = vectors + other_core(vectors)
    bit = 2
    while bit < dp_count:
        vectors = vectors + swap_along(vectors, "dp", bit)
        bit *= 2
    if split:
        grad_hidden, vectors, line_came, plane_last = together(
            grad_hidden, vectors, line_came, plane_last
        )
        sum_up = add_up((line_up[:z_half], line_came)).astype(BF16)
        kinds = mine_qkv[0].shape[0]
        sum_qkv = add_up([part[:kinds] for part in plane_last]).astype(BF16)
        sum_qkv = sum_qkv.reshape((dp_count // 2, -1) + sum_qkv.shape[1:])
        line_came = swap_along(sum_qkv[z_half:], "dp", 2 * z_half)
        line_came, plane_last, sum_up = together(line_came, plane_last, sum_up)
        sum_qkv = halve_line(add_up((sum_qkv[:z_half], line_came)).astype(BF16))
        sum_up = halve_line(sum_up)
        sum_down = add_up([part[kinds:] for part in plane_last])
        sum_down = sum_down.reshape(-1, width // seq_count, 128)
        sum_down = jnp.transpose(sum_down, (0, 2, 1)).reshape(-1, width // seq_count)
        sum_qkv = jnp.transpose(sum_qkv, (1, 0, 2)).reshape(tall, -1)
    grad_inputs = [grad_hidden[j * segment : (j + 1) * segment] for j in range(rows)]
    if split:
        coarse = vectors.astype(BF16)
        terms = jnp.concatenate((coarse, (vectors - coarse.astype(F32)).astype(BF16)))
        grad_inputs = [jnp.concatenate((part, terms)) for part in grad_inputs]
    grad_inputs = from_plane(grad_inputs)
    if split:
        vectors = add_up([part[segment:] for part in grad_inputs])
        vectors = vectors[:8] + vectors[8:]
        grad_inputs = [part[:segment] for part in grad_inputs]
    else:
        vectors = add_up(from_plane([vectors] * seq_count))
    block_width = width // dp_count
    vectors = lax.dynamic_slice_in_dim(vectors, dp_place * block_width, block_width, 1)
    out_cols = width // seq_count
    return (
        by_row(result),
        by_row(grad_inputs),
        vectors[0],
        vectors[1],
        sum_qkv,
        sum_up[:, :out_cols],
        vectors[2],
        sum_up[:, out_cols:],
        sum_down,
    )


def solution(mesh):
    in_specs = (
        P("dp", "seq", None),
        P("dp", "seq", None),
        P("dp"),
        P("dp", "seq"),
        P(),
        P(),
        P("dp", None),
        P("dp", None),
        P(),
        P("dp", None),
        P("dp", None),
    )
    out_specs = (
        P("dp", "seq", None),
        P("dp", "seq", None),
        P("dp"),
        P("dp"),
        P("dp", "seq"),
        P("dp", "seq"),
        P("dp"),
        P("dp", "seq"),
        P("dp", "seq"),
    )
    return jax.shard_map(
        per_device, mesh=mesh, in_specs=in_specs, out_specs=out_specs, check_vma=False
    )
```

```python
import functools

import jax
import jax.numpy as jnp
from jax import lax
from jax.experimental import pallas as pl
from jax.experimental.pallas import tpu as pltpu
from jax.sharding import PartitionSpec as P

EPSILON = 1e-05
HEADS = 8
F32 = jnp.float32
BF16 = jnp.bfloat16
IN_VMEM = pl.BlockSpec(memory_space=pltpu.VMEM)


def nn(left, right):
    return jnp.dot(left, right, preferred_element_type=F32)


def nt(left, right):
    return lax.dot_general(left, right, (((1,), (1,)), ((), ())), preferred_element_type=F32)


def params(vmem):
    return pltpu.CompilerParams(vmem_limit_bytes=vmem * 2**20)


def cost(flops, bytes_accessed):
    return pl.CostEstimate(
        flops=int(flops), bytes_accessed=int(bytes_accessed), transcendentals=0
    )


def attend_kernel(chunk, q_ref, k_ref, v_ref, out_ref, den_ref):
    count = q_ref.shape[0]
    pair = pl.program_id(0)
    lane = lax.broadcasted_iota(jnp.int32, (1, 128), 1)
    low = lane < 64
    keys = k_ref[...]
    values = v_ref[...]
    one = jnp.ones_like(values)
    values_low = jnp.where(low, values, one)
    values_high = jnp.where(low, one, values)
    for start in range(0, count, chunk):
        at = slice(start, start + chunk)
        q = q_ref[at, :] * jnp.asarray(0.125, BF16)
        zero = jnp.zeros_like(q)
        left = nn(jnp.exp(nt(jnp.where(low, q, zero), keys)).astype(BF16), values_low)
        right = nn(jnp.exp(nt(jnp.where(low, zero, q), keys)).astype(BF16), values_high)
        swapped = jnp.where(low, right, left)
        den = pltpu.roll(swapped, 64, 1)
        out_ref[at, :] = (jnp.where(low, left, right) / den).astype(BF16)
        first = lane // 16 == 2 * pair
        second = lane // 16 == 2 * pair + 1
        mine = jnp.where(
            first, jnp.where(low, den, swapped), jnp.where(low, swapped, den)
        )
        den_ref[at, :] = jnp.where(first | second, mine, den_ref[at, :])


def attend(q_source, kv_source, kv_shift):
    count, span = q_source.shape[0], kv_source.shape[0]
    chunk = min(256, count)
    return pl.pallas_call(
        functools.partial(attend_kernel, chunk),
        grid=(4,),
        in_specs=[
            pl.BlockSpec((count, 128), lambda p: (0, p)),
            pl.BlockSpec((span, 128), lambda p: (0, kv_shift + p)),
            pl.BlockSpec((span, 128), lambda p: (0, kv_shift + 4 + p)),
        ],
        out_specs=[
            pl.BlockSpec((count, 128), lambda p: (0, p)),
            pl.BlockSpec((count, 128), lambda p: (0, 0)),
        ],
        out_shape=[
            jax.ShapeDtypeStruct((count, 512), BF16),
            jax.ShapeDtypeStruct((count, 128), F32),
        ],
        compiler_params=params(12),
        cost_estimate=cost(16 * count * span * 1024, 5 * 2**20),
        name="attend",
    )(q_source, kv_source, kv_source)


def attend_row_kernel(chunk, own_ref, out_ref, den_ref):
    count, width = out_ref.shape
    lane = lax.broadcasted_iota(jnp.int32, (1, 128), 1)
    low = lane < 64
    for start in range(0, count, chunk):
        at = slice(start, start + chunk)
        sums = jnp.zeros((chunk, 128), F32)
        for pair in range(width // 128):
            col = pair * 128
            keys = own_ref[:, width + col : width + col + 128]
            values = own_ref[:, 2 * width + col : 2 * width + col + 128]
            one = jnp.ones_like(values)
            q = own_ref[at, col : col + 128] * jnp.asarray(0.125, BF16)
            zero = jnp.zeros_like(q)
            left = nn(
                jnp.exp(nt(jnp.where(low, q, zero), keys)).astype(BF16),
                jnp.where(low, values, one),
            )
            right = nn(
                jnp.exp(nt(jnp.where(low, zero, q), keys)).astype(BF16),
                jnp.where(low, one, values),
            )
            swapped = jnp.where(low, right, left)
            den = pltpu.roll(swapped, 64, 1)
            out_ref[at, col : col + 128] = (jnp.where(low, left, right) / den).astype(BF16)
            first, second = lane // 16 == 2 * pair, lane // 16 == 2 * pair + 1
            sums = jnp.where(first, jnp.where(low, den, swapped), sums)
            sums = jnp.where(second, jnp.where(low, swapped, den), sums)
        den_ref[at, :] = sums


def attend_row(projected):
    count, width = projected.shape[0], projected.shape[1] // 3
    return pl.pallas_call(
        functools.partial(attend_row_kernel, min(256, count)),
        in_specs=[IN_VMEM],
        out_specs=[IN_VMEM] * 2,
        out_shape=[
            jax.ShapeDtypeStruct((count, width), BF16),
            jax.ShapeDtypeStruct((count, 128), F32),
        ],
        compiler_params=params(8),
        cost_estimate=cost(16 * count * count * 1024, 5 * 2**20),
        name="attend_row",
    )(projected)


def head_pair_back(chunk, q_ref, k_ref, v_ref, s_ref, x_ref, dk_ref, dv_ref):
    count, span = q_ref.shape[0], k_ref.shape[0]
    lane = lax.broadcasted_iota(jnp.int32, (1, 128), 1)
    low = lane < 64
    q = q_ref[...] * jnp.asarray(0.125, BF16)
    scaled = s_ref[...]
    extra = x_ref[...]
    zero = jnp.zeros_like(q)
    q_own = (jnp.where(low, q, zero), jnp.where(low, zero, q))
    s_own = (jnp.where(low, scaled, zero), jnp.where(low, zero, scaled))
    s_with = (jnp.where(low, scaled, extra), jnp.where(low, extra, scaled))
    minus = (
        jnp.where((lane == 64) | (lane == 65), -1.0, 0.0).astype(BF16),
        jnp.where((lane == 0) | (lane == 1), -1.0, 0.0).astype(BF16),
    )
    total = jnp.zeros((128, count), F32)
    for start in range(0, span, chunk):
        keys = k_ref[start : start + chunk, :]
        values = v_ref[start : start + chunk, :]
        none = jnp.zeros_like(keys)
        k_own = (jnp.where(low, keys, none), jnp.where(low, none, keys))
        v_with = (jnp.where(low, values, minus[0]), jnp.where(low, minus[1], values))
        dk = dv = 0.0
        for head in range(2):
            weights = jnp.exp(nt(keys, q_own[head]))
            slopes = (weights * nt(v_with[head], s_with[head])).astype(BF16)
            dv = dv + nn(weights.astype(BF16), s_own[head])
            dk = dk + nn(slopes, q_own[head])
            total = total + nn(k_own[head].T, slopes)
        dk_ref[start : start + chunk, :] = dk.astype(BF16)
        dv_ref[start : start + chunk, :] = dv.astype(BF16)
    return (total.T * 0.125).astype(BF16)


def attend_back_kernel(chunk, q_ref, k_ref, v_ref, s_ref, x_ref, dq_ref, dk_ref, dv_ref):
    dq_ref[...] = head_pair_back(chunk, q_ref, k_ref, v_ref, s_ref, x_ref, dk_ref, dv_ref)


def pair_views(col, width, proj_ref, s_ref, x_ref):
    at = [slice(shift + col, shift + col + 128) for shift in (0, width, 2 * width)]
    return [proj_ref.at[:, cols] for cols in at] + [s_ref.at[:, at[0]], x_ref.at[:, at[0]]]


def attend_back_half_kernel(chunk, proj_ref, s_ref, x_ref, dq_ref, dk_ref, dv_ref):
    width = s_ref.shape[1]
    for pair in range(2):
        col = pair * 128
        at = slice(col, col + 128)
        dq_ref[:, at] = head_pair_back(
            chunk,
            *pair_views(col, width, proj_ref, s_ref, x_ref),
            dk_ref.at[:, at],
            dv_ref.at[:, at],
        )


def attend_back_half(projected, scaled, extra):
    count, width = scaled.shape
    return pl.pallas_call(
        functools.partial(attend_back_half_kernel, min(512, count)),
        in_specs=[IN_VMEM] * 3,
        out_specs=[IN_VMEM] * 3,
        out_shape=[jax.ShapeDtypeStruct((count, width // 2), BF16)] * 3,
        compiler_params=params(10),
        cost_estimate=cost(16 * count * count * 1024, 6 * 2**20),
        name="attend_back_half",
    )(projected, scaled, extra)


def attend_back_sum_kernel(
    chunk,
    dp_count,
    own_ref,
    proj_ref,
    s_ref,
    x_ref,
    normed_ref,
    dq_first,
    dk_first,
    dv_first,
    dq_ref,
    dk_ref,
    dv_ref,
    mine_out,
    other_out,
    normed_t,
    joined,
    grad_ref,
    sems,
):
    width = s_ref.shape[1]
    normed_t[...] = normed_ref[...].T

    def weight_part(pair, refs):
        cols = slice((pair % 2) * 128, (pair % 2) * 128 + 128)
        for kind, ref in enumerate(refs):
            joined[:, kind * 128 : (kind + 1) * 128] = ref[:, cols]
        result = nn(normed_t[...], joined[...]).astype(BF16)
        rows = result.shape[0] // dp_count
        per = grad_ref.shape[3]
        for kind in range(3):
            block = pair + 4 * kind
            col, part = (block // per) ^ own_ref[0], block % per
            for d in range(dp_count):
                grad_ref[(d % 2) ^ own_ref[2], col, (d // 2) ^ own_ref[1], part] = result[
                    d * rows : (d + 1) * rows, kind * 128 : (kind + 1) * 128
                ]

    for pair in range(2):
        weight_part(pair, (dq_first, dk_first, dv_first))
    for pair in range(2, 4):
        at = slice((pair - 2) * 128, (pair - 1) * 128)
        dq_ref[:, at] = head_pair_back(
            chunk,
            *pair_views(pair * 128, width, proj_ref, s_ref, x_ref),
            dk_ref.at[:, at],
            dv_ref.at[:, at],
        )
        weight_part(pair, (dq_ref, dk_ref, dv_ref))
    hand_out(grad_ref, (mine_out, other_out), sems)


def attend_back_sum(own, projected, scaled, extra, normed, first_half, seq_count, dp_count):
    count, width = scaled.shape
    pieces = (2, seq_count, dp_count // 2, 12 // seq_count, width // dp_count, 128)
    return pl.pallas_call(
        functools.partial(attend_back_sum_kernel, min(512, count), dp_count),
        in_specs=[pl.BlockSpec(memory_space=pltpu.SMEM)] + [IN_VMEM] * 7,
        out_specs=[IN_VMEM] * 3 + [pl.BlockSpec(memory_space=pl.ANY)] * 2,
        scratch_shapes=[
            pltpu.VMEM((width, count), BF16),
            pltpu.VMEM((count, 384), BF16),
            pltpu.VMEM(pieces, BF16),
            pltpu.SemaphoreType.DMA((2,)),
        ],
        out_shape=[jax.ShapeDtypeStruct((count, width // 2), BF16)] * 3 + outs_of(pieces, True),
        compiler_params=params(12),
        cost_estimate=cost(20 * count * count * 1024, 10 * 2**20),
        name="attend_back_sum",
    )(own, projected, scaled, extra, normed, *first_half)


def attend_back(q_source, kv_source, scaled, extra):
    count, span = q_source.shape[0], kv_source.shape[0]
    chunk = min(512, span)
    own = pl.BlockSpec((count, 128), lambda p: (0, p))
    far = pl.BlockSpec((span, 128), lambda p: (0, p))
    return pl.pallas_call(
        functools.partial(attend_back_kernel, chunk),
        grid=(4,),
        in_specs=[
            own,
            pl.BlockSpec((span, 128), lambda p: (0, p)),
            pl.BlockSpec((span, 128), lambda p: (0, 4 + p)),
            own,
            own,
        ],
        out_specs=[own, far, far],
        out_shape=[
            jax.ShapeDtypeStruct((count, 512), BF16),
            jax.ShapeDtypeStruct((span, 512), BF16),
            jax.ShapeDtypeStruct((span, 512), BF16),
        ],
        compiler_params=params(40),
        cost_estimate=cost(32 * count * span * 1024, 8 * 2**20),
        name="attend_back",
    )(q_source, kv_source, kv_source, scaled, extra)


def norm_parts(tensor):
    center = tensor - jnp.mean(tensor, axis=-1, keepdims=True)
    scale = lax.rsqrt(jnp.mean(center * center, axis=-1, keepdims=True) + EPSILON)
    return center * scale, scale


def norm_back(q, normed, scale):
    return scale * (
        q - jnp.mean(q, axis=-1, keepdims=True) - normed * jnp.mean(q * normed, axis=-1, keepdims=True)
    )


def place_blocks(own_ref, sources, target, sems):
    copies = []
    for core in range(2):
        source = sources[core]
        by_seq = len(source.shape) == 4
        seq_count = source.shape[0] if by_seq else 1
        z_count, rows, cols = source.shape[-3:]
        by_rows = by_seq and cols == target.shape[1]
        for j in range(seq_count):
            for i in range(z_count):
                block = 2 * (own_ref[1] ^ i) + (own_ref[2] ^ core)
                across = slice(None)
                if by_rows:
                    block = block * seq_count + (own_ref[0] ^ j)
                elif by_seq:
                    across = pl.ds(pl.multiple_of((own_ref[0] ^ j) * cols, cols), cols)
                down = pl.ds(pl.multiple_of(block * rows, rows), rows)
                piece = source.at[j, i] if by_seq else source.at[i]
                copy = pltpu.make_async_copy(piece, target.at[down, across], sems.at[len(copies)])
                copies.append(copy)
    return copies


def fetches(own_ref, refs, target, sems, cols=None):
    if cols is not None:
        axes = len(refs[0].shape) - 1
        refs = [ref.at[(slice(None),) * axes + (cols,)] for ref in refs]
        target = target.at[:, cols]
    if len(refs) == 2:
        return place_blocks(own_ref, refs, target, sems)
    return [pltpu.make_async_copy(refs[0], target, sems.at[0])]


def launch(copies):
    for copy in copies:
        copy.start()


def finish(copies):
    for copy in copies:
        copy.wait()


def hand_out(held, outs, sems):
    sources = [held] if len(outs) == 1 else [held.at[0], held.at[1]]
    copies = [
        pltpu.make_async_copy(source, out, sems.at[i])
        for i, (source, out) in enumerate(zip(sources, outs))
    ]
    launch(copies)
    finish(copies)


def outs_of(shape, split):
    if split:
        return [jax.ShapeDtypeStruct(shape[1:], BF16)] * 2
    return [jax.ShapeDtypeStruct(shape, BF16)]


def copies_of(parts):
    count = 1
    for size in parts[0].shape[:-2]:
        count *= size
    return max(1, count * len(parts))


def project_kernel(chunk, parts, own_ref, hidden_ref, gain_ref, *refs):
    sources, (normed_out, out_ref, whole_out, normed_ref, whole_ref, sems, out_sems) = (
        refs[:parts],
        refs[parts:],
    )
    copies = fetches(own_ref, sources, whole_ref, sems)
    launch(copies)
    count = hidden_ref.shape[0]
    for row in range(0, count, chunk):
        at = slice(row, row + chunk)
        normed_ref[at, :] = (norm_parts(hidden_ref[at, :])[0] * gain_ref[...]).astype(BF16)
    finish(copies)
    copies = [
        pltpu.make_async_copy(normed_ref, normed_out, out_sems.at[0]),
        pltpu.make_async_copy(whole_ref, whole_out, out_sems.at[1]),
    ]
    launch(copies)
    for row in range(0, count, chunk):
        at = slice(row, row + chunk)
        out_ref[at, :] = nn(normed_ref[at, :], whole_ref[...]).astype(BF16)
    finish(copies)


def project(own, hidden, gain, parts, cols):
    count, width = hidden.shape
    in_hbm = pl.BlockSpec(memory_space=pltpu.HBM)
    return pl.pallas_call(
        functools.partial(project_kernel, min(512, count), len(parts)),
        in_specs=[pl.BlockSpec(memory_space=pltpu.SMEM)]
        + [IN_VMEM] * 2
        + [pl.BlockSpec(memory_space=pl.ANY)] * len(parts),
        out_specs=[in_hbm, IN_VMEM, in_hbm],
        scratch_shapes=[
            pltpu.VMEM((count, width), BF16),
            pltpu.VMEM((width, cols), BF16),
            pltpu.SemaphoreType.DMA((copies_of(parts),)),
            pltpu.SemaphoreType.DMA((2,)),
        ],
        out_shape=[
            pltpu.HBM((count, width), BF16),
            jax.ShapeDtypeStruct((count, cols), BF16),
            pltpu.HBM((width, cols), BF16),
        ],
        compiler_params=params(10),
        cost_estimate=cost(2 * count * width * cols, 8 * 2**20),
        name="project",
    )(own, hidden, gain, *parts)


def rise_kernel(cfg, own_ref, hidden_ref, att_ref, cot_ref, gain_ref, *refs):
    seq_count, dp_count, split, chunk, up_parts, down_parts = cfg
    up_sources, refs = refs[:up_parts], refs[up_parts:]
    down_sources, refs = refs[:down_parts], refs[down_parts:]
    outs = 2 if split else 1
    out_ref, normed_ref, scale_ref, slope_ref, w_up, w_down, *refs = refs
    grad_outs, refs = refs[:outs], refs[outs:]
    act_ref, cot_t, grad_ref, up_sems, down_sems, out_sems = refs
    count, width = hidden_ref.shape
    raised = act_ref.shape[1]
    up_copies = [
        fetches(own_ref, up_sources, w_up, up_sems.at[i], slice(start, start + 512))
        for i, start in enumerate(range(0, width + raised, 512))
    ]
    down_copies = fetches(own_ref, down_sources, w_down, down_sems)
    for copies in up_copies[:2] + [down_copies] + up_copies[2:]:
        launch(copies)
    cot_t[...] = cot_ref[...].T
    finish(up_copies[0])
    for row in range(0, count, chunk):
        at = slice(row, row + chunk)
        first = hidden_ref[at, :] + nn(att_ref[at, :], w_up[:, :width])
        normed, scale = norm_parts(first)
        normed_ref[at, :] = normed
        scale_ref[at, :] = jnp.broadcast_to(scale, (chunk, scale_ref.shape[1]))
        normed_two = (normed * gain_ref[...]).astype(BF16)
        total = first
        for start in range(0, raised, 512):
            stop = start + 512
            if row == 0:
                finish(up_copies[1 + start // 512])
            v = nn(normed_two, w_up[:, width + start : width + stop])
            square = v * v
            t = jnp.tanh(v * (0.7978845608028654 + 0.035677408136300125 * square))
            half = 0.5 + 0.5 * t
            act = (v * half).astype(BF16)
            slope = half + v * (0.5 - 0.5 * t * t) * (
                0.7978845608028654 + 0.10703222440890037 * square
            )
            act_ref[at, start:stop] = act
            slope_ref[at, start:stop] = slope.astype(BF16)
            if row == 0 and start == 0:
                finish(down_copies)
            total = total + nn(act, w_down[start:stop, :])
        out_ref[at, :] = total.astype(BF16)
    if not split:
        for start in range(0, raised, 512):
            grad_ref[:, start : start + 512] = nn(
                cot_t[...], act_ref[:, start : start + 512]
            ).astype(BF16)
        hand_out(grad_ref, grad_outs, out_sems)
        return
    cols = width // seq_count
    rows = raised // dp_count
    copies = []
    for i in range(dp_count // 2):
        result = nn(cot_t[...], act_ref[:, 2 * i * rows : 2 * (i + 1) * rows]).astype(BF16)
        z = i ^ own_ref[1]
        for s in range(seq_count):
            piece = result[s * cols : (s + 1) * cols, :]
            for core in range(2):
                for part in range(rows // 128):
                    col = core * rows + part * 128
                    grad_ref[core ^ own_ref[2], z, s ^ own_ref[0], part] = piece[:, col : col + 128]
        for core in range(2):
            copy = pltpu.make_async_copy(
                grad_ref.at[core, z], grad_outs[core].at[z], out_sems.at[len(copies)]
            )
            copies.append(copy)
            copy.start()
    finish(copies)


def rise(own, hidden, att, cot, gain, up_parts, down_parts, raised, seq_count, dp_count, split):
    count, width = hidden.shape
    if split:
        parts = raised // dp_count // 128
        grad_shape = (2, dp_count // 2, seq_count, parts, width // seq_count, 128)
    else:
        grad_shape = (width, raised)
    chunk = min(512, count)
    cfg = (seq_count, dp_count, split, chunk, len(up_parts), len(down_parts))
    grads = outs_of(grad_shape, split)
    up_shape, down_shape = (width, width + raised), (raised, width)
    anywhere = pl.BlockSpec(memory_space=pl.ANY)
    return pl.pallas_call(
        functools.partial(rise_kernel, cfg),
        in_specs=[pl.BlockSpec(memory_space=pltpu.SMEM)]
        + [IN_VMEM] * 4
        + [anywhere] * (len(up_parts) + len(down_parts)),
        out_specs=[IN_VMEM] * 6 + [anywhere] * len(grads),
        scratch_shapes=[
            pltpu.VMEM((count, raised), BF16),
            pltpu.VMEM((width, count), BF16),
            pltpu.VMEM(grad_shape, BF16),
            pltpu.SemaphoreType.DMA(((width + raised) // 512, copies_of(up_parts))),
            pltpu.SemaphoreType.DMA((copies_of(down_parts),)),
            pltpu.SemaphoreType.DMA((dp_count,)),
        ],
        out_shape=[
            jax.ShapeDtypeStruct((count, width), BF16),
            jax.ShapeDtypeStruct((count, width), F32),
            jax.ShapeDtypeStruct((count, 128), F32),
            jax.ShapeDtypeStruct((count, raised), BF16),
            jax.ShapeDtypeStruct(up_shape, BF16),
            jax.ShapeDtypeStruct(down_shape, BF16),
        ]
        + grads,
        compiler_params=params(15),
        cost_estimate=cost(7 * 2**30, 24 * 2**20),
        name="rise",
    )(own, hidden, att, cot, gain, *up_parts, *down_parts)


def fall_kernel(
    cfg,
    own_ref,
    cot_ref,
    slope_ref,
    normed_ref,
    scale_ref,
    att_ref,
    den_ref,
    gain_ref,
    w_up,
    w_down,
    first_ref,
    scaled_ref,
    extra_ref,
    gain_sum_ref,
    *refs,
):
    seq_count, dp_count, split, chunk = cfg
    outs = 2 if split else 1
    grad_outs, (raise_ref, normed_t, att_t, branch_ref, grad_ref, out_sems) = (
        refs[:outs],
        refs[outs:],
    )
    count, width = cot_ref.shape
    raised = raise_ref.shape[1]
    gain = gain_ref[...]
    lane = lax.broadcasted_iota(jnp.int32, (128, width), 1)
    spread = lax.broadcasted_iota(jnp.int32, (128, width), 0) == 16 * (lane // 64)
    spread = jnp.where(spread, 1.0, 0.0).astype(BF16)
    row = lax.broadcasted_iota(jnp.int32, (128, 128), 0)
    col = lax.broadcasted_iota(jnp.int32, (128, 128), 1)
    swap = jnp.where((row < 64) != (col < 64), 1.0, 0.0).astype(BF16)
    even = lax.broadcasted_iota(jnp.int32, (1, 128), 1) % 2 == 0
    gain_sum = jnp.zeros((1, width), F32)
    att_t[...] = att_ref[...].T
    for top in range(0, count, chunk):
        at = slice(top, top + chunk)
        cot = cot_ref[at, :]
        normed = normed_ref[at, :]
        normed_t[:, at] = (normed * gain).astype(BF16).T
        back = jnp.zeros((chunk, width), F32)
        for start in range(0, raised, 512):
            stop = start + 512
            grad_raised = (nt(cot, w_down[start:stop, :]) * slope_ref[at, start:stop]).astype(BF16)
            raise_ref[at, start:stop] = grad_raised
            back = back + nt(grad_raised, w_up[:, width + start : width + stop])
        gain_sum = gain_sum + jnp.sum(back * normed, axis=0, keepdims=True)
        grad_first = cot.astype(F32) + norm_back(back * gain, normed, scale_ref[at, :1])
        first_ref[at, :] = grad_first
        branch = grad_first.astype(BF16)
        branch_ref[at, :] = branch
        inverse = 1.0 / den_ref[at, :]
        coarse = inverse.astype(BF16)
        fine = (inverse - coarse.astype(F32)).astype(BF16)
        ratio = nt(branch, w_up[:, :width]) * (nn(coarse, spread) + nn(fine, spread))
        scaled_ref[at, :] = ratio.astype(BF16)
        product = ratio * att_ref[at, :]
        coarse = product.astype(BF16)
        fine = (product - coarse.astype(F32)).astype(BF16)
        for start in range(0, width, 128):
            stop = start + 128
            offset = nn(coarse[:, start:stop], swap) + nn(fine[:, start:stop], swap)
            upper = offset.astype(BF16)
            lower = (offset - upper.astype(F32)).astype(BF16)
            extra_ref[at, start:stop] = jnp.where(even, upper, lower)
    gain_sum_ref[...] = gain_sum
    if not split:
        grad_ref[:, :width] = nn(att_t[...], branch_ref[...]).astype(BF16)
        for start in range(0, raised, 512):
            grad_ref[:, width + start : width + start + 512] = nn(
                normed_t[...], raise_ref[:, start : start + 512]
            ).astype(BF16)
        hand_out(grad_ref, grad_outs, out_sems)
        return
    cols = raised // seq_count
    wide = width // seq_count
    rows = width // dp_count
    copies = []

    def keep(result, s, at):
        for d in range(dp_count):
            grad_ref[(d % 2) ^ own_ref[2], s ^ own_ref[0], (d // 2) ^ own_ref[1], :, at] = result[
                d * rows : (d + 1) * rows, :
            ]

    result = nn(att_t[...], branch_ref[...]).astype(BF16)
    for s in range(seq_count):
        keep(result[:, s * wide : (s + 1) * wide], s, slice(0, wide))
    for s in range(seq_count):
        result = nn(normed_t[...], raise_ref[:, s * cols : (s + 1) * cols]).astype(BF16)
        keep(result, s, slice(wide, wide + cols))
        for core in range(2):
            copy = pltpu.make_async_copy(
                grad_ref.at[core, s ^ own_ref[0]],
                grad_outs[core].at[s ^ own_ref[0]],
                out_sems.at[len(copies)],
            )
            copies.append(copy)
            copy.start()
    finish(copies)


def fall(own, cot, slope, normed, scale, att, den, gain, w_up, w_down, seq_count, dp_count, split):
    count, width = cot.shape
    raised = w_down.shape[0]
    if split:
        grad_shape = (2, seq_count, dp_count // 2, width // dp_count, (width + raised) // seq_count)
    else:
        grad_shape = (width, width + raised)
    grads = outs_of(grad_shape, split)
    cfg = (seq_count, dp_count, split, min(512, count))

    def sds(dtype):
        return jax.ShapeDtypeStruct((count, width), dtype)

    return pl.pallas_call(
        functools.partial(fall_kernel, cfg),
        in_specs=[pl.BlockSpec(memory_space=pltpu.SMEM)] + [IN_VMEM] * 9,
        out_specs=[IN_VMEM] * 4 + [pl.BlockSpec(memory_space=pl.ANY)] * len(grads),
        scratch_shapes=[
            pltpu.VMEM((count, raised), BF16),
            pltpu.VMEM((width, count), BF16),
            pltpu.VMEM((width, count), BF16),
            pltpu.VMEM((count, width), BF16),
            pltpu.VMEM(grad_shape, BF16),
            pltpu.SemaphoreType.DMA((2 * seq_count,)),
        ],
        out_shape=[
            sds(F32),
            sds(BF16),
            sds(BF16),
            jax.ShapeDtypeStruct((1, width), F32),
        ]
        + grads,
        compiler_params=params(17),
        cost_estimate=cost(8 * 2**30, 24 * 2**20),
        name="fall",
    )(own, cot, slope, normed, scale, att, den, gain, w_up, w_down)


def last_kernel(chunk, hidden_ref, first_ref, gain_ref, mask_ref, w_ref, *refs):
    *grads, out_ref, sums_ref = refs
    masked = gain_sum = 0.0
    for top in range(0, hidden_ref.shape[0], chunk):
        at = slice(top, top + chunk)
        back = 0.0
        start = 0
        for ref in grads:
            stop = start + ref.shape[1]
            back = back + nt(ref[at, :], w_ref[:, start:stop])
            start = stop
        normed, scale = norm_parts(hidden_ref[at, :])
        grad = first_ref[at, :] + norm_back(back * gain_ref[...], normed, scale)
        coarse = grad.astype(BF16)
        out_ref[at, :] = coarse
        fine = (grad - coarse.astype(F32)).astype(BF16)
        mask = mask_ref[:, at]
        masked = masked + nn(mask, coarse) + nn(mask, fine)
        gain_sum = gain_sum + jnp.sum(back * normed, axis=0, keepdims=True)
    sums_ref[...] = masked
    sums_ref[1:2, :] = gain_sum


def last(hidden, grad_first, gain, mask, w_qkv, grads):
    count, width = hidden.shape
    return pl.pallas_call(
        functools.partial(last_kernel, min(512, count)),
        in_specs=[IN_VMEM] * (5 + len(grads)),
        out_specs=[IN_VMEM] * 2,
        out_shape=[
            jax.ShapeDtypeStruct((count, width), BF16),
            jax.ShapeDtypeStruct((8, width), F32),
        ],
        compiler_params=params(8),
        cost_estimate=cost(8 * (6 * count * width * width), 8 * (12 * 2**20)),
        name="last",
    )(hidden, grad_first, gain, mask, w_qkv, *grads)


def swap_along(value, axis, mask):
    count = lax.axis_size(axis)
    return lax.ppermute(value, axis, [(i, i ^ mask) for i in range(count)])


def add_up(values):
    total = values[0].astype(F32)
    for value in values[1:]:
        total = total + value.astype(F32)
    return total


def together(*values):
    return lax.optimization_barrier(values)


def from_plane(values):
    return [values[0]] + [swap_along(values[j], "seq", j) for j in range(1, len(values))]


def from_line(values):
    return [values[0]] + [swap_along(values[j], "dp", 2 * j) for j in range(1, len(values))]


def other_core(value):
    return swap_along(value, "dp", 1)


def add_split(left, right):
    return [add_up((left[j], right[j])).astype(BF16) for j in range(left.shape[0])]


def both_cores(value):
    return [value, other_core(value)]


def split_first(value):
    return [value[j] for j in range(value.shape[0])]


def halve_line(value):
    half = value.shape[0] // 2
    while half:
        came = swap_along(value[half:], "dp", 2 * half)
        value = add_up((value[:half], came))
        half //= 2
        if half:
            value = value.astype(BF16)
    return value[0]


def gather_line(value):
    return jnp.stack(from_line([value] * (lax.axis_size("dp") // 2)))


def gather_plane(value):
    return jnp.stack(from_plane([value] * lax.axis_size("seq")))


def own_columns(weight):
    cols = weight.shape[1] // lax.axis_size("seq")
    return lax.dynamic_slice_in_dim(weight, lax.axis_index("seq") * cols, cols, 1)


def pieces_of(whole, own, seq_count, dp_count, flipped):
    row_blocks, col_blocks = (seq_count, dp_count) if flipped else (dp_count, seq_count)
    rows, cols = whole.shape[0] // row_blocks, whole.shape[1] // col_blocks
    whole = whole.reshape(row_blocks, rows, col_blocks, cols)
    whole = jnp.transpose(whole, (0, 2, 1, 3) if flipped else (2, 0, 1, 3))
    whole = whole.reshape(seq_count, dp_count // 2, 2, rows, cols)
    whole = jnp.take(whole, jnp.arange(seq_count) ^ own[0], axis=0)
    whole = jnp.take(whole, jnp.arange(dp_count // 2) ^ own[1], axis=1)
    whole = jnp.take(whole, jnp.arange(2) ^ own[2], axis=2)
    return jnp.transpose(whole, (2, 0, 1, 3, 4))


def per_device(
    inputs,
    cotangent,
    timestep,
    unmask_order,
    mask_embed,
    ln1_gain,
    weight_qkv,
    weight_out,
    ln2_gain,
    weight_up,
    weight_down,
):
    rows, segment, width = inputs.shape
    raised = weight_up.shape[1]
    seq_count, dp_count = lax.axis_size("seq"), lax.axis_size("dp")
    outer = seq_count // rows
    split = outer == 1 and (seq_count, dp_count) == (4, 8)
    place = lax.axis_index("seq")
    dp_place = lax.axis_index("dp")
    row = place % rows
    own = jnp.stack([place, dp_place // 2, dp_place % 2]).astype(jnp.int32)

    def by_partner(value):
        return [lax.dynamic_index_in_dim(value, row ^ j, 0, keepdims=False) for j in range(rows)]

    def to_rows(value):
        return jnp.concatenate(from_plane(by_partner(value)))

    def to_partners(value):
        return from_plane([value[j * segment : (j + 1) * segment] for j in range(rows)])

    def by_row(parts):
        out = jnp.zeros((rows,) + parts[0].shape, parts[0].dtype)
        for j in (0, 3, 2, 1) if rows == 4 else range(rows):
            out = lax.dynamic_update_index_in_dim(out, parts[j], row ^ j, 0)
        return out

    masked = (unmask_order <= timestep[:, None]).astype(BF16)
    masked = jnp.pad(masked[:, None, :], ((0, 0), (0, 15), (0, width - segment)))
    came = by_partner(jnp.concatenate((inputs, masked), axis=1))
    up_and_out = jnp.concatenate((weight_out, weight_up), axis=1)
    if split:
        down_rows = weight_down.shape[0] // seq_count
        own_down = lax.dynamic_slice_in_dim(weight_down, place * down_rows, down_rows, 0)
        line = gather_line(jnp.concatenate((own_columns(weight_qkv), own_down), axis=1))
        came = from_plane(came)
        line, up_and_out = together(line, up_and_out)
        line_up = jnp.stack((up_and_out, swap_along(up_and_out, "dp", 4)))
        line_up = [line_up, swap_along(line_up, "dp", 2)]
        plane_qkv = gather_plane(line[..., :-width])
        line_down = line[..., -width:].reshape(-1, width)
        plane_qkv, line_down, cot = together(plane_qkv, line_down, cotangent)
        parts_qkv = both_cores(plane_qkv)
        cot = from_plane([jnp.concatenate((part, line_down)) for part in by_partner(cot)])
    else:
        came, cot = from_plane(came), from_plane(by_partner(cotangent))
        parts_qkv, parts_up, parts_down = (
            [lax.all_gather(weight, "dp", axis=0, tiled=True)]
            for weight in (weight_qkv, up_and_out, weight_down)
        )

    block = jnp.concatenate([part[:segment] for part in came]).astype(F32)
    mask_row = jnp.concatenate([part[segment, :segment] for part in came])
    hidden = block + mask_row.astype(F32)[:, None] * mask_embed
    normed_one, projected, whole_qkv = project(
        own, hidden, ln1_gain[None, :], parts_qkv, 3 * width
    )
    if outer > 1:
        groups = [[j * rows + i for j in range(outer)] for i in range(rows)]
        far = lax.all_gather(
            projected[:, width:], "seq", axis=0, tiled=True, axis_index_groups=groups
        )
        attended, denominators = attend(projected, far, 0)
    else:
        attended, denominators = attend_row(projected)
    if split:
        line_up, attended = together(line_up, attended)
        parts_up = both_cores(jnp.stack(line_up, axis=1).reshape((-1,) + up_and_out.shape))
        cot, parts_up[0] = together(cot, parts_up[0])
        plane_down = jnp.stack([part[segment:] for part in cot])
        plane_down = plane_down.reshape(seq_count, dp_count // 2, -1, width)
        parts_down = both_cores(plane_down)
    cot = jnp.concatenate([part[:segment] for part in cot])
    outputs, normed, scale, slope, whole_up, whole_down, *grad_down = rise(
        own,
        hidden,
        attended,
        cot,
        ln2_gain[None, :],
        parts_up,
        parts_down,
        raised,
        seq_count,
        dp_count,
        split,
    )
    result = to_partners(outputs)
    grad_first, scaled, extra, sum_gain_two, *grad_up = fall(
        own,
        cot,
        slope,
        normed,
        scale,
        attended,
        denominators,
        ln2_gain[None, :],
        whole_up,
        whole_down,
        seq_count,
        dp_count,
        split,
    )
    mask_rows = jnp.broadcast_to(mask_row[None, :], (8, mask_row.shape[0]))
    if split:
        grad_down[1] = other_core(grad_down[1])
        grad_down, scaled, grad_up, result = together(grad_down, scaled, grad_up, result)
        line_down = from_line(add_split(*grad_down))
        grad_up[1] = other_core(grad_up[1])
        half = attend_back_half(projected, scaled, extra)
        grad_up, half, line_down[1] = together(grad_up, half, line_down[1])
        plane_up = from_plane(add_split(*grad_up))
        *rest, mine_qkv, other_qkv = attend_back_sum(
            own, projected, scaled, extra, normed_one, half, seq_count, dp_count
        )
        plane_up, line_down, rest, mine_qkv, other_qkv = together(
            plane_up, line_down, rest, mine_qkv, other_qkv
        )
        grads = [part for pair in zip(half, rest) for part in pair]
        both_qkv = (mine_qkv, other_core(other_qkv))
        line_up = add_up(plane_up).astype(BF16)
        z_half = line_up.shape[0] // 2
        line_came = swap_along(line_up[z_half:], "dp", 2 * z_half)
        tall = width // dp_count
        down = add_up(line_down).astype(BF16).reshape(seq_count, -1, tall, 128)
        both_qkv, mask_rows = together(both_qkv, mask_rows)
        mine_qkv = [part.reshape(-1, tall, 128) for part in add_split(*both_qkv)]
        plane_last = from_plane([jnp.concatenate((mine_qkv[j], down[j])) for j in range(seq_count)])
    else:
        dq, dk, dv = attend_back(projected, far, scaled, extra)
        both = jnp.concatenate((dk, dv), axis=1)
        both = lax.psum_scatter(
            both, "seq", scatter_dimension=0, tiled=True, axis_index_groups=groups
        )
        grads = [dq, both]
        grad_qkv = lax.dot_general(
            normed_one,
            jnp.concatenate(grads, axis=1),
            (((0,), (0,)), ((), ())),
            preferred_element_type=F32,
        ).astype(BF16)
        cut = functools.partial(pieces_of, own=own, seq_count=seq_count, dp_count=dp_count)
        (grad_up,), (grad_down,) = grad_up, grad_down
        grad_out, grad_up = (
            cut(part, flipped=False) for part in (grad_up[:, :width], grad_up[:, width:])
        )
        grad_up = jnp.concatenate((grad_out, grad_up), axis=-1)
        grad_qkv = cut(grad_qkv, flipped=False)
        grad_down = cut(grad_down, flipped=True)
        sums = []
        for pieces in (grad_qkv, grad_up, grad_down):
            mine = add_up((pieces[0], other_core(pieces[1]))).astype(BF16)
            plane = add_up(from_plane(split_first(mine))).astype(BF16)
            sums.append(add_up(from_line(split_first(plane))))
        sum_qkv, sum_up, sum_down = sums
        sum_down = sum_down.T
    grad_hidden, sums = last(
        hidden, grad_first, ln1_gain[None, :], mask_rows, whole_qkv, grads
    )
    vectors = jnp.concatenate((sums[0:2], sum_gain_two, jnp.zeros((5, width), F32)), axis=0)
    vectors = vectors + other_core(vectors)
    bit = 2
    while bit < dp_count:
        vectors = vectors + swap_along(vectors, "dp", bit)
        bit *= 2
    if split:
        grad_hidden, vectors, line_came, plane_last = together(
            grad_hidden, vectors, line_came, plane_last
        )
        sum_up = add_up((line_up[:z_half], line_came)).astype(BF16)
        kinds = mine_qkv[0].shape[0]
        sum_qkv = add_up([part[:kinds] for part in plane_last]).astype(BF16)
        sum_qkv = sum_qkv.reshape((dp_count // 2, -1) + sum_qkv.shape[1:])
        line_came = swap_along(sum_qkv[z_half:], "dp", 2 * z_half)
        line_came, plane_last, sum_up = together(line_came, plane_last, sum_up)
        sum_qkv = halve_line(add_up((sum_qkv[:z_half], line_came)).astype(BF16))
        sum_up = halve_line(sum_up)
        sum_down = add_up([part[kinds:] for part in plane_last])
        sum_down = sum_down.reshape(-1, width // seq_count, 128)
        sum_down = jnp.transpose(sum_down, (0, 2, 1)).reshape(-1, width // seq_count)
        sum_qkv = jnp.transpose(sum_qkv, (1, 0, 2)).reshape(tall, -1)
    grad_inputs = [grad_hidden[j * segment : (j + 1) * segment] for j in range(rows)]
    if split:
        coarse = vectors.astype(BF16)
        terms = jnp.concatenate((coarse, (vectors - coarse.astype(F32)).astype(BF16)))
        grad_inputs = [jnp.concatenate((part, terms)) for part in grad_inputs]
    grad_inputs = from_plane(grad_inputs)
    if split:
        vectors = add_up([part[segment:] for part in grad_inputs])
        vectors = vectors[:8] + vectors[8:]
        grad_inputs = [part[:segment] for part in grad_inputs]
    else:
        vectors = add_up(from_plane([vectors] * seq_count))
    block_width = width // dp_count
    vectors = lax.dynamic_slice_in_dim(vectors, dp_place * block_width, block_width, 1)
    out_cols = width // seq_count
    return (
        by_row(result),
        by_row(grad_inputs),
        vectors[0],
        vectors[1],
        sum_qkv,
        sum_up[:, :out_cols],
        vectors[2],
        sum_up[:, out_cols:],
        sum_down,
    )


def solution(mesh):
    in_specs = (
        P("dp", "seq", None),
        P("dp", "seq", None),
        P("dp"),
        P("dp", "seq"),
        P(),
        P(),
        P("dp", None),
        P("dp", None),
        P(),
        P("dp", None),
        P("dp", None),
    )
    out_specs = (
        P("dp", "seq", None),
        P("dp", "seq", None),
        P("dp"),
        P("dp"),
        P("dp", "seq"),
        P("dp", "seq"),
        P("dp"),
        P("dp", "seq"),
        P("dp", "seq"),
    )
    return jax.shard_map(
        per_device, mesh=mesh, in_specs=in_specs, out_specs=out_specs, check_vma=False
    )
```

```python
import functools

import jax
import jax.numpy as jnp
from jax import lax
from jax.experimental import pallas as pl
from jax.experimental.pallas import tpu as pltpu
from jax.sharding import PartitionSpec as P

EPSILON = 1e-05
HEADS = 8
F32 = jnp.float32
BF16 = jnp.bfloat16
IN_VMEM = pl.BlockSpec(memory_space=pltpu.VMEM)


def nn(left, right):
    return jnp.dot(left, right, preferred_element_type=F32)


def nt(left, right):
    return lax.dot_general(left, right, (((1,), (1,)), ((), ())), preferred_element_type=F32)


def params(vmem):
    return pltpu.CompilerParams(vmem_limit_bytes=vmem * 2**20)


def cost(flops, bytes_accessed):
    return pl.CostEstimate(
        flops=int(flops), bytes_accessed=int(bytes_accessed), transcendentals=0
    )


def attend_kernel(chunk, q_ref, k_ref, v_ref, out_ref, den_ref):
    count = q_ref.shape[0]
    pair = pl.program_id(0)
    lane = lax.broadcasted_iota(jnp.int32, (1, 128), 1)
    low = lane < 64
    keys = k_ref[...]
    values = v_ref[...]
    one = jnp.ones_like(values)
    values_low = jnp.where(low, values, one)
    values_high = jnp.where(low, one, values)
    for start in range(0, count, chunk):
        at = slice(start, start + chunk)
        q = q_ref[at, :] * jnp.asarray(0.125, BF16)
        zero = jnp.zeros_like(q)
        left = nn(jnp.exp(nt(jnp.where(low, q, zero), keys)).astype(BF16), values_low)
        right = nn(jnp.exp(nt(jnp.where(low, zero, q), keys)).astype(BF16), values_high)
        swapped = jnp.where(low, right, left)
        den = pltpu.roll(swapped, 64, 1)
        out_ref[at, :] = (jnp.where(low, left, right) / den).astype(BF16)
        first = lane // 16 == 2 * pair
        second = lane // 16 == 2 * pair + 1
        mine = jnp.where(
            first, jnp.where(low, den, swapped), jnp.where(low, swapped, den)
        )
        den_ref[at, :] = jnp.where(first | second, mine, den_ref[at, :])


def attend(q_source, kv_source, kv_shift):
    count, span = q_source.shape[0], kv_source.shape[0]
    chunk = min(256, count)
    return pl.pallas_call(
        functools.partial(attend_kernel, chunk),
        grid=(4,),
        in_specs=[
            pl.BlockSpec((count, 128), lambda p: (0, p)),
            pl.BlockSpec((span, 128), lambda p: (0, kv_shift + p)),
            pl.BlockSpec((span, 128), lambda p: (0, kv_shift + 4 + p)),
        ],
        out_specs=[
            pl.BlockSpec((count, 128), lambda p: (0, p)),
            pl.BlockSpec((count, 128), lambda p: (0, 0)),
        ],
        out_shape=[
            jax.ShapeDtypeStruct((count, 512), BF16),
            jax.ShapeDtypeStruct((count, 128), F32),
        ],
        compiler_params=params(12),
        cost_estimate=cost(16 * count * span * 1024, 5 * 2**20),
        name="attend",
    )(q_source, kv_source, kv_source)


def attend_row_kernel(chunk, own_ref, out_ref, den_ref):
    count, width = out_ref.shape
    lane = lax.broadcasted_iota(jnp.int32, (1, 128), 1)
    low = lane < 64
    for start in range(0, count, chunk):
        at = slice(start, start + chunk)
        sums = jnp.zeros((chunk, 128), F32)
        for pair in range(width // 128):
            col = pair * 128
            keys = own_ref[:, width + col : width + col + 128]
            values = own_ref[:, 2 * width + col : 2 * width + col + 128]
            one = jnp.ones_like(values)
            q = own_ref[at, col : col + 128] * jnp.asarray(0.125, BF16)
            zero = jnp.zeros_like(q)
            left = nn(
                jnp.exp(nt(jnp.where(low, q, zero), keys)).astype(BF16),
                jnp.where(low, values, one),
            )
            right = nn(
                jnp.exp(nt(jnp.where(low, zero, q), keys)).astype(BF16),
                jnp.where(low, one, values),
            )
            swapped = jnp.where(low, right, left)
            den = pltpu.roll(swapped, 64, 1)
            out_ref[at, col : col + 128] = (jnp.where(low, left, right) / den).astype(BF16)
            first, second = lane // 16 == 2 * pair, lane // 16 == 2 * pair + 1
            sums = jnp.where(first, jnp.where(low, den, swapped), sums)
            sums = jnp.where(second, jnp.where(low, swapped, den), sums)
        den_ref[at, :] = sums


def attend_row(projected):
    count, width = projected.shape[0], projected.shape[1] // 3
    return pl.pallas_call(
        functools.partial(attend_row_kernel, min(256, count)),
        in_specs=[IN_VMEM],
        out_specs=[IN_VMEM] * 2,
        out_shape=[
            jax.ShapeDtypeStruct((count, width), BF16),
            jax.ShapeDtypeStruct((count, 128), F32),
        ],
        compiler_params=params(8),
        cost_estimate=cost(16 * count * count * 1024, 5 * 2**20),
        name="attend_row",
    )(projected)


def head_pair_back(chunk, q_ref, k_ref, v_ref, s_ref, x_ref, dk_ref, dv_ref):
    count, span = q_ref.shape[0], k_ref.shape[0]
    lane = lax.broadcasted_iota(jnp.int32, (1, 128), 1)
    low = lane < 64
    q = q_ref[...] * jnp.asarray(0.125, BF16)
    scaled = s_ref[...]
    extra = x_ref[...]
    zero = jnp.zeros_like(q)
    q_own = (jnp.where(low, q, zero), jnp.where(low, zero, q))
    s_own = (jnp.where(low, scaled, zero), jnp.where(low, zero, scaled))
    s_with = (jnp.where(low, scaled, extra), jnp.where(low, extra, scaled))
    minus = (
        jnp.where((lane == 64) | (lane == 65), -1.0, 0.0).astype(BF16),
        jnp.where((lane == 0) | (lane == 1), -1.0, 0.0).astype(BF16),
    )
    total = jnp.zeros((128, count), F32)
    for start in range(0, span, chunk):
        keys = k_ref[start : start + chunk, :]
        values = v_ref[start : start + chunk, :]
        none = jnp.zeros_like(keys)
        k_own = (jnp.where(low, keys, none), jnp.where(low, none, keys))
        v_with = (jnp.where(low, values, minus[0]), jnp.where(low, minus[1], values))
        dk = dv = 0.0
        for head in range(2):
            weights = jnp.exp(nt(keys, q_own[head]))
            slopes = (weights * nt(v_with[head], s_with[head])).astype(BF16)
            dv = dv + nn(weights.astype(BF16), s_own[head])
            dk = dk + nn(slopes, q_own[head])
            total = total + nn(k_own[head].T, slopes)
        dk_ref[start : start + chunk, :] = dk.astype(BF16)
        dv_ref[start : start + chunk, :] = dv.astype(BF16)
    return (total.T * 0.125).astype(BF16)


def attend_back_kernel(chunk, q_ref, k_ref, v_ref, s_ref, x_ref, dq_ref, dk_ref, dv_ref):
    dq_ref[...] = head_pair_back(chunk, q_ref, k_ref, v_ref, s_ref, x_ref, dk_ref, dv_ref)


def pair_views(col, width, proj_ref, s_ref, x_ref):
    at = [slice(shift + col, shift + col + 128) for shift in (0, width, 2 * width)]
    return [proj_ref.at[:, cols] for cols in at] + [s_ref.at[:, at[0]], x_ref.at[:, at[0]]]


def attend_back_half_kernel(chunk, proj_ref, s_ref, x_ref, dq_ref, dk_ref, dv_ref):
    width = s_ref.shape[1]
    for pair in range(2):
        col = pair * 128
        at = slice(col, col + 128)
        dq_ref[:, at] = head_pair_back(
            chunk,
            *pair_views(col, width, proj_ref, s_ref, x_ref),
            dk_ref.at[:, at],
            dv_ref.at[:, at],
        )


def attend_back_half(projected, scaled, extra):
    count, width = scaled.shape
    return pl.pallas_call(
        functools.partial(attend_back_half_kernel, min(512, count)),
        in_specs=[IN_VMEM] * 3,
        out_specs=[IN_VMEM] * 3,
        out_shape=[jax.ShapeDtypeStruct((count, width // 2), BF16)] * 3,
        compiler_params=params(9),
        cost_estimate=cost(16 * count * count * 1024, 6 * 2**20),
        name="attend_back_half",
    )(projected, scaled, extra)


def attend_back_sum_kernel(
    chunk,
    dp_count,
    own_ref,
    proj_ref,
    s_ref,
    x_ref,
    normed_ref,
    dq_first,
    dk_first,
    dv_first,
    dq_ref,
    dk_ref,
    dv_ref,
    mine_out,
    other_out,
    normed_t,
    joined,
    grad_ref,
    sems,
):
    width = s_ref.shape[1]
    normed_t[...] = normed_ref[...].T

    def weight_part(pair, refs):
        cols = slice((pair % 2) * 128, (pair % 2) * 128 + 128)
        for kind, ref in enumerate(refs):
            joined[:, kind * 128 : (kind + 1) * 128] = ref[:, cols]
        result = nn(normed_t[...], joined[...]).astype(BF16)
        rows = result.shape[0] // dp_count
        per = grad_ref.shape[3]
        for kind in range(3):
            block = pair + 4 * kind
            col, part = (block // per) ^ own_ref[0], block % per
            for d in range(dp_count):
                grad_ref[(d % 2) ^ own_ref[2], col, (d // 2) ^ own_ref[1], part] = result[
                    d * rows : (d + 1) * rows, kind * 128 : (kind + 1) * 128
                ]

    for pair in range(2):
        weight_part(pair, (dq_first, dk_first, dv_first))
    for pair in range(2, 4):
        at = slice((pair - 2) * 128, (pair - 1) * 128)
        dq_ref[:, at] = head_pair_back(
            chunk,
            *pair_views(pair * 128, width, proj_ref, s_ref, x_ref),
            dk_ref.at[:, at],
            dv_ref.at[:, at],
        )
        weight_part(pair, (dq_ref, dk_ref, dv_ref))
    hand_out(grad_ref, (mine_out, other_out), sems)


def attend_back_sum(own, projected, scaled, extra, normed, first_half, seq_count, dp_count):
    count, width = scaled.shape
    pieces = (2, seq_count, dp_count // 2, 12 // seq_count, width // dp_count, 128)
    return pl.pallas_call(
        functools.partial(attend_back_sum_kernel, min(512, count), dp_count),
        in_specs=[pl.BlockSpec(memory_space=pltpu.SMEM)] + [IN_VMEM] * 7,
        out_specs=[IN_VMEM] * 3 + [pl.BlockSpec(memory_space=pl.ANY)] * 2,
        scratch_shapes=[
            pltpu.VMEM((width, count), BF16),
            pltpu.VMEM((count, 384), BF16),
            pltpu.VMEM(pieces, BF16),
            pltpu.SemaphoreType.DMA((2,)),
        ],
        out_shape=[jax.ShapeDtypeStruct((count, width // 2), BF16)] * 3 + outs_of(pieces, True),
        compiler_params=params(11),
        cost_estimate=cost(20 * count * count * 1024, 10 * 2**20),
        name="attend_back_sum",
    )(own, projected, scaled, extra, normed, *first_half)


def attend_back(q_source, kv_source, scaled, extra):
    count, span = q_source.shape[0], kv_source.shape[0]
    chunk = min(512, span)
    own = pl.BlockSpec((count, 128), lambda p: (0, p))
    far = pl.BlockSpec((span, 128), lambda p: (0, p))
    return pl.pallas_call(
        functools.partial(attend_back_kernel, chunk),
        grid=(4,),
        in_specs=[
            own,
            pl.BlockSpec((span, 128), lambda p: (0, p)),
            pl.BlockSpec((span, 128), lambda p: (0, 4 + p)),
            own,
            own,
        ],
        out_specs=[own, far, far],
        out_shape=[
            jax.ShapeDtypeStruct((count, 512), BF16),
            jax.ShapeDtypeStruct((span, 512), BF16),
            jax.ShapeDtypeStruct((span, 512), BF16),
        ],
        compiler_params=params(40),
        cost_estimate=cost(32 * count * span * 1024, 8 * 2**20),
        name="attend_back",
    )(q_source, kv_source, kv_source, scaled, extra)


def norm_parts(tensor):
    center = tensor - jnp.mean(tensor, axis=-1, keepdims=True)
    scale = lax.rsqrt(jnp.mean(center * center, axis=-1, keepdims=True) + EPSILON)
    return center * scale, scale


def norm_back(q, normed, scale):
    return scale * (
        q - jnp.mean(q, axis=-1, keepdims=True) - normed * jnp.mean(q * normed, axis=-1, keepdims=True)
    )


def place_blocks(own_ref, sources, target, sems):
    copies = []
    for core in range(2):
        source = sources[core]
        by_seq = len(source.shape) == 4
        seq_count = source.shape[0] if by_seq else 1
        z_count, rows, cols = source.shape[-3:]
        by_rows = by_seq and cols == target.shape[1]
        for j in range(seq_count):
            for i in range(z_count):
                block = 2 * (own_ref[1] ^ i) + (own_ref[2] ^ core)
                across = slice(None)
                if by_rows:
                    block = block * seq_count + (own_ref[0] ^ j)
                elif by_seq:
                    across = pl.ds(pl.multiple_of((own_ref[0] ^ j) * cols, cols), cols)
                down = pl.ds(pl.multiple_of(block * rows, rows), rows)
                piece = source.at[j, i] if by_seq else source.at[i]
                copy = pltpu.make_async_copy(piece, target.at[down, across], sems.at[len(copies)])
                copies.append(copy)
    return copies


def fetches(own_ref, refs, target, sems, cols=None):
    if cols is not None:
        axes = len(refs[0].shape) - 1
        refs = [ref.at[(slice(None),) * axes + (cols,)] for ref in refs]
        target = target.at[:, cols]
    if len(refs) == 2:
        return place_blocks(own_ref, refs, target, sems)
    return [pltpu.make_async_copy(refs[0], target, sems.at[0])]


def launch(copies):
    for copy in copies:
        copy.start()


def finish(copies):
    for copy in copies:
        copy.wait()


def hand_out(held, outs, sems):
    sources = [held] if len(outs) == 1 else [held.at[0], held.at[1]]
    copies = [
        pltpu.make_async_copy(source, out, sems.at[i])
        for i, (source, out) in enumerate(zip(sources, outs))
    ]
    launch(copies)
    finish(copies)


def outs_of(shape, split):
    if split:
        return [jax.ShapeDtypeStruct(shape[1:], BF16)] * 2
    return [jax.ShapeDtypeStruct(shape, BF16)]


def copies_of(parts):
    count = 1
    for size in parts[0].shape[:-2]:
        count *= size
    return max(1, count * len(parts))


def project_kernel(chunk, parts, own_ref, hidden_ref, gain_ref, *refs):
    sources, (normed_out, out_ref, whole_out, normed_ref, whole_ref, sems, out_sems) = (
        refs[:parts],
        refs[parts:],
    )
    copies = fetches(own_ref, sources, whole_ref, sems)
    launch(copies)
    count = hidden_ref.shape[0]
    for row in range(0, count, chunk):
        at = slice(row, row + chunk)
        normed_ref[at, :] = (norm_parts(hidden_ref[at, :])[0] * gain_ref[...]).astype(BF16)
    finish(copies)
    copies = [
        pltpu.make_async_copy(normed_ref, normed_out, out_sems.at[0]),
        pltpu.make_async_copy(whole_ref, whole_out, out_sems.at[1]),
    ]
    launch(copies)
    for row in range(0, count, chunk):
        at = slice(row, row + chunk)
        out_ref[at, :] = nn(normed_ref[at, :], whole_ref[...]).astype(BF16)
    finish(copies)


def project(own, hidden, gain, parts, cols):
    count, width = hidden.shape
    in_hbm = pl.BlockSpec(memory_space=pltpu.HBM)
    return pl.pallas_call(
        functools.partial(project_kernel, min(512, count), len(parts)),
        in_specs=[pl.BlockSpec(memory_space=pltpu.SMEM)]
        + [IN_VMEM] * 2
        + [pl.BlockSpec(memory_space=pl.ANY)] * len(parts),
        out_specs=[in_hbm, IN_VMEM, in_hbm],
        scratch_shapes=[
            pltpu.VMEM((count, width), BF16),
            pltpu.VMEM((width, cols), BF16),
            pltpu.SemaphoreType.DMA((copies_of(parts),)),
            pltpu.SemaphoreType.DMA((2,)),
        ],
        out_shape=[
            pltpu.HBM((count, width), BF16),
            jax.ShapeDtypeStruct((count, cols), BF16),
            pltpu.HBM((width, cols), BF16),
        ],
        compiler_params=params(10),
        cost_estimate=cost(4 * (2 * count * width * cols), 4 * (8 * 2**20)),
        name="project",
    )(own, hidden, gain, *parts)


def rise_kernel(cfg, own_ref, hidden_ref, att_ref, cot_ref, gain_ref, *refs):
    seq_count, dp_count, split, chunk, up_parts, down_parts = cfg
    up_sources, refs = refs[:up_parts], refs[up_parts:]
    down_sources, refs = refs[:down_parts], refs[down_parts:]
    outs = 2 if split else 1
    out_ref, normed_ref, scale_ref, slope_ref, w_up, w_down, *refs = refs
    grad_outs, refs = refs[:outs], refs[outs:]
    act_ref, cot_t, grad_ref, up_sems, down_sems, out_sems = refs
    count, width = hidden_ref.shape
    raised = act_ref.shape[1]
    up_copies = [
        fetches(own_ref, up_sources, w_up, up_sems.at[i], slice(start, start + 512))
        for i, start in enumerate(range(0, width + raised, 512))
    ]
    down_copies = fetches(own_ref, down_sources, w_down, down_sems)
    for copies in up_copies[:2] + [down_copies] + up_copies[2:]:
        launch(copies)
    cot_t[...] = cot_ref[...].T
    finish(up_copies[0])
    for row in range(0, count, chunk):
        at = slice(row, row + chunk)
        first = hidden_ref[at, :] + nn(att_ref[at, :], w_up[:, :width])
        normed, scale = norm_parts(first)
        normed_ref[at, :] = normed
        scale_ref[at, :] = jnp.broadcast_to(scale, (chunk, scale_ref.shape[1]))
        normed_two = (normed * gain_ref[...]).astype(BF16)
        total = first
        for start in range(0, raised, 512):
            stop = start + 512
            if row == 0:
                finish(up_copies[1 + start // 512])
            v = nn(normed_two, w_up[:, width + start : width + stop])
            square = v * v
            t = jnp.tanh(v * (0.7978845608028654 + 0.035677408136300125 * square))
            half = 0.5 + 0.5 * t
            act = (v * half).astype(BF16)
            slope = half + v * (0.5 - 0.5 * t * t) * (
                0.7978845608028654 + 0.10703222440890037 * square
            )
            act_ref[at, start:stop] = act
            slope_ref[at, start:stop] = slope.astype(BF16)
            if row == 0 and start == 0:
                finish(down_copies)
            total = total + nn(act, w_down[start:stop, :])
        out_ref[at, :] = total.astype(BF16)
    if not split:
        for start in range(0, raised, 512):
            grad_ref[:, start : start + 512] = nn(
                cot_t[...], act_ref[:, start : start + 512]
            ).astype(BF16)
        hand_out(grad_ref, grad_outs, out_sems)
        return
    cols = width // seq_count
    rows = raised // dp_count
    copies = []
    for i in range(dp_count // 2):
        result = nn(cot_t[...], act_ref[:, 2 * i * rows : 2 * (i + 1) * rows]).astype(BF16)
        z = i ^ own_ref[1]
        for s in range(seq_count):
            piece = result[s * cols : (s + 1) * cols, :]
            for core in range(2):
                for part in range(rows // 128):
                    col = core * rows + part * 128
                    grad_ref[core ^ own_ref[2], z, s ^ own_ref[0], part] = piece[:, col : col + 128]
        for core in range(2):
            copy = pltpu.make_async_copy(
                grad_ref.at[core, z], grad_outs[core].at[z], out_sems.at[len(copies)]
            )
            copies.append(copy)
            copy.start()
    finish(copies)


def rise(own, hidden, att, cot, gain, up_parts, down_parts, raised, seq_count, dp_count, split):
    count, width = hidden.shape
    if split:
        parts = raised // dp_count // 128
        grad_shape = (2, dp_count // 2, seq_count, parts, width // seq_count, 128)
    else:
        grad_shape = (width, raised)
    chunk = min(512, count)
    cfg = (seq_count, dp_count, split, chunk, len(up_parts), len(down_parts))
    grads = outs_of(grad_shape, split)
    up_shape, down_shape = (width, width + raised), (raised, width)
    anywhere = pl.BlockSpec(memory_space=pl.ANY)
    return pl.pallas_call(
        functools.partial(rise_kernel, cfg),
        in_specs=[pl.BlockSpec(memory_space=pltpu.SMEM)]
        + [IN_VMEM] * 4
        + [anywhere] * (len(up_parts) + len(down_parts)),
        out_specs=[IN_VMEM] * 6 + [anywhere] * len(grads),
        scratch_shapes=[
            pltpu.VMEM((count, raised), BF16),
            pltpu.VMEM((width, count), BF16),
            pltpu.VMEM(grad_shape, BF16),
            pltpu.SemaphoreType.DMA(((width + raised) // 512, copies_of(up_parts))),
            pltpu.SemaphoreType.DMA((copies_of(down_parts),)),
            pltpu.SemaphoreType.DMA((dp_count,)),
        ],
        out_shape=[
            jax.ShapeDtypeStruct((count, width), BF16),
            jax.ShapeDtypeStruct((count, width), F32),
            jax.ShapeDtypeStruct((count, 128), F32),
            jax.ShapeDtypeStruct((count, raised), BF16),
            jax.ShapeDtypeStruct(up_shape, BF16),
            jax.ShapeDtypeStruct(down_shape, BF16),
        ]
        + grads,
        compiler_params=params(12),
        cost_estimate=cost(7 * 2**30, 24 * 2**20),
        name="rise",
    )(own, hidden, att, cot, gain, *up_parts, *down_parts)


def fall_kernel(
    cfg,
    own_ref,
    cot_ref,
    slope_ref,
    normed_ref,
    scale_ref,
    att_ref,
    den_ref,
    gain_ref,
    w_up,
    w_down,
    first_ref,
    scaled_ref,
    extra_ref,
    gain_sum_ref,
    *refs,
):
    seq_count, dp_count, split, chunk = cfg
    outs = 2 if split else 1
    grad_outs, (raise_ref, normed_t, att_t, branch_ref, grad_ref, out_sems) = (
        refs[:outs],
        refs[outs:],
    )
    count, width = cot_ref.shape
    raised = raise_ref.shape[1]
    gain = gain_ref[...]
    lane = lax.broadcasted_iota(jnp.int32, (128, width), 1)
    spread = lax.broadcasted_iota(jnp.int32, (128, width), 0) == 16 * (lane // 64)
    spread = jnp.where(spread, 1.0, 0.0).astype(BF16)
    row = lax.broadcasted_iota(jnp.int32, (128, 128), 0)
    col = lax.broadcasted_iota(jnp.int32, (128, 128), 1)
    swap = jnp.where((row < 64) != (col < 64), 1.0, 0.0).astype(BF16)
    even = lax.broadcasted_iota(jnp.int32, (1, 128), 1) % 2 == 0
    gain_sum = jnp.zeros((1, width), F32)
    att_t[...] = att_ref[...].T
    for top in range(0, count, chunk):
        at = slice(top, top + chunk)
        cot = cot_ref[at, :]
        normed = normed_ref[at, :]
        normed_t[:, at] = (normed * gain).astype(BF16).T
        back = jnp.zeros((chunk, width), F32)
        for start in range(0, raised, 512):
            stop = start + 512
            grad_raised = (nt(cot, w_down[start:stop, :]) * slope_ref[at, start:stop]).astype(BF16)
            raise_ref[at, start:stop] = grad_raised
            back = back + nt(grad_raised, w_up[:, width + start : width + stop])
        gain_sum = gain_sum + jnp.sum(back * normed, axis=0, keepdims=True)
        grad_first = cot.astype(F32) + norm_back(back * gain, normed, scale_ref[at, :1])
        first_ref[at, :] = grad_first
        branch = grad_first.astype(BF16)
        branch_ref[at, :] = branch
        inverse = 1.0 / den_ref[at, :]
        coarse = inverse.astype(BF16)
        fine = (inverse - coarse.astype(F32)).astype(BF16)
        ratio = nt(branch, w_up[:, :width]) * (nn(coarse, spread) + nn(fine, spread))
        scaled_ref[at, :] = ratio.astype(BF16)
        product = ratio * att_ref[at, :]
        coarse = product.astype(BF16)
        fine = (product - coarse.astype(F32)).astype(BF16)
        for start in range(0, width, 128):
            stop = start + 128
            offset = nn(coarse[:, start:stop], swap) + nn(fine[:, start:stop], swap)
            upper = offset.astype(BF16)
            lower = (offset - upper.astype(F32)).astype(BF16)
            extra_ref[at, start:stop] = jnp.where(even, upper, lower)
    gain_sum_ref[...] = gain_sum
    if not split:
        grad_ref[:, :width] = nn(att_t[...], branch_ref[...]).astype(BF16)
        for start in range(0, raised, 512):
            grad_ref[:, width + start : width + start + 512] = nn(
                normed_t[...], raise_ref[:, start : start + 512]
            ).astype(BF16)
        hand_out(grad_ref, grad_outs, out_sems)
        return
    cols = raised // seq_count
    wide = width // seq_count
    rows = width // dp_count
    copies = []

    def keep(result, s, at):
        for d in range(dp_count):
            grad_ref[(d % 2) ^ own_ref[2], s ^ own_ref[0], (d // 2) ^ own_ref[1], :, at] = result[
                d * rows : (d + 1) * rows, :
            ]

    result = nn(att_t[...], branch_ref[...]).astype(BF16)
    for s in range(seq_count):
        keep(result[:, s * wide : (s + 1) * wide], s, slice(0, wide))
    for s in range(seq_count):
        result = nn(normed_t[...], raise_ref[:, s * cols : (s + 1) * cols]).astype(BF16)
        keep(result, s, slice(wide, wide + cols))
        for core in range(2):
            copy = pltpu.make_async_copy(
                grad_ref.at[core, s ^ own_ref[0]],
                grad_outs[core].at[s ^ own_ref[0]],
                out_sems.at[len(copies)],
            )
            copies.append(copy)
            copy.start()
    finish(copies)


def fall(own, cot, slope, normed, scale, att, den, gain, w_up, w_down, seq_count, dp_count, split):
    count, width = cot.shape
    raised = w_down.shape[0]
    if split:
        grad_shape = (2, seq_count, dp_count // 2, width // dp_count, (width + raised) // seq_count)
    else:
        grad_shape = (width, width + raised)
    grads = outs_of(grad_shape, split)
    cfg = (seq_count, dp_count, split, min(512, count))

    def sds(dtype):
        return jax.ShapeDtypeStruct((count, width), dtype)

    return pl.pallas_call(
        functools.partial(fall_kernel, cfg),
        in_specs=[pl.BlockSpec(memory_space=pltpu.SMEM)] + [IN_VMEM] * 9,
        out_specs=[IN_VMEM] * 4 + [pl.BlockSpec(memory_space=pl.ANY)] * len(grads),
        scratch_shapes=[
            pltpu.VMEM((count, raised), BF16),
            pltpu.VMEM((width, count), BF16),
            pltpu.VMEM((width, count), BF16),
            pltpu.VMEM((count, width), BF16),
            pltpu.VMEM(grad_shape, BF16),
            pltpu.SemaphoreType.DMA((2 * seq_count,)),
        ],
        out_shape=[
            sds(F32),
            sds(BF16),
            sds(BF16),
            jax.ShapeDtypeStruct((1, width), F32),
        ]
        + grads,
        compiler_params=params(14),
        cost_estimate=cost(4 * (8 * 2**30), 4 * (24 * 2**20)),
        name="fall",
    )(own, cot, slope, normed, scale, att, den, gain, w_up, w_down)


def last_kernel(chunk, hidden_ref, first_ref, gain_ref, mask_ref, w_ref, *refs):
    *grads, out_ref, sums_ref = refs
    masked = gain_sum = 0.0
    for top in range(0, hidden_ref.shape[0], chunk):
        at = slice(top, top + chunk)
        back = 0.0
        start = 0
        for ref in grads:
            stop = start + ref.shape[1]
            back = back + nt(ref[at, :], w_ref[:, start:stop])
            start = stop
        normed, scale = norm_parts(hidden_ref[at, :])
        grad = first_ref[at, :] + norm_back(back * gain_ref[...], normed, scale)
        coarse = grad.astype(BF16)
        out_ref[at, :] = coarse
        fine = (grad - coarse.astype(F32)).astype(BF16)
        mask = mask_ref[:, at]
        masked = masked + nn(mask, coarse) + nn(mask, fine)
        gain_sum = gain_sum + jnp.sum(back * normed, axis=0, keepdims=True)
    sums_ref[...] = masked
    sums_ref[1:2, :] = gain_sum


def last(hidden, grad_first, gain, mask, w_qkv, grads):
    count, width = hidden.shape
    return pl.pallas_call(
        functools.partial(last_kernel, min(512, count)),
        in_specs=[IN_VMEM] * (5 + len(grads)),
        out_specs=[IN_VMEM] * 2,
        out_shape=[
            jax.ShapeDtypeStruct((count, width), BF16),
            jax.ShapeDtypeStruct((8, width), F32),
        ],
        compiler_params=params(8),
        cost_estimate=cost(8 * (6 * count * width * width), 8 * (12 * 2**20)),
        name="last",
    )(hidden, grad_first, gain, mask, w_qkv, *grads)


def swap_along(value, axis, mask):
    count = lax.axis_size(axis)
    return lax.ppermute(value, axis, [(i, i ^ mask) for i in range(count)])


def add_up(values):
    total = values[0].astype(F32)
    for value in values[1:]:
        total = total + value.astype(F32)
    return total


def together(*values):
    return lax.optimization_barrier(values)


def from_plane(values):
    return [values[0]] + [swap_along(values[j], "seq", j) for j in range(1, len(values))]


def from_line(values):
    return [values[0]] + [swap_along(values[j], "dp", 2 * j) for j in range(1, len(values))]


def other_core(value):
    return swap_along(value, "dp", 1)


def add_split(left, right):
    return [add_up((left[j], right[j])).astype(BF16) for j in range(left.shape[0])]


def both_cores(value):
    return [value, other_core(value)]


def split_first(value):
    return [value[j] for j in range(value.shape[0])]


def halve_line(value):
    half = value.shape[0] // 2
    while half:
        came = swap_along(value[half:], "dp", 2 * half)
        value = add_up((value[:half], came))
        half //= 2
        if half:
            value = value.astype(BF16)
    return value[0]


def gather_line(value):
    return jnp.stack(from_line([value] * (lax.axis_size("dp") // 2)))


def gather_plane(value):
    return jnp.stack(from_plane([value] * lax.axis_size("seq")))


def own_columns(weight):
    cols = weight.shape[1] // lax.axis_size("seq")
    return lax.dynamic_slice_in_dim(weight, lax.axis_index("seq") * cols, cols, 1)


def pieces_of(whole, own, seq_count, dp_count, flipped):
    row_blocks, col_blocks = (seq_count, dp_count) if flipped else (dp_count, seq_count)
    rows, cols = whole.shape[0] // row_blocks, whole.shape[1] // col_blocks
    whole = whole.reshape(row_blocks, rows, col_blocks, cols)
    whole = jnp.transpose(whole, (0, 2, 1, 3) if flipped else (2, 0, 1, 3))
    whole = whole.reshape(seq_count, dp_count // 2, 2, rows, cols)
    whole = jnp.take(whole, jnp.arange(seq_count) ^ own[0], axis=0)
    whole = jnp.take(whole, jnp.arange(dp_count // 2) ^ own[1], axis=1)
    whole = jnp.take(whole, jnp.arange(2) ^ own[2], axis=2)
    return jnp.transpose(whole, (2, 0, 1, 3, 4))


def per_device(
    inputs,
    cotangent,
    timestep,
    unmask_order,
    mask_embed,
    ln1_gain,
    weight_qkv,
    weight_out,
    ln2_gain,
    weight_up,
    weight_down,
):
    rows, segment, width = inputs.shape
    raised = weight_up.shape[1]
    seq_count, dp_count = lax.axis_size("seq"), lax.axis_size("dp")
    outer = seq_count // rows
    split = outer == 1 and (seq_count, dp_count) == (4, 8)
    place = lax.axis_index("seq")
    dp_place = lax.axis_index("dp")
    row = place % rows
    own = jnp.stack([place, dp_place // 2, dp_place % 2]).astype(jnp.int32)

    def by_partner(value):
        return [lax.dynamic_index_in_dim(value, row ^ j, 0, keepdims=False) for j in range(rows)]

    def to_rows(value):
        return jnp.concatenate(from_plane(by_partner(value)))

    def to_partners(value):
        return from_plane([value[j * segment : (j + 1) * segment] for j in range(rows)])

    def by_row(parts):
        out = jnp.zeros((rows,) + parts[0].shape, parts[0].dtype)
        for j in (0, 3, 2, 1) if rows == 4 else range(rows):
            out = lax.dynamic_update_index_in_dim(out, parts[j], row ^ j, 0)
        return out

    masked = (unmask_order <= timestep[:, None]).astype(BF16)
    masked = jnp.pad(masked[:, None, :], ((0, 0), (0, 15), (0, width - segment)))
    came = by_partner(jnp.concatenate((inputs, masked), axis=1))
    up_and_out = jnp.concatenate((weight_out, weight_up), axis=1)
    if split:
        down_rows = weight_down.shape[0] // seq_count
        own_down = lax.dynamic_slice_in_dim(weight_down, place * down_rows, down_rows, 0)
        line = gather_line(jnp.concatenate((own_columns(weight_qkv), own_down), axis=1))
        came = from_plane(came)
        line, up_and_out = together(line, up_and_out)
        line_up = jnp.stack((up_and_out, swap_along(up_and_out, "dp", 4)))
        line_up = [line_up, swap_along(line_up, "dp", 2)]
        plane_qkv = gather_plane(line[..., :-width])
        line_down = line[..., -width:].reshape(-1, width)
        cot = cotangent
        parts_qkv = both_cores(plane_qkv)
        cot = from_plane([jnp.concatenate((part, line_down)) for part in by_partner(cot)])
    else:
        came, cot = from_plane(came), from_plane(by_partner(cotangent))
        parts_qkv, parts_up, parts_down = (
            [lax.all_gather(weight, "dp", axis=0, tiled=True)]
            for weight in (weight_qkv, up_and_out, weight_down)
        )

    block = jnp.concatenate([part[:segment] for part in came]).astype(F32)
    mask_row = jnp.concatenate([part[segment, :segment] for part in came])
    hidden = block + mask_row.astype(F32)[:, None] * mask_embed
    normed_one, projected, whole_qkv = project(
        own, hidden, ln1_gain[None, :], parts_qkv, 3 * width
    )
    if outer > 1:
        groups = [[j * rows + i for j in range(outer)] for i in range(rows)]
        far = lax.all_gather(
            projected[:, width:], "seq", axis=0, tiled=True, axis_index_groups=groups
        )
        attended, denominators = attend(projected, far, 0)
    else:
        attended, denominators = attend_row(projected)
    if split:
        line_up, attended = together(line_up, attended)
        parts_up = both_cores(jnp.stack(line_up, axis=1).reshape((-1,) + up_and_out.shape))
        cot, parts_up[0] = together(cot, parts_up[0])
        plane_down = jnp.stack([part[segment:] for part in cot])
        plane_down = plane_down.reshape(seq_count, dp_count // 2, -1, width)
        parts_down = both_cores(plane_down)
    cot = jnp.concatenate([part[:segment] for part in cot])
    outputs, normed, scale, slope, whole_up, whole_down, *grad_down = rise(
        own,
        hidden,
        attended,
        cot,
        ln2_gain[None, :],
        parts_up,
        parts_down,
        raised,
        seq_count,
        dp_count,
        split,
    )
    result = to_partners(outputs)
    grad_first, scaled, extra, sum_gain_two, *grad_up = fall(
        own,
        cot,
        slope,
        normed,
        scale,
        attended,
        denominators,
        ln2_gain[None, :],
        whole_up,
        whole_down,
        seq_count,
        dp_count,
        split,
    )
    mask_rows = jnp.broadcast_to(mask_row[None, :], (8, mask_row.shape[0]))
    if split:
        grad_down[1] = other_core(grad_down[1])
        grad_down, scaled, grad_up, result = together(grad_down, scaled, grad_up, result)
        line_down = from_line(add_split(*grad_down))
        grad_up[1] = other_core(grad_up[1])
        half = attend_back_half(projected, scaled, extra)
        grad_up, half, line_down[1] = together(grad_up, half, line_down[1])
        plane_up = from_plane(add_split(*grad_up))
        *rest, mine_qkv, other_qkv = attend_back_sum(
            own, projected, scaled, extra, normed_one, half, seq_count, dp_count
        )
        plane_up, line_down, rest, mine_qkv, other_qkv = together(
            plane_up, line_down, rest, mine_qkv, other_qkv
        )
        grads = [part for pair in zip(half, rest) for part in pair]
        both_qkv = (mine_qkv, other_core(other_qkv))
        line_up = add_up(plane_up).astype(BF16)
        z_half = line_up.shape[0] // 2
        line_came = swap_along(line_up[z_half:], "dp", 2 * z_half)
        tall = width // dp_count
        down = add_up(line_down).astype(BF16).reshape(seq_count, -1, tall, 128)
        both_qkv, mask_rows = together(both_qkv, mask_rows)
        mine_qkv = [part.reshape(-1, tall, 128) for part in add_split(*both_qkv)]
        plane_last = from_plane([jnp.concatenate((mine_qkv[j], down[j])) for j in range(seq_count)])
    else:
        dq, dk, dv = attend_back(projected, far, scaled, extra)
        both = jnp.concatenate((dk, dv), axis=1)
        both = lax.psum_scatter(
            both, "seq", scatter_dimension=0, tiled=True, axis_index_groups=groups
        )
        grads = [dq, both]
        grad_qkv = lax.dot_general(
            normed_one,
            jnp.concatenate(grads, axis=1),
            (((0,), (0,)), ((), ())),
            preferred_element_type=F32,
        ).astype(BF16)
        cut = functools.partial(pieces_of, own=own, seq_count=seq_count, dp_count=dp_count)
        (grad_up,), (grad_down,) = grad_up, grad_down
        grad_out, grad_up = (
            cut(part, flipped=False) for part in (grad_up[:, :width], grad_up[:, width:])
        )
        grad_up = jnp.concatenate((grad_out, grad_up), axis=-1)
        grad_qkv = cut(grad_qkv, flipped=False)
        grad_down = cut(grad_down, flipped=True)
        sums = []
        for pieces in (grad_qkv, grad_up, grad_down):
            mine = add_up((pieces[0], other_core(pieces[1]))).astype(BF16)
            plane = add_up(from_plane(split_first(mine))).astype(BF16)
            sums.append(add_up(from_line(split_first(plane))))
        sum_qkv, sum_up, sum_down = sums
        sum_down = sum_down.T
    grad_hidden, sums = last(
        hidden, grad_first, ln1_gain[None, :], mask_rows, whole_qkv, grads
    )
    vectors = jnp.concatenate((sums[0:2], sum_gain_two, jnp.zeros((5, width), F32)), axis=0)
    vectors = vectors + other_core(vectors)
    bit = 2
    while bit < dp_count:
        vectors = vectors + swap_along(vectors, "dp", bit)
        bit *= 2
    if split:
        grad_hidden, vectors, line_came, plane_last = together(
            grad_hidden, vectors, line_came, plane_last
        )
        sum_up = add_up((line_up[:z_half], line_came)).astype(BF16)
        kinds = mine_qkv[0].shape[0]
        sum_qkv = add_up([part[:kinds] for part in plane_last]).astype(BF16)
        sum_qkv = sum_qkv.reshape((dp_count // 2, -1) + sum_qkv.shape[1:])
        line_came = swap_along(sum_qkv[z_half:], "dp", 2 * z_half)
        line_came, plane_last, sum_up = together(line_came, plane_last, sum_up)
        sum_qkv = halve_line(add_up((sum_qkv[:z_half], line_came)).astype(BF16))
        sum_up = halve_line(sum_up)
        sum_down = add_up([part[kinds:] for part in plane_last])
        sum_down = sum_down.reshape(-1, width // seq_count, 128)
        sum_down = jnp.transpose(sum_down, (0, 2, 1)).reshape(-1, width // seq_count)
        sum_qkv = jnp.transpose(sum_qkv, (1, 0, 2)).reshape(tall, -1)
    grad_inputs = [grad_hidden[j * segment : (j + 1) * segment] for j in range(rows)]
    if split:
        coarse = vectors.astype(BF16)
        terms = jnp.concatenate((coarse, (vectors - coarse.astype(F32)).astype(BF16)))
        grad_inputs = [jnp.concatenate((part, terms)) for part in grad_inputs]
    grad_inputs = from_plane(grad_inputs)
    if split:
        vectors = add_up([part[segment:] for part in grad_inputs])
        vectors = vectors[:8] + vectors[8:]
        grad_inputs = [part[:segment] for part in grad_inputs]
    else:
        vectors = add_up(from_plane([vectors] * seq_count))
    block_width = width // dp_count
    vectors = lax.dynamic_slice_in_dim(vectors, dp_place * block_width, block_width, 1)
    out_cols = width // seq_count
    return (
        by_row(result),
        by_row(grad_inputs),
        vectors[0],
        vectors[1],
        sum_qkv,
        sum_up[:, :out_cols],
        vectors[2],
        sum_up[:, out_cols:],
        sum_down,
    )


def solution(mesh):
    in_specs = (
        P("dp", "seq", None),
        P("dp", "seq", None),
        P("dp"),
        P("dp", "seq"),
        P(),
        P(),
        P("dp", None),
        P("dp", None),
        P(),
        P("dp", None),
        P("dp", None),
    )
    out_specs = (
        P("dp", "seq", None),
        P("dp", "seq", None),
        P("dp"),
        P("dp"),
        P("dp", "seq"),
        P("dp", "seq"),
        P("dp"),
        P("dp", "seq"),
        P("dp", "seq"),
    )
    return jax.shard_map(
        per_device, mesh=mesh, in_specs=in_specs, out_specs=out_specs, check_vma=False
    )
```

```python
import functools

import jax
import jax.numpy as jnp
from jax import lax
from jax.experimental import pallas as pl
from jax.experimental.pallas import tpu as pltpu
from jax.sharding import PartitionSpec as P

EPSILON = 1e-05
HEADS = 8
F32 = jnp.float32
BF16 = jnp.bfloat16
IN_VMEM = pl.BlockSpec(memory_space=pltpu.VMEM)


def nn(left, right):
    return jnp.dot(left, right, preferred_element_type=F32)


def nt(left, right):
    return lax.dot_general(left, right, (((1,), (1,)), ((), ())), preferred_element_type=F32)


def params(vmem):
    return pltpu.CompilerParams(vmem_limit_bytes=vmem * 2**20)


def cost(flops, bytes_accessed):
    return pl.CostEstimate(
        flops=int(flops), bytes_accessed=int(bytes_accessed), transcendentals=0
    )


def attend_kernel(chunk, q_ref, k_ref, v_ref, out_ref, den_ref):
    count = q_ref.shape[0]
    pair = pl.program_id(0)
    lane = lax.broadcasted_iota(jnp.int32, (1, 128), 1)
    low = lane < 64
    keys = k_ref[...]
    values = v_ref[...]
    one = jnp.ones_like(values)
    values_low = jnp.where(low, values, one)
    values_high = jnp.where(low, one, values)
    for start in range(0, count, chunk):
        at = slice(start, start + chunk)
        q = q_ref[at, :] * jnp.asarray(0.125, BF16)
        zero = jnp.zeros_like(q)
        left = nn(jnp.exp(nt(jnp.where(low, q, zero), keys)).astype(BF16), values_low)
        right = nn(jnp.exp(nt(jnp.where(low, zero, q), keys)).astype(BF16), values_high)
        swapped = jnp.where(low, right, left)
        den = pltpu.roll(swapped, 64, 1)
        out_ref[at, :] = (jnp.where(low, left, right) / den).astype(BF16)
        first = lane // 16 == 2 * pair
        second = lane // 16 == 2 * pair + 1
        mine = jnp.where(
            first, jnp.where(low, den, swapped), jnp.where(low, swapped, den)
        )
        den_ref[at, :] = jnp.where(first | second, mine, den_ref[at, :])


def attend(q_source, kv_source, kv_shift):
    count, span = q_source.shape[0], kv_source.shape[0]
    chunk = min(256, count)
    return pl.pallas_call(
        functools.partial(attend_kernel, chunk),
        grid=(4,),
        in_specs=[
            pl.BlockSpec((count, 128), lambda p: (0, p)),
            pl.BlockSpec((span, 128), lambda p: (0, kv_shift + p)),
            pl.BlockSpec((span, 128), lambda p: (0, kv_shift + 4 + p)),
        ],
        out_specs=[
            pl.BlockSpec((count, 128), lambda p: (0, p)),
            pl.BlockSpec((count, 128), lambda p: (0, 0)),
        ],
        out_shape=[
            jax.ShapeDtypeStruct((count, 512), BF16),
            jax.ShapeDtypeStruct((count, 128), F32),
        ],
        compiler_params=params(12),
        cost_estimate=cost(16 * count * span * 1024, 5 * 2**20),
        name="attend",
    )(q_source, kv_source, kv_source)


def attend_row_kernel(chunk, own_ref, out_ref, den_ref):
    count, width = out_ref.shape
    lane = lax.broadcasted_iota(jnp.int32, (1, 128), 1)
    low = lane < 64
    for start in range(0, count, chunk):
        at = slice(start, start + chunk)
        sums = jnp.zeros((chunk, 128), F32)
        for pair in range(width // 128):
            col = pair * 128
            keys = own_ref[:, width + col : width + col + 128]
            values = own_ref[:, 2 * width + col : 2 * width + col + 128]
            one = jnp.ones_like(values)
            q = own_ref[at, col : col + 128] * jnp.asarray(0.125, BF16)
            zero = jnp.zeros_like(q)
            left = nn(
                jnp.exp(nt(jnp.where(low, q, zero), keys)).astype(BF16),
                jnp.where(low, values, one),
            )
            right = nn(
                jnp.exp(nt(jnp.where(low, zero, q), keys)).astype(BF16),
                jnp.where(low, one, values),
            )
            swapped = jnp.where(low, right, left)
            den = pltpu.roll(swapped, 64, 1)
            out_ref[at, col : col + 128] = (jnp.where(low, left, right) / den).astype(BF16)
            first, second = lane // 16 == 2 * pair, lane // 16 == 2 * pair + 1
            sums = jnp.where(first, jnp.where(low, den, swapped), sums)
            sums = jnp.where(second, jnp.where(low, swapped, den), sums)
        den_ref[at, :] = sums


def attend_row(projected):
    count, width = projected.shape[0], projected.shape[1] // 3
    return pl.pallas_call(
        functools.partial(attend_row_kernel, min(256, count)),
        in_specs=[IN_VMEM],
        out_specs=[IN_VMEM] * 2,
        out_shape=[
            jax.ShapeDtypeStruct((count, width), BF16),
            jax.ShapeDtypeStruct((count, 128), F32),
        ],
        compiler_params=params(8),
        cost_estimate=cost(16 * count * count * 1024, 5 * 2**20),
        name="attend_row",
    )(projected)


def head_pair_back(chunk, q_ref, k_ref, v_ref, s_ref, x_ref, dk_ref, dv_ref):
    count, span = q_ref.shape[0], k_ref.shape[0]
    lane = lax.broadcasted_iota(jnp.int32, (1, 128), 1)
    low = lane < 64
    q = q_ref[...] * jnp.asarray(0.125, BF16)
    scaled = s_ref[...]
    extra = x_ref[...]
    zero = jnp.zeros_like(q)
    q_own = (jnp.where(low, q, zero), jnp.where(low, zero, q))
    s_own = (jnp.where(low, scaled, zero), jnp.where(low, zero, scaled))
    s_with = (jnp.where(low, scaled, extra), jnp.where(low, extra, scaled))
    minus = (
        jnp.where((lane == 64) | (lane == 65), -1.0, 0.0).astype(BF16),
        jnp.where((lane == 0) | (lane == 1), -1.0, 0.0).astype(BF16),
    )
    total = jnp.zeros((128, count), F32)
    for start in range(0, span, chunk):
        keys = k_ref[start : start + chunk, :]
        values = v_ref[start : start + chunk, :]
        none = jnp.zeros_like(keys)
        k_own = (jnp.where(low, keys, none), jnp.where(low, none, keys))
        v_with = (jnp.where(low, values, minus[0]), jnp.where(low, minus[1], values))
        dk = dv = 0.0
        for head in range(2):
            weights = jnp.exp(nt(keys, q_own[head]))
            slopes = (weights * nt(v_with[head], s_with[head])).astype(BF16)
            dv = dv + nn(weights.astype(BF16), s_own[head])
            dk = dk + nn(slopes, q_own[head])
            total = total + nn(k_own[head].T, slopes)
        dk_ref[start : start + chunk, :] = dk.astype(BF16)
        dv_ref[start : start + chunk, :] = dv.astype(BF16)
    return (total.T * 0.125).astype(BF16)


def attend_back_kernel(chunk, q_ref, k_ref, v_ref, s_ref, x_ref, dq_ref, dk_ref, dv_ref):
    dq_ref[...] = head_pair_back(chunk, q_ref, k_ref, v_ref, s_ref, x_ref, dk_ref, dv_ref)


def pair_views(col, width, proj_ref, s_ref, x_ref):
    at = [slice(shift + col, shift + col + 128) for shift in (0, width, 2 * width)]
    return [proj_ref.at[:, cols] for cols in at] + [s_ref.at[:, at[0]], x_ref.at[:, at[0]]]


def attend_back_half_kernel(chunk, proj_ref, s_ref, x_ref, dq_ref, dk_ref, dv_ref):
    width = s_ref.shape[1]
    for pair in range(2):
        col = pair * 128
        at = slice(col, col + 128)
        dq_ref[:, at] = head_pair_back(
            chunk,
            *pair_views(col, width, proj_ref, s_ref, x_ref),
            dk_ref.at[:, at],
            dv_ref.at[:, at],
        )


def attend_back_half(projected, scaled, extra):
    count, width = scaled.shape
    return pl.pallas_call(
        functools.partial(attend_back_half_kernel, min(512, count)),
        in_specs=[IN_VMEM] * 3,
        out_specs=[IN_VMEM] * 3,
        out_shape=[jax.ShapeDtypeStruct((count, width // 2), BF16)] * 3,
        compiler_params=params(9),
        cost_estimate=cost(16 * count * count * 1024, 6 * 2**20),
        name="attend_back_half",
    )(projected, scaled, extra)


def attend_back_sum_kernel(
    chunk,
    dp_count,
    own_ref,
    proj_ref,
    s_ref,
    x_ref,
    normed_ref,
    dq_first,
    dk_first,
    dv_first,
    dq_ref,
    dk_ref,
    dv_ref,
    mine_out,
    other_out,
    normed_t,
    joined,
    grad_ref,
    sems,
):
    width = s_ref.shape[1]
    normed_t[...] = normed_ref[...].T

    def weight_part(pairs, refs):
        for kind, ref in enumerate(refs):
            joined[:, kind * 256 : (kind + 1) * 256] = ref[...]
        result = nn(normed_t[...], joined[...]).astype(BF16)
        rows = result.shape[0] // dp_count
        per = grad_ref.shape[3]
        for kind in range(3):
            for i, pair in enumerate(pairs):
                block = pair + 4 * kind
                col, part = (block // per) ^ own_ref[0], block % per
                at = slice(kind * 256 + i * 128, kind * 256 + (i + 1) * 128)
                for d in range(dp_count):
                    grad_ref[(d % 2) ^ own_ref[2], col, (d // 2) ^ own_ref[1], part] = result[
                        d * rows : (d + 1) * rows, at
                    ]

    weight_part((0, 1), (dq_first, dk_first, dv_first))
    for pair in range(2, 4):
        at = slice((pair - 2) * 128, (pair - 1) * 128)
        dq_ref[:, at] = head_pair_back(
            chunk,
            *pair_views(pair * 128, width, proj_ref, s_ref, x_ref),
            dk_ref.at[:, at],
            dv_ref.at[:, at],
        )
    weight_part((2, 3), (dq_ref, dk_ref, dv_ref))
    hand_out(grad_ref, (mine_out, other_out), sems)


def attend_back_sum(own, projected, scaled, extra, normed, first_half, seq_count, dp_count):
    count, width = scaled.shape
    pieces = (2, seq_count, dp_count // 2, 12 // seq_count, width // dp_count, 128)
    return pl.pallas_call(
        functools.partial(attend_back_sum_kernel, min(512, count), dp_count),
        in_specs=[pl.BlockSpec(memory_space=pltpu.SMEM)] + [IN_VMEM] * 7,
        out_specs=[IN_VMEM] * 3 + [pl.BlockSpec(memory_space=pl.ANY)] * 2,
        scratch_shapes=[
            pltpu.VMEM((width, count), BF16),
            pltpu.VMEM((count, 768), BF16),
            pltpu.VMEM(pieces, BF16),
            pltpu.SemaphoreType.DMA((2,)),
        ],
        out_shape=[jax.ShapeDtypeStruct((count, width // 2), BF16)] * 3 + outs_of(pieces, True),
        compiler_params=params(13),
        cost_estimate=cost(20 * count * count * 1024, 10 * 2**20),
        name="attend_back_sum",
    )(own, projected, scaled, extra, normed, *first_half)


def attend_back(q_source, kv_source, scaled, extra):
    count, span = q_source.shape[0], kv_source.shape[0]
    chunk = min(512, span)
    own = pl.BlockSpec((count, 128), lambda p: (0, p))
    far = pl.BlockSpec((span, 128), lambda p: (0, p))
    return pl.pallas_call(
        functools.partial(attend_back_kernel, chunk),
        grid=(4,),
        in_specs=[
            own,
            pl.BlockSpec((span, 128), lambda p: (0, p)),
            pl.BlockSpec((span, 128), lambda p: (0, 4 + p)),
            own,
            own,
        ],
        out_specs=[own, far, far],
        out_shape=[
            jax.ShapeDtypeStruct((count, 512), BF16),
            jax.ShapeDtypeStruct((span, 512), BF16),
            jax.ShapeDtypeStruct((span, 512), BF16),
        ],
        compiler_params=params(40),
        cost_estimate=cost(32 * count * span * 1024, 8 * 2**20),
        name="attend_back",
    )(q_source, kv_source, kv_source, scaled, extra)


def norm_parts(tensor):
    center = tensor - jnp.mean(tensor, axis=-1, keepdims=True)
    scale = lax.rsqrt(jnp.mean(center * center, axis=-1, keepdims=True) + EPSILON)
    return center * scale, scale


def norm_back(q, normed, scale):
    return scale * (
        q - jnp.mean(q, axis=-1, keepdims=True) - normed * jnp.mean(q * normed, axis=-1, keepdims=True)
    )


def place_blocks(own_ref, sources, target, sems):
    copies = []
    for core in range(2):
        source = sources[core]
        by_seq = len(source.shape) == 4
        seq_count = source.shape[0] if by_seq else 1
        z_count, rows, cols = source.shape[-3:]
        by_rows = by_seq and cols == target.shape[1]
        for j in range(seq_count):
            for i in range(z_count):
                block = 2 * (own_ref[1] ^ i) + (own_ref[2] ^ core)
                across = slice(None)
                if by_rows:
                    block = block * seq_count + (own_ref[0] ^ j)
                elif by_seq:
                    across = pl.ds(pl.multiple_of((own_ref[0] ^ j) * cols, cols), cols)
                down = pl.ds(pl.multiple_of(block * rows, rows), rows)
                piece = source.at[j, i] if by_seq else source.at[i]
                copy = pltpu.make_async_copy(piece, target.at[down, across], sems.at[len(copies)])
                copies.append(copy)
    return copies


def fetches(own_ref, refs, target, sems, cols=None):
    if cols is not None:
        axes = len(refs[0].shape) - 1
        refs = [ref.at[(slice(None),) * axes + (cols,)] for ref in refs]
        target = target.at[:, cols]
    if len(refs) == 2:
        return place_blocks(own_ref, refs, target, sems)
    return [pltpu.make_async_copy(refs[0], target, sems.at[0])]


def launch(copies):
    for copy in copies:
        copy.start()


def finish(copies):
    for copy in copies:
        copy.wait()


def hand_out(held, outs, sems):
    sources = [held] if len(outs) == 1 else [held.at[0], held.at[1]]
    copies = [
        pltpu.make_async_copy(source, out, sems.at[i])
        for i, (source, out) in enumerate(zip(sources, outs))
    ]
    launch(copies)
    finish(copies)


def outs_of(shape, split):
    if split:
        return [jax.ShapeDtypeStruct(shape[1:], BF16)] * 2
    return [jax.ShapeDtypeStruct(shape, BF16)]


def copies_of(parts):
    count = 1
    for size in parts[0].shape[:-2]:
        count *= size
    return max(1, count * len(parts))


def project_kernel(chunk, parts, own_ref, hidden_ref, gain_ref, *refs):
    sources, (normed_out, out_ref, whole_out, normed_ref, whole_ref, sems, out_sems) = (
        refs[:parts],
        refs[parts:],
    )
    copies = fetches(own_ref, sources, whole_ref, sems)
    launch(copies)
    count = hidden_ref.shape[0]
    for row in range(0, count, chunk):
        at = slice(row, row + chunk)
        normed_ref[at, :] = (norm_parts(hidden_ref[at, :])[0] * gain_ref[...]).astype(BF16)
    finish(copies)
    copies = [
        pltpu.make_async_copy(normed_ref, normed_out, out_sems.at[0]),
        pltpu.make_async_copy(whole_ref, whole_out, out_sems.at[1]),
    ]
    launch(copies)
    for row in range(0, count, chunk):
        at = slice(row, row + chunk)
        out_ref[at, :] = nn(normed_ref[at, :], whole_ref[...]).astype(BF16)
    finish(copies)


def project(own, hidden, gain, parts, cols):
    count, width = hidden.shape
    in_hbm = pl.BlockSpec(memory_space=pltpu.HBM)
    return pl.pallas_call(
        functools.partial(project_kernel, min(512, count), len(parts)),
        in_specs=[pl.BlockSpec(memory_space=pltpu.SMEM)]
        + [IN_VMEM] * 2
        + [pl.BlockSpec(memory_space=pl.ANY)] * len(parts),
        out_specs=[in_hbm, IN_VMEM, in_hbm],
        scratch_shapes=[
            pltpu.VMEM((count, width), BF16),
            pltpu.VMEM((width, cols), BF16),
            pltpu.SemaphoreType.DMA((copies_of(parts),)),
            pltpu.SemaphoreType.DMA((2,)),
        ],
        out_shape=[
            pltpu.HBM((count, width), BF16),
            jax.ShapeDtypeStruct((count, cols), BF16),
            pltpu.HBM((width, cols), BF16),
        ],
        compiler_params=params(10),
        cost_estimate=cost(4 * (2 * count * width * cols), 4 * (8 * 2**20)),
        name="project",
    )(own, hidden, gain, *parts)


def rise_kernel(cfg, own_ref, hidden_ref, att_ref, cot_ref, gain_ref, *refs):
    seq_count, dp_count, split, chunk, up_parts, down_parts = cfg
    up_sources, refs = refs[:up_parts], refs[up_parts:]
    down_sources, refs = refs[:down_parts], refs[down_parts:]
    outs = 2 if split else 1
    out_ref, normed_ref, scale_ref, slope_ref, w_up, w_down, *refs = refs
    grad_outs, refs = refs[:outs], refs[outs:]
    act_ref, cot_t, grad_ref, up_sems, down_sems, out_sems = refs
    count, width = hidden_ref.shape
    raised = act_ref.shape[1]
    up_copies = [
        fetches(own_ref, up_sources, w_up, up_sems.at[i], slice(start, start + 512))
        for i, start in enumerate(range(0, width + raised, 512))
    ]
    down_copies = fetches(own_ref, down_sources, w_down, down_sems)
    for copies in up_copies[:2] + [down_copies] + up_copies[2:]:
        launch(copies)
    cot_t[...] = cot_ref[...].T
    finish(up_copies[0])
    for row in range(0, count, chunk):
        at = slice(row, row + chunk)
        first = hidden_ref[at, :] + nn(att_ref[at, :], w_up[:, :width])
        normed, scale = norm_parts(first)
        normed_ref[at, :] = normed
        scale_ref[at, :] = jnp.broadcast_to(scale, (chunk, scale_ref.shape[1]))
        normed_two = (normed * gain_ref[...]).astype(BF16)
        total = first
        for start in range(0, raised, 512):
            stop = start + 512
            if row == 0:
                finish(up_copies[1 + start // 512])
            v = nn(normed_two, w_up[:, width + start : width + stop])
            square = v * v
            t = jnp.tanh(v * (0.7978845608028654 + 0.035677408136300125 * square))
            half = 0.5 + 0.5 * t
            act = (v * half).astype(BF16)
            slope = half + v * (0.5 - 0.5 * t * t) * (
                0.7978845608028654 + 0.10703222440890037 * square
            )
            act_ref[at, start:stop] = act
            slope_ref[at, start:stop] = slope.astype(BF16)
            if row == 0 and start == 0:
                finish(down_copies)
            total = total + nn(act, w_down[start:stop, :])
        out_ref[at, :] = total.astype(BF16)
    if not split:
        for start in range(0, raised, 512):
            grad_ref[:, start : start + 512] = nn(
                cot_t[...], act_ref[:, start : start + 512]
            ).astype(BF16)
        hand_out(grad_ref, grad_outs, out_sems)
        return
    cols = width // seq_count
    rows = raised // dp_count
    copies = []
    for i in range(dp_count // 2):
        result = nn(cot_t[...], act_ref[:, 2 * i * rows : 2 * (i + 1) * rows]).astype(BF16)
        z = i ^ own_ref[1]
        for s in range(seq_count):
            piece = result[s * cols : (s + 1) * cols, :]
            for core in range(2):
                for part in range(rows // 128):
                    col = core * rows + part * 128
                    grad_ref[core ^ own_ref[2], z, s ^ own_ref[0], part] = piece[:, col : col + 128]
        for core in range(2):
            copy = pltpu.make_async_copy(
                grad_ref.at[core, z], grad_outs[core].at[z], out_sems.at[len(copies)]
            )
            copies.append(copy)
            copy.start()
    finish(copies)


def rise(own, hidden, att, cot, gain, up_parts, down_parts, raised, seq_count, dp_count, split):
    count, width = hidden.shape
    if split:
        parts = raised // dp_count // 128
        grad_shape = (2, dp_count // 2, seq_count, parts, width // seq_count, 128)
    else:
        grad_shape = (width, raised)
    chunk = min(512, count)
    cfg = (seq_count, dp_count, split, chunk, len(up_parts), len(down_parts))
    grads = outs_of(grad_shape, split)
    up_shape, down_shape = (width, width + raised), (raised, width)
    anywhere = pl.BlockSpec(memory_space=pl.ANY)
    return pl.pallas_call(
        functools.partial(rise_kernel, cfg),
        in_specs=[pl.BlockSpec(memory_space=pltpu.SMEM)]
        + [IN_VMEM] * 4
        + [anywhere] * (len(up_parts) + len(down_parts)),
        out_specs=[IN_VMEM] * 6 + [anywhere] * len(grads),
        scratch_shapes=[
            pltpu.VMEM((count, raised), BF16),
            pltpu.VMEM((width, count), BF16),
            pltpu.VMEM(grad_shape, BF16),
            pltpu.SemaphoreType.DMA(((width + raised) // 512, copies_of(up_parts))),
            pltpu.SemaphoreType.DMA((copies_of(down_parts),)),
            pltpu.SemaphoreType.DMA((dp_count,)),
        ],
        out_shape=[
            jax.ShapeDtypeStruct((count, width), BF16),
            jax.ShapeDtypeStruct((count, width), F32),
            jax.ShapeDtypeStruct((count, 128), F32),
            jax.ShapeDtypeStruct((count, raised), BF16),
            jax.ShapeDtypeStruct(up_shape, BF16),
            jax.ShapeDtypeStruct(down_shape, BF16),
        ]
        + grads,
        compiler_params=params(12),
        cost_estimate=cost(7 * 2**30, 24 * 2**20),
        name="rise",
    )(own, hidden, att, cot, gain, *up_parts, *down_parts)


def fall_kernel(
    cfg,
    own_ref,
    cot_ref,
    slope_ref,
    normed_ref,
    scale_ref,
    att_ref,
    den_ref,
    gain_ref,
    w_up,
    w_down,
    first_ref,
    scaled_ref,
    extra_ref,
    gain_sum_ref,
    *refs,
):
    seq_count, dp_count, split, chunk = cfg
    outs = 2 if split else 1
    grad_outs, (raise_ref, normed_t, att_t, branch_ref, grad_ref, out_sems) = (
        refs[:outs],
        refs[outs:],
    )
    count, width = cot_ref.shape
    raised = raise_ref.shape[1]
    gain = gain_ref[...]
    lane = lax.broadcasted_iota(jnp.int32, (128, width), 1)
    spread = lax.broadcasted_iota(jnp.int32, (128, width), 0) == 16 * (lane // 64)
    spread = jnp.where(spread, 1.0, 0.0).astype(BF16)
    row = lax.broadcasted_iota(jnp.int32, (128, 128), 0)
    col = lax.broadcasted_iota(jnp.int32, (128, 128), 1)
    swap = jnp.where((row < 64) != (col < 64), 1.0, 0.0).astype(BF16)
    even = lax.broadcasted_iota(jnp.int32, (1, 128), 1) % 2 == 0
    gain_sum = jnp.zeros((1, width), F32)
    att_t[...] = att_ref[...].T
    for top in range(0, count, chunk):
        at = slice(top, top + chunk)
        cot = cot_ref[at, :]
        normed = normed_ref[at, :]
        normed_t[:, at] = (normed * gain).astype(BF16).T
        back = jnp.zeros((chunk, width), F32)
        for start in range(0, raised, 512):
            stop = start + 512
            grad_raised = (nt(cot, w_down[start:stop, :]) * slope_ref[at, start:stop]).astype(BF16)
            raise_ref[at, start:stop] = grad_raised
            back = back + nt(grad_raised, w_up[:, width + start : width + stop])
        gain_sum = gain_sum + jnp.sum(back * normed, axis=0, keepdims=True)
        grad_first = cot.astype(F32) + norm_back(back * gain, normed, scale_ref[at, :1])
        first_ref[at, :] = grad_first
        branch = grad_first.astype(BF16)
        branch_ref[at, :] = branch
        inverse = 1.0 / den_ref[at, :]
        coarse = inverse.astype(BF16)
        fine = (inverse - coarse.astype(F32)).astype(BF16)
        ratio = nt(branch, w_up[:, :width]) * (nn(coarse, spread) + nn(fine, spread))
        scaled_ref[at, :] = ratio.astype(BF16)
        product = ratio * att_ref[at, :]
        coarse = product.astype(BF16)
        fine = (product - coarse.astype(F32)).astype(BF16)
        for start in range(0, width, 128):
            stop = start + 128
            offset = nn(coarse[:, start:stop], swap) + nn(fine[:, start:stop], swap)
            upper = offset.astype(BF16)
            lower = (offset - upper.astype(F32)).astype(BF16)
            extra_ref[at, start:stop] = jnp.where(even, upper, lower)
    gain_sum_ref[...] = gain_sum
    if not split:
        grad_ref[:, :width] = nn(att_t[...], branch_ref[...]).astype(BF16)
        for start in range(0, raised, 512):
            grad_ref[:, width + start : width + start + 512] = nn(
                normed_t[...], raise_ref[:, start : start + 512]
            ).astype(BF16)
        hand_out(grad_ref, grad_outs, out_sems)
        return
    cols = raised // seq_count
    wide = width // seq_count
    rows = width // dp_count
    copies = []

    def keep(result, s, at):
        for d in range(dp_count):
            grad_ref[(d % 2) ^ own_ref[2], s ^ own_ref[0], (d // 2) ^ own_ref[1], :, at] = result[
                d * rows : (d + 1) * rows, :
            ]

    result = nn(att_t[...], branch_ref[...]).astype(BF16)
    for s in range(seq_count):
        keep(result[:, s * wide : (s + 1) * wide], s, slice(0, wide))
    for s in range(seq_count):
        result = nn(normed_t[...], raise_ref[:, s * cols : (s + 1) * cols]).astype(BF16)
        keep(result, s, slice(wide, wide + cols))
        for core in range(2):
            copy = pltpu.make_async_copy(
                grad_ref.at[core, s ^ own_ref[0]],
                grad_outs[core].at[s ^ own_ref[0]],
                out_sems.at[len(copies)],
            )
            copies.append(copy)
            copy.start()
    finish(copies)


def fall(own, cot, slope, normed, scale, att, den, gain, w_up, w_down, seq_count, dp_count, split):
    count, width = cot.shape
    raised = w_down.shape[0]
    if split:
        grad_shape = (2, seq_count, dp_count // 2, width // dp_count, (width + raised) // seq_count)
    else:
        grad_shape = (width, width + raised)
    grads = outs_of(grad_shape, split)
    cfg = (seq_count, dp_count, split, min(512, count))

    def sds(dtype):
        return jax.ShapeDtypeStruct((count, width), dtype)

    return pl.pallas_call(
        functools.partial(fall_kernel, cfg),
        in_specs=[pl.BlockSpec(memory_space=pltpu.SMEM)] + [IN_VMEM] * 9,
        out_specs=[IN_VMEM] * 4 + [pl.BlockSpec(memory_space=pl.ANY)] * len(grads),
        scratch_shapes=[
            pltpu.VMEM((count, raised), BF16),
            pltpu.VMEM((width, count), BF16),
            pltpu.VMEM((width, count), BF16),
            pltpu.VMEM((count, width), BF16),
            pltpu.VMEM(grad_shape, BF16),
            pltpu.SemaphoreType.DMA((2 * seq_count,)),
        ],
        out_shape=[
            sds(F32),
            sds(BF16),
            sds(BF16),
            jax.ShapeDtypeStruct((1, width), F32),
        ]
        + grads,
        compiler_params=params(14),
        cost_estimate=cost(4 * (8 * 2**30), 4 * (24 * 2**20)),
        name="fall",
    )(own, cot, slope, normed, scale, att, den, gain, w_up, w_down)


def last_kernel(chunk, hidden_ref, first_ref, gain_ref, mask_ref, w_ref, *refs):
    *grads, out_ref, sums_ref = refs
    masked = gain_sum = 0.0
    for top in range(0, hidden_ref.shape[0], chunk):
        at = slice(top, top + chunk)
        back = 0.0
        start = 0
        for ref in grads:
            stop = start + ref.shape[1]
            back = back + nt(ref[at, :], w_ref[:, start:stop])
            start = stop
        normed, scale = norm_parts(hidden_ref[at, :])
        grad = first_ref[at, :] + norm_back(back * gain_ref[...], normed, scale)
        coarse = grad.astype(BF16)
        out_ref[at, :] = coarse
        fine = (grad - coarse.astype(F32)).astype(BF16)
        mask = mask_ref[:, at]
        masked = masked + nn(mask, coarse) + nn(mask, fine)
        gain_sum = gain_sum + jnp.sum(back * normed, axis=0, keepdims=True)
    sums_ref[...] = masked
    sums_ref[1:2, :] = gain_sum


def last(hidden, grad_first, gain, mask, w_qkv, grads):
    count, width = hidden.shape
    return pl.pallas_call(
        functools.partial(last_kernel, min(512, count)),
        in_specs=[IN_VMEM] * (5 + len(grads)),
        out_specs=[IN_VMEM] * 2,
        out_shape=[
            jax.ShapeDtypeStruct((count, width), BF16),
            jax.ShapeDtypeStruct((8, width), F32),
        ],
        compiler_params=params(8),
        cost_estimate=cost(8 * (6 * count * width * width), 8 * (12 * 2**20)),
        name="last",
    )(hidden, grad_first, gain, mask, w_qkv, *grads)


def swap_along(value, axis, mask):
    count = lax.axis_size(axis)
    return lax.ppermute(value, axis, [(i, i ^ mask) for i in range(count)])


def add_up(values):
    total = values[0].astype(F32)
    for value in values[1:]:
        total = total + value.astype(F32)
    return total


def together(*values):
    return lax.optimization_barrier(values)


def from_plane(values):
    return [values[0]] + [swap_along(values[j], "seq", j) for j in range(1, len(values))]


def from_line(values):
    return [values[0]] + [swap_along(values[j], "dp", 2 * j) for j in range(1, len(values))]


def other_core(value):
    return swap_along(value, "dp", 1)


def add_split(left, right):
    return [add_up((left[j], right[j])).astype(BF16) for j in range(left.shape[0])]


def both_cores(value):
    return [value, other_core(value)]


def split_first(value):
    return [value[j] for j in range(value.shape[0])]


def halve_line(value):
    half = value.shape[0] // 2
    while half:
        came = swap_along(value[half:], "dp", 2 * half)
        value = add_up((value[:half], came))
        half //= 2
        if half:
            value = value.astype(BF16)
    return value[0]


def gather_line(value):
    return jnp.stack(from_line([value] * (lax.axis_size("dp") // 2)))


def gather_plane(value):
    return jnp.stack(from_plane([value] * lax.axis_size("seq")))


def own_columns(weight):
    cols = weight.shape[1] // lax.axis_size("seq")
    return lax.dynamic_slice_in_dim(weight, lax.axis_index("seq") * cols, cols, 1)


def pieces_of(whole, own, seq_count, dp_count, flipped):
    row_blocks, col_blocks = (seq_count, dp_count) if flipped else (dp_count, seq_count)
    rows, cols = whole.shape[0] // row_blocks, whole.shape[1] // col_blocks
    whole = whole.reshape(row_blocks, rows, col_blocks, cols)
    whole = jnp.transpose(whole, (0, 2, 1, 3) if flipped else (2, 0, 1, 3))
    whole = whole.reshape(seq_count, dp_count // 2, 2, rows, cols)
    whole = jnp.take(whole, jnp.arange(seq_count) ^ own[0], axis=0)
    whole = jnp.take(whole, jnp.arange(dp_count // 2) ^ own[1], axis=1)
    whole = jnp.take(whole, jnp.arange(2) ^ own[2], axis=2)
    return jnp.transpose(whole, (2, 0, 1, 3, 4))


def per_device(
    inputs,
    cotangent,
    timestep,
    unmask_order,
    mask_embed,
    ln1_gain,
    weight_qkv,
    weight_out,
    ln2_gain,
    weight_up,
    weight_down,
):
    rows, segment, width = inputs.shape
    raised = weight_up.shape[1]
    seq_count, dp_count = lax.axis_size("seq"), lax.axis_size("dp")
    outer = seq_count // rows
    split = outer == 1 and (seq_count, dp_count) == (4, 8)
    place = lax.axis_index("seq")
    dp_place = lax.axis_index("dp")
    row = place % rows
    own = jnp.stack([place, dp_place // 2, dp_place % 2]).astype(jnp.int32)

    def by_partner(value):
        return [lax.dynamic_index_in_dim(value, row ^ j, 0, keepdims=False) for j in range(rows)]

    def to_rows(value):
        return jnp.concatenate(from_plane(by_partner(value)))

    def to_partners(value):
        return from_plane([value[j * segment : (j + 1) * segment] for j in range(rows)])

    def by_row(parts):
        out = jnp.zeros((rows,) + parts[0].shape, parts[0].dtype)
        for j in (0, 3, 2, 1) if rows == 4 else range(rows):
            out = lax.dynamic_update_index_in_dim(out, parts[j], row ^ j, 0)
        return out

    masked = (unmask_order <= timestep[:, None]).astype(BF16)
    masked = jnp.pad(masked[:, None, :], ((0, 0), (0, 15), (0, width - segment)))
    came = by_partner(jnp.concatenate((inputs, masked), axis=1))
    up_and_out = jnp.concatenate((weight_out, weight_up), axis=1)
    if split:
        down_rows = weight_down.shape[0] // seq_count
        own_down = lax.dynamic_slice_in_dim(weight_down, place * down_rows, down_rows, 0)
        line = gather_line(jnp.concatenate((own_columns(weight_qkv), own_down), axis=1))
        came = from_plane(came)
        line, up_and_out = together(line, up_and_out)
        line_up = jnp.stack((up_and_out, swap_along(up_and_out, "dp", 4)))
        line_up = [line_up, swap_along(line_up, "dp", 2)]
        plane_qkv = gather_plane(line[..., :-width])
        line_down = line[..., -width:].reshape(-1, width)
        cot = cotangent
        parts_qkv = both_cores(plane_qkv)
        cot = from_plane([jnp.concatenate((part, line_down)) for part in by_partner(cot)])
    else:
        came, cot = from_plane(came), from_plane(by_partner(cotangent))
        parts_qkv, parts_up, parts_down = (
            [lax.all_gather(weight, "dp", axis=0, tiled=True)]
            for weight in (weight_qkv, up_and_out, weight_down)
        )

    block = jnp.concatenate([part[:segment] for part in came]).astype(F32)
    mask_row = jnp.concatenate([part[segment, :segment] for part in came])
    hidden = block + mask_row.astype(F32)[:, None] * mask_embed
    normed_one, projected, whole_qkv = project(
        own, hidden, ln1_gain[None, :], parts_qkv, 3 * width
    )
    if outer > 1:
        groups = [[j * rows + i for j in range(outer)] for i in range(rows)]
        far = lax.all_gather(
            projected[:, width:], "seq", axis=0, tiled=True, axis_index_groups=groups
        )
        attended, denominators = attend(projected, far, 0)
    else:
        attended, denominators = attend_row(projected)
    if split:
        line_up, attended = together(line_up, attended)
        parts_up = both_cores(jnp.stack(line_up, axis=1).reshape((-1,) + up_and_out.shape))
        cot, parts_up[0] = together(cot, parts_up[0])
        plane_down = jnp.stack([part[segment:] for part in cot])
        plane_down = plane_down.reshape(seq_count, dp_count // 2, -1, width)
        parts_down = both_cores(plane_down)
    cot = jnp.concatenate([part[:segment] for part in cot])
    outputs, normed, scale, slope, whole_up, whole_down, *grad_down = rise(
        own,
        hidden,
        attended,
        cot,
        ln2_gain[None, :],
        parts_up,
        parts_down,
        raised,
        seq_count,
        dp_count,
        split,
    )
    result = to_partners(outputs)
    grad_first, scaled, extra, sum_gain_two, *grad_up = fall(
        own,
        cot,
        slope,
        normed,
        scale,
        attended,
        denominators,
        ln2_gain[None, :],
        whole_up,
        whole_down,
        seq_count,
        dp_count,
        split,
    )
    mask_rows = jnp.broadcast_to(mask_row[None, :], (8, mask_row.shape[0]))
    if split:
        grad_down[1] = other_core(grad_down[1])
        grad_down, scaled, grad_up, result = together(grad_down, scaled, grad_up, result)
        line_down = from_line(add_split(*grad_down))
        grad_up[1] = other_core(grad_up[1])
        half = attend_back_half(projected, scaled, extra)
        grad_up, half, line_down[1] = together(grad_up, half, line_down[1])
        plane_up = from_plane(add_split(*grad_up))
        *rest, mine_qkv, other_qkv = attend_back_sum(
            own, projected, scaled, extra, normed_one, half, seq_count, dp_count
        )
        plane_up, line_down, rest, mine_qkv, other_qkv = together(
            plane_up, line_down, rest, mine_qkv, other_qkv
        )
        grads = [part for pair in zip(half, rest) for part in pair]
        both_qkv = (mine_qkv, other_core(other_qkv))
        line_up = add_up(plane_up).astype(BF16)
        z_half = line_up.shape[0] // 2
        line_came = swap_along(line_up[z_half:], "dp", 2 * z_half)
        tall = width // dp_count
        down = add_up(line_down).astype(BF16).reshape(seq_count, -1, tall, 128)
        both_qkv, mask_rows = together(both_qkv, mask_rows)
        mine_qkv = [part.reshape(-1, tall, 128) for part in add_split(*both_qkv)]
        plane_last = from_plane([jnp.concatenate((mine_qkv[j], down[j])) for j in range(seq_count)])
    else:
        dq, dk, dv = attend_back(projected, far, scaled, extra)
        both = jnp.concatenate((dk, dv), axis=1)
        both = lax.psum_scatter(
            both, "seq", scatter_dimension=0, tiled=True, axis_index_groups=groups
        )
        grads = [dq, both]
        grad_qkv = lax.dot_general(
            normed_one,
            jnp.concatenate(grads, axis=1),
            (((0,), (0,)), ((), ())),
            preferred_element_type=F32,
        ).astype(BF16)
        cut = functools.partial(pieces_of, own=own, seq_count=seq_count, dp_count=dp_count)
        (grad_up,), (grad_down,) = grad_up, grad_down
        grad_out, grad_up = (
            cut(part, flipped=False) for part in (grad_up[:, :width], grad_up[:, width:])
        )
        grad_up = jnp.concatenate((grad_out, grad_up), axis=-1)
        grad_qkv = cut(grad_qkv, flipped=False)
        grad_down = cut(grad_down, flipped=True)
        sums = []
        for pieces in (grad_qkv, grad_up, grad_down):
            mine = add_up((pieces[0], other_core(pieces[1]))).astype(BF16)
            plane = add_up(from_plane(split_first(mine))).astype(BF16)
            sums.append(add_up(from_line(split_first(plane))))
        sum_qkv, sum_up, sum_down = sums
        sum_down = sum_down.T
    grad_hidden, sums = last(
        hidden, grad_first, ln1_gain[None, :], mask_rows, whole_qkv, grads
    )
    vectors = jnp.concatenate((sums[0:2], sum_gain_two, jnp.zeros((5, width), F32)), axis=0)
    vectors = vectors + other_core(vectors)
    bit = 2
    while bit < dp_count:
        vectors = vectors + swap_along(vectors, "dp", bit)
        bit *= 2
    if split:
        grad_hidden, vectors, line_came, plane_last = together(
            grad_hidden, vectors, line_came, plane_last
        )
        sum_up = add_up((line_up[:z_half], line_came)).astype(BF16)
        kinds = mine_qkv[0].shape[0]
        sum_qkv = add_up([part[:kinds] for part in plane_last]).astype(BF16)
        sum_qkv = sum_qkv.reshape((dp_count // 2, -1) + sum_qkv.shape[1:])
        line_came = swap_along(sum_qkv[z_half:], "dp", 2 * z_half)
        line_came, plane_last, sum_up = together(line_came, plane_last, sum_up)
        sum_qkv = halve_line(add_up((sum_qkv[:z_half], line_came)).astype(BF16))
        sum_up = halve_line(sum_up)
        sum_down = add_up([part[kinds:] for part in plane_last])
        sum_down = sum_down.reshape(-1, width // seq_count, 128)
        sum_down = jnp.transpose(sum_down, (0, 2, 1)).reshape(-1, width // seq_count)
        sum_qkv = jnp.transpose(sum_qkv, (1, 0, 2)).reshape(tall, -1)
    grad_inputs = [grad_hidden[j * segment : (j + 1) * segment] for j in range(rows)]
    if split:
        coarse = vectors.astype(BF16)
        terms = jnp.concatenate((coarse, (vectors - coarse.astype(F32)).astype(BF16)))
        grad_inputs = [jnp.concatenate((part, terms)) for part in grad_inputs]
    grad_inputs = from_plane(grad_inputs)
    if split:
        vectors = add_up([part[segment:] for part in grad_inputs])
        vectors = vectors[:8] + vectors[8:]
        grad_inputs = [part[:segment] for part in grad_inputs]
    else:
        vectors = add_up(from_plane([vectors] * seq_count))
    block_width = width // dp_count
    vectors = lax.dynamic_slice_in_dim(vectors, dp_place * block_width, block_width, 1)
    out_cols = width // seq_count
    return (
        by_row(result),
        by_row(grad_inputs),
        vectors[0],
        vectors[1],
        sum_qkv,
        sum_up[:, :out_cols],
        vectors[2],
        sum_up[:, out_cols:],
        sum_down,
    )


def solution(mesh):
    in_specs = (
        P("dp", "seq", None),
        P("dp", "seq", None),
        P("dp"),
        P("dp", "seq"),
        P(),
        P(),
        P("dp", None),
        P("dp", None),
        P(),
        P("dp", None),
        P("dp", None),
    )
    out_specs = (
        P("dp", "seq", None),
        P("dp", "seq", None),
        P("dp"),
        P("dp"),
        P("dp", "seq"),
        P("dp", "seq"),
        P("dp"),
        P("dp", "seq"),
        P("dp", "seq"),
    )
    return jax.shard_map(
        per_device, mesh=mesh, in_specs=in_specs, out_specs=out_specs, check_vma=False
    )
```

```python
import functools

import jax
import jax.numpy as jnp
from jax import lax
from jax.experimental import pallas as pl
from jax.experimental.pallas import tpu as pltpu
from jax.sharding import PartitionSpec as P

EPSILON = 1e-05
HEADS = 8
F32 = jnp.float32
BF16 = jnp.bfloat16
IN_VMEM = pl.BlockSpec(memory_space=pltpu.VMEM)


def nn(left, right):
    return jnp.dot(left, right, preferred_element_type=F32)


def nt(left, right):
    return lax.dot_general(left, right, (((1,), (1,)), ((), ())), preferred_element_type=F32)


def params(vmem):
    return pltpu.CompilerParams(vmem_limit_bytes=vmem * 2**20)


def cost(flops, bytes_accessed):
    return pl.CostEstimate(
        flops=int(flops), bytes_accessed=int(bytes_accessed), transcendentals=0
    )


def attend_kernel(chunk, q_ref, k_ref, v_ref, out_ref, den_ref):
    count = q_ref.shape[0]
    pair = pl.program_id(0)
    lane = lax.broadcasted_iota(jnp.int32, (1, 128), 1)
    low = lane < 64
    keys = k_ref[...]
    values = v_ref[...]
    one = jnp.ones_like(values)
    values_low = jnp.where(low, values, one)
    values_high = jnp.where(low, one, values)
    for start in range(0, count, chunk):
        at = slice(start, start + chunk)
        q = q_ref[at, :] * jnp.asarray(0.125, BF16)
        zero = jnp.zeros_like(q)
        left = nn(jnp.exp(nt(jnp.where(low, q, zero), keys)).astype(BF16), values_low)
        right = nn(jnp.exp(nt(jnp.where(low, zero, q), keys)).astype(BF16), values_high)
        swapped = jnp.where(low, right, left)
        den = pltpu.roll(swapped, 64, 1)
        out_ref[at, :] = (jnp.where(low, left, right) / den).astype(BF16)
        first = lane // 16 == 2 * pair
        second = lane // 16 == 2 * pair + 1
        mine = jnp.where(
            first, jnp.where(low, den, swapped), jnp.where(low, swapped, den)
        )
        den_ref[at, :] = jnp.where(first | second, mine, den_ref[at, :])


def attend(q_source, kv_source, kv_shift):
    count, span = q_source.shape[0], kv_source.shape[0]
    chunk = min(256, count)
    return pl.pallas_call(
        functools.partial(attend_kernel, chunk),
        grid=(4,),
        in_specs=[
            pl.BlockSpec((count, 128), lambda p: (0, p)),
            pl.BlockSpec((span, 128), lambda p: (0, kv_shift + p)),
            pl.BlockSpec((span, 128), lambda p: (0, kv_shift + 4 + p)),
        ],
        out_specs=[
            pl.BlockSpec((count, 128), lambda p: (0, p)),
            pl.BlockSpec((count, 128), lambda p: (0, 0)),
        ],
        out_shape=[
            jax.ShapeDtypeStruct((count, 512), BF16),
            jax.ShapeDtypeStruct((count, 128), F32),
        ],
        compiler_params=params(12),
        cost_estimate=cost(16 * count * span * 1024, 5 * 2**20),
        name="attend",
    )(q_source, kv_source, kv_source)


def attend_row_kernel(chunk, own_ref, out_ref, den_ref):
    count, width = out_ref.shape
    lane = lax.broadcasted_iota(jnp.int32, (1, 128), 1)
    low = lane < 64
    for start in range(0, count, chunk):
        at = slice(start, start + chunk)
        sums = jnp.zeros((chunk, 128), F32)
        for pair in range(width // 128):
            col = pair * 128
            keys = own_ref[:, width + col : width + col + 128]
            values = own_ref[:, 2 * width + col : 2 * width + col + 128]
            one = jnp.ones_like(values)
            q = own_ref[at, col : col + 128] * jnp.asarray(0.125, BF16)
            zero = jnp.zeros_like(q)
            left = nn(
                jnp.exp(nt(jnp.where(low, q, zero), keys)).astype(BF16),
                jnp.where(low, values, one),
            )
            right = nn(
                jnp.exp(nt(jnp.where(low, zero, q), keys)).astype(BF16),
                jnp.where(low, one, values),
            )
            swapped = jnp.where(low, right, left)
            den = pltpu.roll(swapped, 64, 1)
            out_ref[at, col : col + 128] = (jnp.where(low, left, right) / den).astype(BF16)
            first, second = lane // 16 == 2 * pair, lane // 16 == 2 * pair + 1
            sums = jnp.where(first, jnp.where(low, den, swapped), sums)
            sums = jnp.where(second, jnp.where(low, swapped, den), sums)
        den_ref[at, :] = sums


def attend_row(projected):
    count, width = projected.shape[0], projected.shape[1] // 3
    return pl.pallas_call(
        functools.partial(attend_row_kernel, min(256, count)),
        in_specs=[IN_VMEM],
        out_specs=[IN_VMEM] * 2,
        out_shape=[
            jax.ShapeDtypeStruct((count, width), BF16),
            jax.ShapeDtypeStruct((count, 128), F32),
        ],
        compiler_params=params(8),
        cost_estimate=cost(16 * count * count * 1024, 5 * 2**20),
        name="attend_row",
    )(projected)


def head_pair_back(chunk, q_ref, k_ref, v_ref, s_ref, x_ref, dk_ref, dv_ref):
    count, span = q_ref.shape[0], k_ref.shape[0]
    lane = lax.broadcasted_iota(jnp.int32, (1, 128), 1)
    low = lane < 64
    q = q_ref[...] * jnp.asarray(0.125, BF16)
    scaled = s_ref[...]
    extra = x_ref[...]
    zero = jnp.zeros_like(q)
    q_own = (jnp.where(low, q, zero), jnp.where(low, zero, q))
    s_own = (jnp.where(low, scaled, zero), jnp.where(low, zero, scaled))
    s_with = (jnp.where(low, scaled, extra), jnp.where(low, extra, scaled))
    minus = (
        jnp.where((lane == 64) | (lane == 65), -1.0, 0.0).astype(BF16),
        jnp.where((lane == 0) | (lane == 1), -1.0, 0.0).astype(BF16),
    )
    total = jnp.zeros((128, count), F32)
    for start in range(0, span, chunk):
        keys = k_ref[start : start + chunk, :]
        values = v_ref[start : start + chunk, :]
        none = jnp.zeros_like(keys)
        k_own = (jnp.where(low, keys, none), jnp.where(low, none, keys))
        v_with = (jnp.where(low, values, minus[0]), jnp.where(low, minus[1], values))
        dk = dv = 0.0
        for head in range(2):
            weights = jnp.exp(nt(keys, q_own[head]))
            slopes = (weights * nt(v_with[head], s_with[head])).astype(BF16)
            dv = dv + nn(weights.astype(BF16), s_own[head])
            dk = dk + nn(slopes, q_own[head])
            total = total + nn(k_own[head].T, slopes)
        dk_ref[start : start + chunk, :] = dk.astype(BF16)
        dv_ref[start : start + chunk, :] = dv.astype(BF16)
    return (total.T * 0.125).astype(BF16)


def attend_back_kernel(chunk, q_ref, k_ref, v_ref, s_ref, x_ref, dq_ref, dk_ref, dv_ref):
    dq_ref[...] = head_pair_back(chunk, q_ref, k_ref, v_ref, s_ref, x_ref, dk_ref, dv_ref)


def pair_views(col, width, proj_ref, s_ref, x_ref):
    at = [slice(shift + col, shift + col + 128) for shift in (0, width, 2 * width)]
    return [proj_ref.at[:, cols] for cols in at] + [s_ref.at[:, at[0]], x_ref.at[:, at[0]]]


def attend_back_half_kernel(chunk, proj_ref, s_ref, x_ref, dq_ref, dk_ref, dv_ref):
    width = s_ref.shape[1]
    for pair in range(2):
        col = pair * 128
        at = slice(col, col + 128)
        dq_ref[:, at] = head_pair_back(
            chunk,
            *pair_views(col, width, proj_ref, s_ref, x_ref),
            dk_ref.at[:, at],
            dv_ref.at[:, at],
        )


def attend_back_half(projected, scaled, extra):
    count, width = scaled.shape
    return pl.pallas_call(
        functools.partial(attend_back_half_kernel, min(512, count)),
        in_specs=[IN_VMEM] * 3,
        out_specs=[IN_VMEM] * 3,
        out_shape=[jax.ShapeDtypeStruct((count, width // 2), BF16)] * 3,
        compiler_params=params(9),
        cost_estimate=cost(16 * count * count * 1024, 6 * 2**20),
        name="attend_back_half",
    )(projected, scaled, extra)


def attend_back_sum_kernel(
    chunk,
    dp_count,
    own_ref,
    proj_ref,
    s_ref,
    x_ref,
    normed_ref,
    dq_first,
    dk_first,
    dv_first,
    dq_ref,
    dk_ref,
    dv_ref,
    mine_out,
    other_out,
    normed_t,
    joined,
    grad_ref,
    sems,
):
    width = s_ref.shape[1]
    normed_t[...] = normed_ref[...].T

    def weight_part(pairs, refs):
        for kind, ref in enumerate(refs):
            joined[:, kind * 256 : (kind + 1) * 256] = ref[...]
        result = nn(normed_t[...], joined[...]).astype(BF16)
        rows = result.shape[0] // dp_count
        per = grad_ref.shape[3]
        for kind in range(3):
            for i, pair in enumerate(pairs):
                block = pair + 4 * kind
                col, part = (block // per) ^ own_ref[0], block % per
                at = slice(kind * 256 + i * 128, kind * 256 + (i + 1) * 128)
                for d in range(dp_count):
                    grad_ref[(d % 2) ^ own_ref[2], col, (d // 2) ^ own_ref[1], part] = result[
                        d * rows : (d + 1) * rows, at
                    ]

    weight_part((0, 1), (dq_first, dk_first, dv_first))
    for pair in range(2, 4):
        at = slice((pair - 2) * 128, (pair - 1) * 128)
        dq_ref[:, at] = head_pair_back(
            chunk,
            *pair_views(pair * 128, width, proj_ref, s_ref, x_ref),
            dk_ref.at[:, at],
            dv_ref.at[:, at],
        )
    weight_part((2, 3), (dq_ref, dk_ref, dv_ref))
    hand_out(grad_ref, (mine_out, other_out), sems)


def attend_back_sum(own, projected, scaled, extra, normed, first_half, seq_count, dp_count):
    count, width = scaled.shape
    pieces = (2, seq_count, dp_count // 2, 12 // seq_count, width // dp_count, 128)
    return pl.pallas_call(
        functools.partial(attend_back_sum_kernel, min(512, count), dp_count),
        in_specs=[pl.BlockSpec(memory_space=pltpu.SMEM)] + [IN_VMEM] * 7,
        out_specs=[IN_VMEM] * 3 + [pl.BlockSpec(memory_space=pl.ANY)] * 2,
        scratch_shapes=[
            pltpu.VMEM((width, count), BF16),
            pltpu.VMEM((count, 768), BF16),
            pltpu.VMEM(pieces, BF16),
            pltpu.SemaphoreType.DMA((2,)),
        ],
        out_shape=[jax.ShapeDtypeStruct((count, width // 2), BF16)] * 3 + outs_of(pieces, True),
        compiler_params=params(13),
        cost_estimate=cost(20 * count * count * 1024, 10 * 2**20),
        name="attend_back_sum",
    )(own, projected, scaled, extra, normed, *first_half)


def attend_back(q_source, kv_source, scaled, extra):
    count, span = q_source.shape[0], kv_source.shape[0]
    chunk = min(512, span)
    own = pl.BlockSpec((count, 128), lambda p: (0, p))
    far = pl.BlockSpec((span, 128), lambda p: (0, p))
    return pl.pallas_call(
        functools.partial(attend_back_kernel, chunk),
        grid=(4,),
        in_specs=[
            own,
            pl.BlockSpec((span, 128), lambda p: (0, p)),
            pl.BlockSpec((span, 128), lambda p: (0, 4 + p)),
            own,
            own,
        ],
        out_specs=[own, far, far],
        out_shape=[
            jax.ShapeDtypeStruct((count, 512), BF16),
            jax.ShapeDtypeStruct((span, 512), BF16),
            jax.ShapeDtypeStruct((span, 512), BF16),
        ],
        compiler_params=params(40),
        cost_estimate=cost(32 * count * span * 1024, 8 * 2**20),
        name="attend_back",
    )(q_source, kv_source, kv_source, scaled, extra)


def norm_parts(tensor):
    center = tensor - jnp.mean(tensor, axis=-1, keepdims=True)
    scale = lax.rsqrt(jnp.mean(center * center, axis=-1, keepdims=True) + EPSILON)
    return center * scale, scale


def norm_back(q, normed, scale):
    return scale * (
        q - jnp.mean(q, axis=-1, keepdims=True) - normed * jnp.mean(q * normed, axis=-1, keepdims=True)
    )


def place_blocks(own_ref, sources, target, sems):
    copies = []
    for core in range(2):
        source = sources[core]
        by_seq = len(source.shape) == 4
        seq_count = source.shape[0] if by_seq else 1
        z_count, rows, cols = source.shape[-3:]
        by_rows = by_seq and cols == target.shape[1]
        for j in range(seq_count):
            for i in range(z_count):
                block = 2 * (own_ref[1] ^ i) + (own_ref[2] ^ core)
                across = slice(None)
                if by_rows:
                    block = block * seq_count + (own_ref[0] ^ j)
                elif by_seq:
                    across = pl.ds(pl.multiple_of((own_ref[0] ^ j) * cols, cols), cols)
                down = pl.ds(pl.multiple_of(block * rows, rows), rows)
                piece = source.at[j, i] if by_seq else source.at[i]
                copy = pltpu.make_async_copy(piece, target.at[down, across], sems.at[len(copies)])
                copies.append(copy)
    return copies


def fetches(own_ref, refs, target, sems, cols=None):
    if cols is not None:
        axes = len(refs[0].shape) - 1
        refs = [ref.at[(slice(None),) * axes + (cols,)] for ref in refs]
        target = target.at[:, cols]
    if len(refs) == 2:
        return place_blocks(own_ref, refs, target, sems)
    return [pltpu.make_async_copy(refs[0], target, sems.at[0])]


def launch(copies):
    for copy in copies:
        copy.start()


def finish(copies):
    for copy in copies:
        copy.wait()


def hand_out(held, outs, sems):
    sources = [held] if len(outs) == 1 else [held.at[0], held.at[1]]
    copies = [
        pltpu.make_async_copy(source, out, sems.at[i])
        for i, (source, out) in enumerate(zip(sources, outs))
    ]
    launch(copies)
    finish(copies)


def outs_of(shape, split):
    if split:
        return [jax.ShapeDtypeStruct(shape[1:], BF16)] * 2
    return [jax.ShapeDtypeStruct(shape, BF16)]


def copies_of(parts):
    count = 1
    for size in parts[0].shape[:-2]:
        count *= size
    return max(1, count * len(parts))


def project_kernel(chunk, parts, own_ref, hidden_ref, gain_ref, *refs):
    sources, (normed_out, out_ref, whole_out, normed_ref, whole_ref, sems, out_sems) = (
        refs[:parts],
        refs[parts:],
    )
    copies = fetches(own_ref, sources, whole_ref, sems)
    launch(copies)
    count = hidden_ref.shape[0]
    for row in range(0, count, chunk):
        at = slice(row, row + chunk)
        normed_ref[at, :] = (norm_parts(hidden_ref[at, :])[0] * gain_ref[...]).astype(BF16)
    finish(copies)
    copies = [
        pltpu.make_async_copy(normed_ref, normed_out, out_sems.at[0]),
        pltpu.make_async_copy(whole_ref, whole_out, out_sems.at[1]),
    ]
    launch(copies)
    for row in range(0, count, chunk):
        at = slice(row, row + chunk)
        out_ref[at, :] = nn(normed_ref[at, :], whole_ref[...]).astype(BF16)
    finish(copies)


def project(own, hidden, gain, parts, cols):
    count, width = hidden.shape
    in_hbm = pl.BlockSpec(memory_space=pltpu.HBM)
    return pl.pallas_call(
        functools.partial(project_kernel, min(512, count), len(parts)),
        in_specs=[pl.BlockSpec(memory_space=pltpu.SMEM)]
        + [IN_VMEM] * 2
        + [pl.BlockSpec(memory_space=pl.ANY)] * len(parts),
        out_specs=[in_hbm, IN_VMEM, in_hbm],
        scratch_shapes=[
            pltpu.VMEM((count, width), BF16),
            pltpu.VMEM((width, cols), BF16),
            pltpu.SemaphoreType.DMA((copies_of(parts),)),
            pltpu.SemaphoreType.DMA((2,)),
        ],
        out_shape=[
            pltpu.HBM((count, width), BF16),
            jax.ShapeDtypeStruct((count, cols), BF16),
            pltpu.HBM((width, cols), BF16),
        ],
        compiler_params=params(10),
        cost_estimate=cost(4 * (2 * count * width * cols), 4 * (8 * 2**20)),
        name="project",
    )(own, hidden, gain, *parts)


def rise_kernel(cfg, own_ref, hidden_ref, att_ref, cot_ref, gain_ref, *refs):
    seq_count, dp_count, split, chunk, up_parts, down_parts = cfg
    up_sources, refs = refs[:up_parts], refs[up_parts:]
    down_sources, refs = refs[:down_parts], refs[down_parts:]
    outs = 2 if split else 1
    out_ref, normed_ref, scale_ref, slope_ref, w_up, w_down, *refs = refs
    grad_outs, refs = refs[:outs], refs[outs:]
    act_ref, cot_t, grad_ref, up_sems, down_sems, out_sems = refs
    count, width = hidden_ref.shape
    raised = act_ref.shape[1]
    up_copies = [
        fetches(own_ref, up_sources, w_up, up_sems.at[i], slice(start, start + 512))
        for i, start in enumerate(range(0, width + raised, 512))
    ]
    down_copies = fetches(own_ref, down_sources, w_down, down_sems)
    for copies in up_copies[:2] + [down_copies] + up_copies[2:]:
        launch(copies)
    cot_t[...] = cot_ref[...].T
    finish(up_copies[0])
    for row in range(0, count, chunk):
        at = slice(row, row + chunk)
        first = hidden_ref[at, :] + nn(att_ref[at, :], w_up[:, :width])
        normed, scale = norm_parts(first)
        normed_ref[at, :] = normed
        scale_ref[at, :] = jnp.broadcast_to(scale, (chunk, scale_ref.shape[1]))
        normed_two = (normed * gain_ref[...]).astype(BF16)
        total = first
        for start in range(0, raised, 512):
            stop = start + 512
            if row == 0:
                finish(up_copies[1 + start // 512])
            v = nn(normed_two, w_up[:, width + start : width + stop])
            square = v * v
            t = jnp.tanh(v * (0.7978845608028654 + 0.035677408136300125 * square))
            half = 0.5 + 0.5 * t
            act = (v * half).astype(BF16)
            slope = half + v * (0.5 - 0.5 * t * t) * (
                0.7978845608028654 + 0.10703222440890037 * square
            )
            act_ref[at, start:stop] = act
            slope_ref[at, start:stop] = slope.astype(BF16)
            if row == 0 and start == 0:
                finish(down_copies)
            total = total + nn(act, w_down[start:stop, :])
        out_ref[at, :] = total.astype(BF16)
    if not split:
        for start in range(0, raised, 512):
            grad_ref[:, start : start + 512] = nn(
                cot_t[...], act_ref[:, start : start + 512]
            ).astype(BF16)
        hand_out(grad_ref, grad_outs, out_sems)
        return
    cols = width // seq_count
    rows = raised // dp_count
    copies = []
    for i in range(dp_count // 2):
        result = nn(cot_t[...], act_ref[:, 2 * i * rows : 2 * (i + 1) * rows]).astype(BF16)
        z = i ^ own_ref[1]
        for s in range(seq_count):
            piece = result[s * cols : (s + 1) * cols, :]
            for core in range(2):
                for part in range(rows // 128):
                    col = core * rows + part * 128
                    grad_ref[core ^ own_ref[2], z, s ^ own_ref[0], part] = piece[:, col : col + 128]
        for core in range(2):
            copy = pltpu.make_async_copy(
                grad_ref.at[core, z], grad_outs[core].at[z], out_sems.at[len(copies)]
            )
            copies.append(copy)
            copy.start()
    finish(copies)


def rise(own, hidden, att, cot, gain, up_parts, down_parts, raised, seq_count, dp_count, split):
    count, width = hidden.shape
    if split:
        parts = raised // dp_count // 128
        grad_shape = (2, dp_count // 2, seq_count, parts, width // seq_count, 128)
    else:
        grad_shape = (width, raised)
    chunk = min(512, count)
    cfg = (seq_count, dp_count, split, chunk, len(up_parts), len(down_parts))
    grads = outs_of(grad_shape, split)
    up_shape, down_shape = (width, width + raised), (raised, width)
    anywhere = pl.BlockSpec(memory_space=pl.ANY)
    return pl.pallas_call(
        functools.partial(rise_kernel, cfg),
        in_specs=[pl.BlockSpec(memory_space=pltpu.SMEM)]
        + [IN_VMEM] * 4
        + [anywhere] * (len(up_parts) + len(down_parts)),
        out_specs=[IN_VMEM] * 6 + [anywhere] * len(grads),
        scratch_shapes=[
            pltpu.VMEM((count, raised), BF16),
            pltpu.VMEM((width, count), BF16),
            pltpu.VMEM(grad_shape, BF16),
            pltpu.SemaphoreType.DMA(((width + raised) // 512, copies_of(up_parts))),
            pltpu.SemaphoreType.DMA((copies_of(down_parts),)),
            pltpu.SemaphoreType.DMA((dp_count,)),
        ],
        out_shape=[
            jax.ShapeDtypeStruct((count, width), BF16),
            jax.ShapeDtypeStruct((count, width), F32),
            jax.ShapeDtypeStruct((count, 128), F32),
            jax.ShapeDtypeStruct((count, raised), BF16),
            jax.ShapeDtypeStruct(up_shape, BF16),
            jax.ShapeDtypeStruct(down_shape, BF16),
        ]
        + grads,
        compiler_params=params(12),
        cost_estimate=cost(7 * 2**30, 24 * 2**20),
        name="rise",
    )(own, hidden, att, cot, gain, *up_parts, *down_parts)


def fall_kernel(
    cfg,
    own_ref,
    cot_ref,
    slope_ref,
    normed_ref,
    scale_ref,
    att_ref,
    den_ref,
    gain_ref,
    w_up,
    w_down,
    first_ref,
    scaled_ref,
    extra_ref,
    gain_sum_ref,
    *refs,
):
    seq_count, dp_count, split, chunk = cfg
    outs = 2 if split else 1
    grad_outs, (raise_ref, normed_t, att_t, branch_ref, grad_ref, out_sems) = (
        refs[:outs],
        refs[outs:],
    )
    count, width = cot_ref.shape
    raised = raise_ref.shape[1]
    gain = gain_ref[...]
    lane = lax.broadcasted_iota(jnp.int32, (128, width), 1)
    spread = lax.broadcasted_iota(jnp.int32, (128, width), 0) == 16 * (lane // 64)
    spread = jnp.where(spread, 1.0, 0.0).astype(BF16)
    row = lax.broadcasted_iota(jnp.int32, (128, 128), 0)
    col = lax.broadcasted_iota(jnp.int32, (128, 128), 1)
    swap = jnp.where((row < 64) != (col < 64), 1.0, 0.0).astype(BF16)
    even = lax.broadcasted_iota(jnp.int32, (1, 128), 1) % 2 == 0
    gain_sum = jnp.zeros((1, width), F32)
    att_t[...] = att_ref[...].T
    for top in range(0, count, chunk):
        at = slice(top, top + chunk)
        cot = cot_ref[at, :]
        normed = normed_ref[at, :]
        normed_t[:, at] = (normed * gain).astype(BF16).T
        back = jnp.zeros((chunk, width), F32)
        for start in range(0, raised, 512):
            stop = start + 512
            grad_raised = (nt(cot, w_down[start:stop, :]) * slope_ref[at, start:stop]).astype(BF16)
            raise_ref[at, start:stop] = grad_raised
            back = back + nt(grad_raised, w_up[:, width + start : width + stop])
        gain_sum = gain_sum + jnp.sum(back * normed, axis=0, keepdims=True)
        grad_first = cot.astype(F32) + norm_back(back * gain, normed, scale_ref[at, :1])
        first_ref[at, :] = grad_first
        branch = grad_first.astype(BF16)
        branch_ref[at, :] = branch
        den = den_ref[at, :]
        coarse = den.astype(BF16)
        fine = (den - coarse.astype(F32)).astype(BF16)
        ratio = nt(branch, w_up[:, :width]) / (nn(coarse, spread) + nn(fine, spread))
        scaled_ref[at, :] = ratio.astype(BF16)
        product = ratio * att_ref[at, :]
        coarse = product.astype(BF16)
        fine = (product - coarse.astype(F32)).astype(BF16)
        for start in range(0, width, 128):
            stop = start + 128
            offset = nn(coarse[:, start:stop], swap) + nn(fine[:, start:stop], swap)
            upper = offset.astype(BF16)
            lower = (offset - upper.astype(F32)).astype(BF16)
            extra_ref[at, start:stop] = jnp.where(even, upper, lower)
    gain_sum_ref[...] = gain_sum
    if not split:
        grad_ref[:, :width] = nn(att_t[...], branch_ref[...]).astype(BF16)
        for start in range(0, raised, 512):
            grad_ref[:, width + start : width + start + 512] = nn(
                normed_t[...], raise_ref[:, start : start + 512]
            ).astype(BF16)
        hand_out(grad_ref, grad_outs, out_sems)
        return
    cols = raised // seq_count
    wide = width // seq_count
    rows = width // dp_count
    copies = []

    def keep(result, s, at):
        for d in range(dp_count):
            grad_ref[(d % 2) ^ own_ref[2], s ^ own_ref[0], (d // 2) ^ own_ref[1], :, at] = result[
                d * rows : (d + 1) * rows, :
            ]

    result = nn(att_t[...], branch_ref[...]).astype(BF16)
    for s in range(seq_count):
        keep(result[:, s * wide : (s + 1) * wide], s, slice(0, wide))
    for s in range(seq_count):
        result = nn(normed_t[...], raise_ref[:, s * cols : (s + 1) * cols]).astype(BF16)
        keep(result, s, slice(wide, wide + cols))
        for core in range(2):
            copy = pltpu.make_async_copy(
                grad_ref.at[core, s ^ own_ref[0]],
                grad_outs[core].at[s ^ own_ref[0]],
                out_sems.at[len(copies)],
            )
            copies.append(copy)
            copy.start()
    finish(copies)


def fall(own, cot, slope, normed, scale, att, den, gain, w_up, w_down, seq_count, dp_count, split):
    count, width = cot.shape
    raised = w_down.shape[0]
    if split:
        grad_shape = (2, seq_count, dp_count // 2, width // dp_count, (width + raised) // seq_count)
    else:
        grad_shape = (width, width + raised)
    grads = outs_of(grad_shape, split)
    cfg = (seq_count, dp_count, split, min(512, count))

    def sds(dtype):
        return jax.ShapeDtypeStruct((count, width), dtype)

    return pl.pallas_call(
        functools.partial(fall_kernel, cfg),
        in_specs=[pl.BlockSpec(memory_space=pltpu.SMEM)] + [IN_VMEM] * 9,
        out_specs=[IN_VMEM] * 4 + [pl.BlockSpec(memory_space=pl.ANY)] * len(grads),
        scratch_shapes=[
            pltpu.VMEM((count, raised), BF16),
            pltpu.VMEM((width, count), BF16),
            pltpu.VMEM((width, count), BF16),
            pltpu.VMEM((count, width), BF16),
            pltpu.VMEM(grad_shape, BF16),
            pltpu.SemaphoreType.DMA((2 * seq_count,)),
        ],
        out_shape=[
            sds(F32),
            sds(BF16),
            sds(BF16),
            jax.ShapeDtypeStruct((1, width), F32),
        ]
        + grads,
        compiler_params=params(14),
        cost_estimate=cost(4 * (8 * 2**30), 4 * (24 * 2**20)),
        name="fall",
    )(own, cot, slope, normed, scale, att, den, gain, w_up, w_down)


def last_kernel(chunk, hidden_ref, first_ref, gain_ref, mask_ref, w_ref, *refs):
    *grads, out_ref, sums_ref = refs
    masked = gain_sum = 0.0
    for top in range(0, hidden_ref.shape[0], chunk):
        at = slice(top, top + chunk)
        back = 0.0
        start = 0
        for ref in grads:
            stop = start + ref.shape[1]
            back = back + nt(ref[at, :], w_ref[:, start:stop])
            start = stop
        normed, scale = norm_parts(hidden_ref[at, :])
        grad = first_ref[at, :] + norm_back(back * gain_ref[...], normed, scale)
        coarse = grad.astype(BF16)
        out_ref[at, :] = coarse
        fine = (grad - coarse.astype(F32)).astype(BF16)
        mask = mask_ref[:, at]
        masked = masked + nn(mask, coarse) + nn(mask, fine)
        gain_sum = gain_sum + jnp.sum(back * normed, axis=0, keepdims=True)
    sums_ref[...] = masked
    sums_ref[1:2, :] = gain_sum


def last(hidden, grad_first, gain, mask, w_qkv, grads):
    count, width = hidden.shape
    return pl.pallas_call(
        functools.partial(last_kernel, min(512, count)),
        in_specs=[IN_VMEM] * (5 + len(grads)),
        out_specs=[IN_VMEM] * 2,
        out_shape=[
            jax.ShapeDtypeStruct((count, width), BF16),
            jax.ShapeDtypeStruct((8, width), F32),
        ],
        compiler_params=params(8),
        cost_estimate=cost(8 * (6 * count * width * width), 8 * (12 * 2**20)),
        name="last",
    )(hidden, grad_first, gain, mask, w_qkv, *grads)


def swap_along(value, axis, mask):
    count = lax.axis_size(axis)
    return lax.ppermute(value, axis, [(i, i ^ mask) for i in range(count)])


def add_up(values):
    total = values[0].astype(F32)
    for value in values[1:]:
        total = total + value.astype(F32)
    return total


def together(*values):
    return lax.optimization_barrier(values)


def from_plane(values):
    return [values[0]] + [swap_along(values[j], "seq", j) for j in range(1, len(values))]


def from_line(values):
    return [values[0]] + [swap_along(values[j], "dp", 2 * j) for j in range(1, len(values))]


def other_core(value):
    return swap_along(value, "dp", 1)


def add_split(left, right):
    return [add_up((left[j], right[j])).astype(BF16) for j in range(left.shape[0])]


def both_cores(value):
    return [value, other_core(value)]


def split_first(value):
    return [value[j] for j in range(value.shape[0])]


def halve_line(value):
    half = value.shape[0] // 2
    while half:
        came = swap_along(value[half:], "dp", 2 * half)
        value = add_up((value[:half], came))
        half //= 2
        if half:
            value = value.astype(BF16)
    return value[0]


def gather_line(value):
    return jnp.stack(from_line([value] * (lax.axis_size("dp") // 2)))


def gather_plane(value):
    return jnp.stack(from_plane([value] * lax.axis_size("seq")))


def own_columns(weight):
    cols = weight.shape[1] // lax.axis_size("seq")
    return lax.dynamic_slice_in_dim(weight, lax.axis_index("seq") * cols, cols, 1)


def pieces_of(whole, own, seq_count, dp_count, flipped):
    row_blocks, col_blocks = (seq_count, dp_count) if flipped else (dp_count, seq_count)
    rows, cols = whole.shape[0] // row_blocks, whole.shape[1] // col_blocks
    whole = whole.reshape(row_blocks, rows, col_blocks, cols)
    whole = jnp.transpose(whole, (0, 2, 1, 3) if flipped else (2, 0, 1, 3))
    whole = whole.reshape(seq_count, dp_count // 2, 2, rows, cols)
    whole = jnp.take(whole, jnp.arange(seq_count) ^ own[0], axis=0)
    whole = jnp.take(whole, jnp.arange(dp_count // 2) ^ own[1], axis=1)
    whole = jnp.take(whole, jnp.arange(2) ^ own[2], axis=2)
    return jnp.transpose(whole, (2, 0, 1, 3, 4))


def per_device(
    inputs,
    cotangent,
    timestep,
    unmask_order,
    mask_embed,
    ln1_gain,
    weight_qkv,
    weight_out,
    ln2_gain,
    weight_up,
    weight_down,
):
    rows, segment, width = inputs.shape
    raised = weight_up.shape[1]
    seq_count, dp_count = lax.axis_size("seq"), lax.axis_size("dp")
    outer = seq_count // rows
    split = outer == 1 and (seq_count, dp_count) == (4, 8)
    place = lax.axis_index("seq")
    dp_place = lax.axis_index("dp")
    row = place % rows
    own = jnp.stack([place, dp_place // 2, dp_place % 2]).astype(jnp.int32)

    def by_partner(value):
        return [lax.dynamic_index_in_dim(value, row ^ j, 0, keepdims=False) for j in range(rows)]

    def to_rows(value):
        return jnp.concatenate(from_plane(by_partner(value)))

    def to_partners(value):
        return from_plane([value[j * segment : (j + 1) * segment] for j in range(rows)])

    def by_row(parts):
        out = jnp.zeros((rows,) + parts[0].shape, parts[0].dtype)
        for j in (0, 3, 2, 1) if rows == 4 else range(rows):
            out = lax.dynamic_update_index_in_dim(out, parts[j], row ^ j, 0)
        return out

    masked = (unmask_order <= timestep[:, None]).astype(BF16)
    masked = jnp.pad(masked[:, None, :], ((0, 0), (0, 15), (0, width - segment)))
    came = by_partner(jnp.concatenate((inputs, masked), axis=1))
    up_and_out = jnp.concatenate((weight_out, weight_up), axis=1)
    if split:
        down_rows = weight_down.shape[0] // seq_count
        own_down = lax.dynamic_slice_in_dim(weight_down, place * down_rows, down_rows, 0)
        line = gather_line(jnp.concatenate((own_columns(weight_qkv), own_down), axis=1))
        came = from_plane(came)
        line, up_and_out = together(line, up_and_out)
        line_up = jnp.stack((up_and_out, swap_along(up_and_out, "dp", 4)))
        line_up = [line_up, swap_along(line_up, "dp", 2)]
        plane_qkv = gather_plane(line[..., :-width])
        line_down = line[..., -width:].reshape(-1, width)
        cot = cotangent
        parts_qkv = both_cores(plane_qkv)
        cot = from_plane([jnp.concatenate((part, line_down)) for part in by_partner(cot)])
    else:
        came, cot = from_plane(came), from_plane(by_partner(cotangent))
        parts_qkv, parts_up, parts_down = (
            [lax.all_gather(weight, "dp", axis=0, tiled=True)]
            for weight in (weight_qkv, up_and_out, weight_down)
        )

    block = jnp.concatenate([part[:segment] for part in came]).astype(F32)
    mask_row = jnp.concatenate([part[segment, :segment] for part in came])
    hidden = block + mask_row.astype(F32)[:, None] * mask_embed
    normed_one, projected, whole_qkv = project(
        own, hidden, ln1_gain[None, :], parts_qkv, 3 * width
    )
    if outer > 1:
        groups = [[j * rows + i for j in range(outer)] for i in range(rows)]
        far = lax.all_gather(
            projected[:, width:], "seq", axis=0, tiled=True, axis_index_groups=groups
        )
        attended, denominators = attend(projected, far, 0)
    else:
        attended, denominators = attend_row(projected)
    if split:
        line_up, attended = together(line_up, attended)
        parts_up = both_cores(jnp.stack(line_up, axis=1).reshape((-1,) + up_and_out.shape))
        cot, parts_up[0] = together(cot, parts_up[0])
        plane_down = jnp.stack([part[segment:] for part in cot])
        plane_down = plane_down.reshape(seq_count, dp_count // 2, -1, width)
        parts_down = both_cores(plane_down)
    cot = jnp.concatenate([part[:segment] for part in cot])
    outputs, normed, scale, slope, whole_up, whole_down, *grad_down = rise(
        own,
        hidden,
        attended,
        cot,
        ln2_gain[None, :],
        parts_up,
        parts_down,
        raised,
        seq_count,
        dp_count,
        split,
    )
    result = to_partners(outputs)
    grad_first, scaled, extra, sum_gain_two, *grad_up = fall(
        own,
        cot,
        slope,
        normed,
        scale,
        attended,
        denominators,
        ln2_gain[None, :],
        whole_up,
        whole_down,
        seq_count,
        dp_count,
        split,
    )
    mask_rows = jnp.broadcast_to(mask_row[None, :], (8, mask_row.shape[0]))
    if split:
        grad_down[1] = other_core(grad_down[1])
        grad_down, scaled, grad_up, result = together(grad_down, scaled, grad_up, result)
        line_down = from_line(add_split(*grad_down))
        grad_up[1] = other_core(grad_up[1])
        half = attend_back_half(projected, scaled, extra)
        grad_up, half, line_down[1] = together(grad_up, half, line_down[1])
        plane_up = from_plane(add_split(*grad_up))
        *rest, mine_qkv, other_qkv = attend_back_sum(
            own, projected, scaled, extra, normed_one, half, seq_count, dp_count
        )
        plane_up, line_down, rest, mine_qkv, other_qkv = together(
            plane_up, line_down, rest, mine_qkv, other_qkv
        )
        grads = [part for pair in zip(half, rest) for part in pair]
        both_qkv = (mine_qkv, other_core(other_qkv))
        line_up = add_up(plane_up).astype(BF16)
        z_half = line_up.shape[0] // 2
        line_came = swap_along(line_up[z_half:], "dp", 2 * z_half)
        tall = width // dp_count
        down = add_up(line_down).astype(BF16).reshape(seq_count, -1, tall, 128)
        both_qkv, mask_rows = together(both_qkv, mask_rows)
        mine_qkv = [part.reshape(-1, tall, 128) for part in add_split(*both_qkv)]
        plane_last = from_plane([jnp.concatenate((mine_qkv[j], down[j])) for j in range(seq_count)])
    else:
        dq, dk, dv = attend_back(projected, far, scaled, extra)
        both = jnp.concatenate((dk, dv), axis=1)
        both = lax.psum_scatter(
            both, "seq", scatter_dimension=0, tiled=True, axis_index_groups=groups
        )
        grads = [dq, both]
        grad_qkv = lax.dot_general(
            normed_one,
            jnp.concatenate(grads, axis=1),
            (((0,), (0,)), ((), ())),
            preferred_element_type=F32,
        ).astype(BF16)
        cut = functools.partial(pieces_of, own=own, seq_count=seq_count, dp_count=dp_count)
        (grad_up,), (grad_down,) = grad_up, grad_down
        grad_out, grad_up = (
            cut(part, flipped=False) for part in (grad_up[:, :width], grad_up[:, width:])
        )
        grad_up = jnp.concatenate((grad_out, grad_up), axis=-1)
        grad_qkv = cut(grad_qkv, flipped=False)
        grad_down = cut(grad_down, flipped=True)
        sums = []
        for pieces in (grad_qkv, grad_up, grad_down):
            mine = add_up((pieces[0], other_core(pieces[1]))).astype(BF16)
            plane = add_up(from_plane(split_first(mine))).astype(BF16)
            sums.append(add_up(from_line(split_first(plane))))
        sum_qkv, sum_up, sum_down = sums
        sum_down = sum_down.T
    grad_hidden, sums = last(
        hidden, grad_first, ln1_gain[None, :], mask_rows, whole_qkv, grads
    )
    vectors = jnp.concatenate((sums[0:2], sum_gain_two, jnp.zeros((5, width), F32)), axis=0)
    vectors = vectors + other_core(vectors)
    bit = 2
    while bit < dp_count:
        vectors = vectors + swap_along(vectors, "dp", bit)
        bit *= 2
    if split:
        grad_hidden, vectors, line_came, plane_last = together(
            grad_hidden, vectors, line_came, plane_last
        )
        sum_up = add_up((line_up[:z_half], line_came)).astype(BF16)
        kinds = mine_qkv[0].shape[0]
        sum_qkv = add_up([part[:kinds] for part in plane_last]).astype(BF16)
        sum_qkv = sum_qkv.reshape((dp_count // 2, -1) + sum_qkv.shape[1:])
        line_came = swap_along(sum_qkv[z_half:], "dp", 2 * z_half)
        line_came, plane_last, sum_up = together(line_came, plane_last, sum_up)
        sum_qkv = halve_line(add_up((sum_qkv[:z_half], line_came)).astype(BF16))
        sum_up = halve_line(sum_up)
        sum_down = add_up([part[kinds:] for part in plane_last])
        sum_down = sum_down.reshape(-1, width // seq_count, 128)
        sum_down = jnp.transpose(sum_down, (0, 2, 1)).reshape(-1, width // seq_count)
        sum_qkv = jnp.transpose(sum_qkv, (1, 0, 2)).reshape(tall, -1)
    grad_inputs = [grad_hidden[j * segment : (j + 1) * segment] for j in range(rows)]
    if split:
        coarse = vectors.astype(BF16)
        terms = jnp.concatenate((coarse, (vectors - coarse.astype(F32)).astype(BF16)))
        grad_inputs = [jnp.concatenate((part, terms)) for part in grad_inputs]
    grad_inputs = from_plane(grad_inputs)
    if split:
        vectors = add_up([part[segment:] for part in grad_inputs])
        vectors = vectors[:8] + vectors[8:]
        grad_inputs = [part[:segment] for part in grad_inputs]
    else:
        vectors = add_up(from_plane([vectors] * seq_count))
    block_width = width // dp_count
    vectors = lax.dynamic_slice_in_dim(vectors, dp_place * block_width, block_width, 1)
    out_cols = width // seq_count
    return (
        by_row(result),
        by_row(grad_inputs),
        vectors[0],
        vectors[1],
        sum_qkv,
        sum_up[:, :out_cols],
        vectors[2],
        sum_up[:, out_cols:],
        sum_down,
    )


def solution(mesh):
    in_specs = (
        P("dp", "seq", None),
        P("dp", "seq", None),
        P("dp"),
        P("dp", "seq"),
        P(),
        P(),
        P("dp", None),
        P("dp", None),
        P(),
        P("dp", None),
        P("dp", None),
    )
    out_specs = (
        P("dp", "seq", None),
        P("dp", "seq", None),
        P("dp"),
        P("dp"),
        P("dp", "seq"),
        P("dp", "seq"),
        P("dp"),
        P("dp", "seq"),
        P("dp", "seq"),
    )
    return jax.shard_map(
        per_device, mesh=mesh, in_specs=in_specs, out_specs=out_specs, check_vma=False
    )
```

```python
import functools

import jax
import jax.numpy as jnp
from jax import lax
from jax.experimental import pallas as pl
from jax.experimental.pallas import tpu as pltpu
from jax.sharding import PartitionSpec as P

EPSILON = 1e-05
HEADS = 8
F32 = jnp.float32
BF16 = jnp.bfloat16
IN_VMEM = pl.BlockSpec(memory_space=pltpu.VMEM)


def nn(left, right):
    return jnp.dot(left, right, preferred_element_type=F32)


def nt(left, right):
    return lax.dot_general(left, right, (((1,), (1,)), ((), ())), preferred_element_type=F32)


def params(vmem):
    return pltpu.CompilerParams(vmem_limit_bytes=vmem * 2**20)


def cost(flops, bytes_accessed):
    return pl.CostEstimate(
        flops=int(flops), bytes_accessed=int(bytes_accessed), transcendentals=0
    )


def attend_kernel(chunk, q_ref, k_ref, v_ref, out_ref, den_ref):
    count = q_ref.shape[0]
    pair = pl.program_id(0)
    lane = lax.broadcasted_iota(jnp.int32, (1, 128), 1)
    low = lane < 64
    keys = k_ref[...]
    values = v_ref[...]
    one = jnp.ones_like(values)
    values_low = jnp.where(low, values, one)
    values_high = jnp.where(low, one, values)
    for start in range(0, count, chunk):
        at = slice(start, start + chunk)
        q = q_ref[at, :] * jnp.asarray(0.125, BF16)
        zero = jnp.zeros_like(q)
        left = nn(jnp.exp(nt(jnp.where(low, q, zero), keys)).astype(BF16), values_low)
        right = nn(jnp.exp(nt(jnp.where(low, zero, q), keys)).astype(BF16), values_high)
        swapped = jnp.where(low, right, left)
        den = pltpu.roll(swapped, 64, 1)
        out_ref[at, :] = (jnp.where(low, left, right) / den).astype(BF16)
        first = lane // 16 == 2 * pair
        second = lane // 16 == 2 * pair + 1
        mine = jnp.where(
            first, jnp.where(low, den, swapped), jnp.where(low, swapped, den)
        )
        den_ref[at, :] = jnp.where(first | second, mine, den_ref[at, :])


def attend(q_source, kv_source, kv_shift):
    count, span = q_source.shape[0], kv_source.shape[0]
    chunk = min(256, count)
    return pl.pallas_call(
        functools.partial(attend_kernel, chunk),
        grid=(4,),
        in_specs=[
            pl.BlockSpec((count, 128), lambda p: (0, p)),
            pl.BlockSpec((span, 128), lambda p: (0, kv_shift + p)),
            pl.BlockSpec((span, 128), lambda p: (0, kv_shift + 4 + p)),
        ],
        out_specs=[
            pl.BlockSpec((count, 128), lambda p: (0, p)),
            pl.BlockSpec((count, 128), lambda p: (0, 0)),
        ],
        out_shape=[
            jax.ShapeDtypeStruct((count, 512), BF16),
            jax.ShapeDtypeStruct((count, 128), F32),
        ],
        compiler_params=params(12),
        cost_estimate=cost(16 * count * span * 1024, 5 * 2**20),
        name="attend",
    )(q_source, kv_source, kv_source)


def attend_row_kernel(chunk, own_ref, out_ref, den_ref):
    count, width = out_ref.shape
    lane = lax.broadcasted_iota(jnp.int32, (1, 128), 1)
    low = lane < 64
    for start in range(0, count, chunk):
        at = slice(start, start + chunk)
        sums = jnp.zeros((chunk, 128), F32)
        for pair in range(width // 128):
            col = pair * 128
            keys = own_ref[:, width + col : width + col + 128]
            values = own_ref[:, 2 * width + col : 2 * width + col + 128]
            one = jnp.ones_like(values)
            q = own_ref[at, col : col + 128] * jnp.asarray(0.125, BF16)
            zero = jnp.zeros_like(q)
            left = nn(
                jnp.exp(nt(jnp.where(low, q, zero), keys)).astype(BF16),
                jnp.where(low, values, one),
            )
            right = nn(
                jnp.exp(nt(jnp.where(low, zero, q), keys)).astype(BF16),
                jnp.where(low, one, values),
            )
            swapped = jnp.where(low, right, left)
            den = pltpu.roll(swapped, 64, 1)
            out_ref[at, col : col + 128] = (jnp.where(low, left, right) / den).astype(BF16)
            first, second = lane // 16 == 2 * pair, lane // 16 == 2 * pair + 1
            sums = jnp.where(first, jnp.where(low, den, swapped), sums)
            sums = jnp.where(second, jnp.where(low, swapped, den), sums)
        den_ref[at, :] = sums


def attend_row(projected):
    count, width = projected.shape[0], projected.shape[1] // 3
    return pl.pallas_call(
        functools.partial(attend_row_kernel, min(256, count)),
        in_specs=[IN_VMEM],
        out_specs=[IN_VMEM] * 2,
        out_shape=[
            jax.ShapeDtypeStruct((count, width), BF16),
            jax.ShapeDtypeStruct((count, 128), F32),
        ],
        compiler_params=params(8),
        cost_estimate=cost(16 * count * count * 1024, 5 * 2**20),
        name="attend_row",
    )(projected)


def head_pair_back(chunk, q_ref, k_ref, v_ref, s_ref, x_ref, dk_ref, dv_ref):
    count, span = q_ref.shape[0], k_ref.shape[0]
    lane = lax.broadcasted_iota(jnp.int32, (1, 128), 1)
    low = lane < 64
    q = q_ref[...] * jnp.asarray(0.125, BF16)
    scaled = s_ref[...]
    extra = x_ref[...]
    zero = jnp.zeros_like(q)
    q_own = (jnp.where(low, q, zero), jnp.where(low, zero, q))
    s_own = (jnp.where(low, scaled, zero), jnp.where(low, zero, scaled))
    s_with = (jnp.where(low, scaled, extra), jnp.where(low, extra, scaled))
    minus = (
        jnp.where((lane == 64) | (lane == 65), -1.0, 0.0).astype(BF16),
        jnp.where((lane == 0) | (lane == 1), -1.0, 0.0).astype(BF16),
    )
    total = jnp.zeros((128, count), F32)
    for start in range(0, span, chunk):
        keys = k_ref[start : start + chunk, :]
        values = v_ref[start : start + chunk, :]
        none = jnp.zeros_like(keys)
        k_own = (jnp.where(low, keys, none), jnp.where(low, none, keys))
        v_with = (jnp.where(low, values, minus[0]), jnp.where(low, minus[1], values))
        dk = dv = 0.0
        for head in range(2):
            weights = jnp.exp(nt(keys, q_own[head]))
            slopes = (weights * nt(v_with[head], s_with[head])).astype(BF16)
            dv = dv + nn(weights.astype(BF16), s_own[head])
            dk = dk + nn(slopes, q_own[head])
            total = total + nn(k_own[head].T, slopes)
        dk_ref[start : start + chunk, :] = dk.astype(BF16)
        dv_ref[start : start + chunk, :] = dv.astype(BF16)
    return (total.T * 0.125).astype(BF16)


def attend_back_kernel(chunk, q_ref, k_ref, v_ref, s_ref, x_ref, dq_ref, dk_ref, dv_ref):
    dq_ref[...] = head_pair_back(chunk, q_ref, k_ref, v_ref, s_ref, x_ref, dk_ref, dv_ref)


def pair_views(col, width, proj_ref, s_ref, x_ref):
    at = [slice(shift + col, shift + col + 128) for shift in (0, width, 2 * width)]
    return [proj_ref.at[:, cols] for cols in at] + [s_ref.at[:, at[0]], x_ref.at[:, at[0]]]


def attend_back_half_kernel(chunk, proj_ref, s_ref, x_ref, dq_ref, dk_ref, dv_ref):
    width = s_ref.shape[1]
    for pair in range(2):
        col = pair * 128
        at = slice(col, col + 128)
        dq_ref[:, at] = head_pair_back(
            chunk,
            *pair_views(col, width, proj_ref, s_ref, x_ref),
            dk_ref.at[:, at],
            dv_ref.at[:, at],
        )


def attend_back_half(projected, scaled, extra):
    count, width = scaled.shape
    return pl.pallas_call(
        functools.partial(attend_back_half_kernel, min(512, count)),
        in_specs=[IN_VMEM] * 3,
        out_specs=[IN_VMEM] * 3,
        out_shape=[jax.ShapeDtypeStruct((count, width // 2), BF16)] * 3,
        compiler_params=params(9),
        cost_estimate=cost(16 * count * count * 1024, 6 * 2**20),
        name="attend_back_half",
    )(projected, scaled, extra)


def attend_back_sum_kernel(
    chunk,
    dp_count,
    own_ref,
    proj_ref,
    s_ref,
    x_ref,
    normed_ref,
    dq_first,
    dk_first,
    dv_first,
    dq_ref,
    dk_ref,
    dv_ref,
    mine_out,
    other_out,
    normed_t,
    joined,
    grad_ref,
    sems,
):
    width = s_ref.shape[1]
    normed_t[...] = normed_ref[...].T

    def weight_part(pairs, refs):
        for kind, ref in enumerate(refs):
            joined[:, kind * 256 : (kind + 1) * 256] = ref[...]
        result = nn(normed_t[...], joined[...]).astype(BF16)
        rows = result.shape[0] // dp_count
        per = grad_ref.shape[3]
        for kind in range(3):
            for i, pair in enumerate(pairs):
                block = pair + 4 * kind
                col, part = (block // per) ^ own_ref[0], block % per
                at = slice(kind * 256 + i * 128, kind * 256 + (i + 1) * 128)
                for d in range(dp_count):
                    grad_ref[(d % 2) ^ own_ref[2], col, (d // 2) ^ own_ref[1], part] = result[
                        d * rows : (d + 1) * rows, at
                    ]

    weight_part((0, 1), (dq_first, dk_first, dv_first))
    for pair in range(2, 4):
        at = slice((pair - 2) * 128, (pair - 1) * 128)
        dq_ref[:, at] = head_pair_back(
            chunk,
            *pair_views(pair * 128, width, proj_ref, s_ref, x_ref),
            dk_ref.at[:, at],
            dv_ref.at[:, at],
        )
    weight_part((2, 3), (dq_ref, dk_ref, dv_ref))
    hand_out(grad_ref, (mine_out, other_out), sems)


def attend_back_sum(own, projected, scaled, extra, normed, first_half, seq_count, dp_count):
    count, width = scaled.shape
    pieces = (2, seq_count, dp_count // 2, 12 // seq_count, width // dp_count, 128)
    return pl.pallas_call(
        functools.partial(attend_back_sum_kernel, min(512, count), dp_count),
        in_specs=[pl.BlockSpec(memory_space=pltpu.SMEM)] + [IN_VMEM] * 7,
        out_specs=[IN_VMEM] * 3 + [pl.BlockSpec(memory_space=pl.ANY)] * 2,
        scratch_shapes=[
            pltpu.VMEM((width, count), BF16),
            pltpu.VMEM((count, 768), BF16),
            pltpu.VMEM(pieces, BF16),
            pltpu.SemaphoreType.DMA((2,)),
        ],
        out_shape=[jax.ShapeDtypeStruct((count, width // 2), BF16)] * 3 + outs_of(pieces, True),
        compiler_params=params(13),
        cost_estimate=cost(20 * count * count * 1024, 10 * 2**20),
        name="attend_back_sum",
    )(own, projected, scaled, extra, normed, *first_half)


def attend_back(q_source, kv_source, scaled, extra):
    count, span = q_source.shape[0], kv_source.shape[0]
    chunk = min(512, span)
    own = pl.BlockSpec((count, 128), lambda p: (0, p))
    far = pl.BlockSpec((span, 128), lambda p: (0, p))
    return pl.pallas_call(
        functools.partial(attend_back_kernel, chunk),
        grid=(4,),
        in_specs=[
            own,
            pl.BlockSpec((span, 128), lambda p: (0, p)),
            pl.BlockSpec((span, 128), lambda p: (0, 4 + p)),
            own,
            own,
        ],
        out_specs=[own, far, far],
        out_shape=[
            jax.ShapeDtypeStruct((count, 512), BF16),
            jax.ShapeDtypeStruct((span, 512), BF16),
            jax.ShapeDtypeStruct((span, 512), BF16),
        ],
        compiler_params=params(40),
        cost_estimate=cost(32 * count * span * 1024, 8 * 2**20),
        name="attend_back",
    )(q_source, kv_source, kv_source, scaled, extra)


def norm_parts(tensor):
    center = tensor - jnp.mean(tensor, axis=-1, keepdims=True)
    scale = lax.rsqrt(jnp.mean(center * center, axis=-1, keepdims=True) + EPSILON)
    return center * scale, scale


def norm_back(q, normed, scale):
    return scale * (
        q - jnp.mean(q, axis=-1, keepdims=True) - normed * jnp.mean(q * normed, axis=-1, keepdims=True)
    )


def place_blocks(own_ref, sources, target, sems):
    copies = []
    for core in range(2):
        source = sources[core]
        by_seq = len(source.shape) == 4
        seq_count = source.shape[0] if by_seq else 1
        z_count, rows, cols = source.shape[-3:]
        by_rows = by_seq and cols == target.shape[1]
        for j in range(seq_count):
            for i in range(z_count):
                block = 2 * (own_ref[1] ^ i) + (own_ref[2] ^ core)
                across = slice(None)
                if by_rows:
                    block = block * seq_count + (own_ref[0] ^ j)
                elif by_seq:
                    across = pl.ds(pl.multiple_of((own_ref[0] ^ j) * cols, cols), cols)
                down = pl.ds(pl.multiple_of(block * rows, rows), rows)
                piece = source.at[j, i] if by_seq else source.at[i]
                copy = pltpu.make_async_copy(piece, target.at[down, across], sems.at[len(copies)])
                copies.append(copy)
    return copies


def fetches(own_ref, refs, target, sems, cols=None):
    if cols is not None:
        axes = len(refs[0].shape) - 1
        refs = [ref.at[(slice(None),) * axes + (cols,)] for ref in refs]
        target = target.at[:, cols]
    if len(refs) == 2:
        return place_blocks(own_ref, refs, target, sems)
    return [pltpu.make_async_copy(refs[0], target, sems.at[0])]


def launch(copies):
    for copy in copies:
        copy.start()


def finish(copies):
    for copy in copies:
        copy.wait()


def hand_out(held, outs, sems):
    sources = [held] if len(outs) == 1 else [held.at[0], held.at[1]]
    copies = [
        pltpu.make_async_copy(source, out, sems.at[i])
        for i, (source, out) in enumerate(zip(sources, outs))
    ]
    launch(copies)
    finish(copies)


def outs_of(shape, split):
    if split:
        return [jax.ShapeDtypeStruct(shape[1:], BF16)] * 2
    return [jax.ShapeDtypeStruct(shape, BF16)]


def copies_of(parts):
    count = 1
    for size in parts[0].shape[:-2]:
        count *= size
    return max(1, count * len(parts))


def project_kernel(chunk, parts, own_ref, hidden_ref, gain_ref, *refs):
    sources, (normed_out, out_ref, whole_out, normed_ref, whole_ref, sems, out_sems) = (
        refs[:parts],
        refs[parts:],
    )
    copies = fetches(own_ref, sources, whole_ref, sems)
    launch(copies)
    count = hidden_ref.shape[0]
    for row in range(0, count, chunk):
        at = slice(row, row + chunk)
        normed_ref[at, :] = (norm_parts(hidden_ref[at, :])[0] * gain_ref[...]).astype(BF16)
    finish(copies)
    copies = [
        pltpu.make_async_copy(normed_ref, normed_out, out_sems.at[0]),
        pltpu.make_async_copy(whole_ref, whole_out, out_sems.at[1]),
    ]
    launch(copies)
    for row in range(0, count, chunk):
        at = slice(row, row + chunk)
        out_ref[at, :] = nn(normed_ref[at, :], whole_ref[...]).astype(BF16)
    finish(copies)


def project(own, hidden, gain, parts, cols):
    count, width = hidden.shape
    in_hbm = pl.BlockSpec(memory_space=pltpu.HBM)
    return pl.pallas_call(
        functools.partial(project_kernel, min(512, count), len(parts)),
        in_specs=[pl.BlockSpec(memory_space=pltpu.SMEM)]
        + [IN_VMEM] * 2
        + [pl.BlockSpec(memory_space=pl.ANY)] * len(parts),
        out_specs=[in_hbm, IN_VMEM, in_hbm],
        scratch_shapes=[
            pltpu.VMEM((count, width), BF16),
            pltpu.VMEM((width, cols), BF16),
            pltpu.SemaphoreType.DMA((copies_of(parts),)),
            pltpu.SemaphoreType.DMA((2,)),
        ],
        out_shape=[
            pltpu.HBM((count, width), BF16),
            jax.ShapeDtypeStruct((count, cols), BF16),
            pltpu.HBM((width, cols), BF16),
        ],
        compiler_params=params(10),
        cost_estimate=cost(4 * (2 * count * width * cols), 4 * (8 * 2**20)),
        name="project",
    )(own, hidden, gain, *parts)


def rise_kernel(cfg, own_ref, hidden_ref, att_ref, cot_ref, gain_ref, *refs):
    seq_count, dp_count, split, chunk, up_parts, down_parts = cfg
    up_sources, refs = refs[:up_parts], refs[up_parts:]
    down_sources, refs = refs[:down_parts], refs[down_parts:]
    outs = 2 if split else 1
    out_ref, normed_ref, scale_ref, slope_ref, w_up, w_down, *refs = refs
    grad_outs, refs = refs[:outs], refs[outs:]
    act_ref, cot_t, grad_ref, up_sems, down_sems, out_sems = refs
    count, width = hidden_ref.shape
    raised = act_ref.shape[1]
    up_copies = [
        fetches(own_ref, up_sources, w_up, up_sems.at[i], slice(start, start + 512))
        for i, start in enumerate(range(0, width + raised, 512))
    ]
    down_copies = fetches(own_ref, down_sources, w_down, down_sems)
    for copies in up_copies[:2] + [down_copies] + up_copies[2:]:
        launch(copies)
    cot_t[...] = cot_ref[...].T
    finish(up_copies[0])
    for row in range(0, count, chunk):
        at = slice(row, row + chunk)
        first = hidden_ref[at, :] + nn(att_ref[at, :], w_up[:, :width])
        normed, scale = norm_parts(first)
        normed_ref[at, :] = normed
        scale_ref[at, :] = jnp.broadcast_to(scale, (chunk, scale_ref.shape[1]))
        normed_two = (normed * gain_ref[...]).astype(BF16)
        total = first
        for start in range(0, raised, 512):
            stop = start + 512
            if row == 0:
                finish(up_copies[1 + start // 512])
            v = nn(normed_two, w_up[:, width + start : width + stop])
            square = v * v
            t = jnp.tanh(v * (0.7978845608028654 + 0.035677408136300125 * square))
            half = 0.5 + 0.5 * t
            act = (v * half).astype(BF16)
            slope = half + v * (0.5 - 0.5 * t * t) * (
                0.7978845608028654 + 0.10703222440890037 * square
            )
            act_ref[at, start:stop] = act
            slope_ref[at, start:stop] = slope.astype(BF16)
            if row == 0 and start == 0:
                finish(down_copies)
            total = total + nn(act, w_down[start:stop, :])
        out_ref[at, :] = total.astype(BF16)
    if not split:
        for start in range(0, raised, 512):
            grad_ref[:, start : start + 512] = nn(
                cot_t[...], act_ref[:, start : start + 512]
            ).astype(BF16)
        hand_out(grad_ref, grad_outs, out_sems)
        return
    cols = width // seq_count
    rows = raised // dp_count
    copies = []
    for i in range(dp_count // 2):
        result = nn(cot_t[...], act_ref[:, 2 * i * rows : 2 * (i + 1) * rows]).astype(BF16)
        z = i ^ own_ref[1]
        for s in range(seq_count):
            piece = result[s * cols : (s + 1) * cols, :]
            for core in range(2):
                for part in range(rows // 128):
                    col = core * rows + part * 128
                    grad_ref[core ^ own_ref[2], z, s ^ own_ref[0], part] = piece[:, col : col + 128]
        for core in range(2):
            copy = pltpu.make_async_copy(
                grad_ref.at[core, z], grad_outs[core].at[z], out_sems.at[len(copies)]
            )
            copies.append(copy)
            copy.start()
    finish(copies)


def rise(own, hidden, att, cot, gain, up_parts, down_parts, raised, seq_count, dp_count, split):
    count, width = hidden.shape
    if split:
        parts = raised // dp_count // 128
        grad_shape = (2, dp_count // 2, seq_count, parts, width // seq_count, 128)
    else:
        grad_shape = (width, raised)
    chunk = min(512, count)
    cfg = (seq_count, dp_count, split, chunk, len(up_parts), len(down_parts))
    grads = outs_of(grad_shape, split)
    up_shape, down_shape = (width, width + raised), (raised, width)
    anywhere = pl.BlockSpec(memory_space=pl.ANY)
    return pl.pallas_call(
        functools.partial(rise_kernel, cfg),
        in_specs=[pl.BlockSpec(memory_space=pltpu.SMEM)]
        + [IN_VMEM] * 4
        + [anywhere] * (len(up_parts) + len(down_parts)),
        out_specs=[IN_VMEM] * 6 + [anywhere] * len(grads),
        scratch_shapes=[
            pltpu.VMEM((count, raised), BF16),
            pltpu.VMEM((width, count), BF16),
            pltpu.VMEM(grad_shape, BF16),
            pltpu.SemaphoreType.DMA(((width + raised) // 512, copies_of(up_parts))),
            pltpu.SemaphoreType.DMA((copies_of(down_parts),)),
            pltpu.SemaphoreType.DMA((dp_count,)),
        ],
        out_shape=[
            jax.ShapeDtypeStruct((count, width), BF16),
            jax.ShapeDtypeStruct((count, width), F32),
            jax.ShapeDtypeStruct((count, 128), F32),
            jax.ShapeDtypeStruct((count, raised), BF16),
            jax.ShapeDtypeStruct(up_shape, BF16),
            jax.ShapeDtypeStruct(down_shape, BF16),
        ]
        + grads,
        compiler_params=params(12),
        cost_estimate=cost(7 * 2**30, 24 * 2**20),
        name="rise",
    )(own, hidden, att, cot, gain, *up_parts, *down_parts)


def fall_kernel(
    cfg,
    own_ref,
    cot_ref,
    slope_ref,
    normed_ref,
    scale_ref,
    att_ref,
    den_ref,
    gain_ref,
    w_up,
    w_down,
    first_ref,
    scaled_ref,
    extra_ref,
    gain_sum_ref,
    *refs,
):
    seq_count, dp_count, split, chunk = cfg
    outs = 2 if split else 1
    grad_outs, (raise_ref, normed_t, att_t, branch_ref, grad_ref, out_sems) = (
        refs[:outs],
        refs[outs:],
    )
    count, width = cot_ref.shape
    raised = raise_ref.shape[1]
    gain = gain_ref[...]
    lane = lax.broadcasted_iota(jnp.int32, (128, width), 1)
    spread = lax.broadcasted_iota(jnp.int32, (128, width), 0) == 16 * (lane // 64)
    spread = jnp.where(spread, 1.0, 0.0).astype(BF16)
    spread = jnp.concatenate((spread, spread))
    row = lax.broadcasted_iota(jnp.int32, (128, 128), 0)
    col = lax.broadcasted_iota(jnp.int32, (128, 128), 1)
    swap = jnp.where((row < 64) != (col < 64), 1.0, 0.0).astype(BF16)
    swap = jnp.concatenate((swap, swap))
    even = lax.broadcasted_iota(jnp.int32, (1, 128), 1) % 2 == 0
    gain_sum = jnp.zeros((1, width), F32)
    att_t[...] = att_ref[...].T
    for top in range(0, count, chunk):
        at = slice(top, top + chunk)
        cot = cot_ref[at, :]
        normed = normed_ref[at, :]
        normed_t[:, at] = (normed * gain).astype(BF16).T
        back = jnp.zeros((chunk, width), F32)
        for start in range(0, raised, 512):
            stop = start + 512
            grad_raised = (nt(cot, w_down[start:stop, :]) * slope_ref[at, start:stop]).astype(BF16)
            raise_ref[at, start:stop] = grad_raised
            back = back + nt(grad_raised, w_up[:, width + start : width + stop])
        gain_sum = gain_sum + jnp.sum(back * normed, axis=0, keepdims=True)
        grad_first = cot.astype(F32) + norm_back(back * gain, normed, scale_ref[at, :1])
        first_ref[at, :] = grad_first
        branch = grad_first.astype(BF16)
        branch_ref[at, :] = branch
        den = den_ref[at, :]
        coarse = den.astype(BF16)
        fine = (den - coarse.astype(F32)).astype(BF16)
        terms = jnp.concatenate((coarse, fine), axis=1)
        ratio = nt(branch, w_up[:, :width]) / nn(terms, spread)
        scaled_ref[at, :] = ratio.astype(BF16)
        product = ratio * att_ref[at, :]
        coarse = product.astype(BF16)
        fine = (product - coarse.astype(F32)).astype(BF16)
        for start in range(0, width, 128):
            stop = start + 128
            terms = jnp.concatenate((coarse[:, start:stop], fine[:, start:stop]), axis=1)
            offset = nn(terms, swap)
            upper = offset.astype(BF16)
            lower = (offset - upper.astype(F32)).astype(BF16)
            extra_ref[at, start:stop] = jnp.where(even, upper, lower)
    gain_sum_ref[...] = gain_sum
    if not split:
        grad_ref[:, :width] = nn(att_t[...], branch_ref[...]).astype(BF16)
        for start in range(0, raised, 512):
            grad_ref[:, width + start : width + start + 512] = nn(
                normed_t[...], raise_ref[:, start : start + 512]
            ).astype(BF16)
        hand_out(grad_ref, grad_outs, out_sems)
        return
    cols = raised // seq_count
    wide = width // seq_count
    rows = width // dp_count
    copies = []

    def keep(result, s, at):
        for d in range(dp_count):
            grad_ref[(d % 2) ^ own_ref[2], s ^ own_ref[0], (d // 2) ^ own_ref[1], :, at] = result[
                d * rows : (d + 1) * rows, :
            ]

    result = nn(att_t[...], branch_ref[...]).astype(BF16)
    for s in range(seq_count):
        keep(result[:, s * wide : (s + 1) * wide], s, slice(0, wide))
    for s in range(seq_count):
        result = nn(normed_t[...], raise_ref[:, s * cols : (s + 1) * cols]).astype(BF16)
        keep(result, s, slice(wide, wide + cols))
        for core in range(2):
            copy = pltpu.make_async_copy(
                grad_ref.at[core, s ^ own_ref[0]],
                grad_outs[core].at[s ^ own_ref[0]],
                out_sems.at[len(copies)],
            )
            copies.append(copy)
            copy.start()
    finish(copies)


def fall(own, cot, slope, normed, scale, att, den, gain, w_up, w_down, seq_count, dp_count, split):
    count, width = cot.shape
    raised = w_down.shape[0]
    if split:
        grad_shape = (2, seq_count, dp_count // 2, width // dp_count, (width + raised) // seq_count)
    else:
        grad_shape = (width, width + raised)
    grads = outs_of(grad_shape, split)
    cfg = (seq_count, dp_count, split, min(512, count))

    def sds(dtype):
        return jax.ShapeDtypeStruct((count, width), dtype)

    return pl.pallas_call(
        functools.partial(fall_kernel, cfg),
        in_specs=[pl.BlockSpec(memory_space=pltpu.SMEM)] + [IN_VMEM] * 9,
        out_specs=[IN_VMEM] * 4 + [pl.BlockSpec(memory_space=pl.ANY)] * len(grads),
        scratch_shapes=[
            pltpu.VMEM((count, raised), BF16),
            pltpu.VMEM((width, count), BF16),
            pltpu.VMEM((width, count), BF16),
            pltpu.VMEM((count, width), BF16),
            pltpu.VMEM(grad_shape, BF16),
            pltpu.SemaphoreType.DMA((2 * seq_count,)),
        ],
        out_shape=[
            sds(F32),
            sds(BF16),
            sds(BF16),
            jax.ShapeDtypeStruct((1, width), F32),
        ]
        + grads,
        compiler_params=params(14),
        cost_estimate=cost(4 * (8 * 2**30), 4 * (24 * 2**20)),
        name="fall",
    )(own, cot, slope, normed, scale, att, den, gain, w_up, w_down)


def last_kernel(chunk, hidden_ref, first_ref, gain_ref, mask_ref, w_ref, *refs):
    *grads, out_ref, sums_ref = refs
    masked = gain_sum = 0.0
    for top in range(0, hidden_ref.shape[0], chunk):
        at = slice(top, top + chunk)
        back = 0.0
        start = 0
        for ref in grads:
            stop = start + ref.shape[1]
            back = back + nt(ref[at, :], w_ref[:, start:stop])
            start = stop
        normed, scale = norm_parts(hidden_ref[at, :])
        grad = first_ref[at, :] + norm_back(back * gain_ref[...], normed, scale)
        coarse = grad.astype(BF16)
        out_ref[at, :] = coarse
        fine = (grad - coarse.astype(F32)).astype(BF16)
        mask = mask_ref[:, at]
        masked = masked + nn(mask, coarse) + nn(mask, fine)
        gain_sum = gain_sum + jnp.sum(back * normed, axis=0, keepdims=True)
    sums_ref[...] = masked
    sums_ref[1:2, :] = gain_sum


def last(hidden, grad_first, gain, mask, w_qkv, grads):
    count, width = hidden.shape
    return pl.pallas_call(
        functools.partial(last_kernel, min(512, count)),
        in_specs=[IN_VMEM] * (5 + len(grads)),
        out_specs=[IN_VMEM] * 2,
        out_shape=[
            jax.ShapeDtypeStruct((count, width), BF16),
            jax.ShapeDtypeStruct((8, width), F32),
        ],
        compiler_params=params(8),
        cost_estimate=cost(8 * (6 * count * width * width), 8 * (12 * 2**20)),
        name="last",
    )(hidden, grad_first, gain, mask, w_qkv, *grads)


def swap_along(value, axis, mask):
    count = lax.axis_size(axis)
    return lax.ppermute(value, axis, [(i, i ^ mask) for i in range(count)])


def add_up(values):
    total = values[0].astype(F32)
    for value in values[1:]:
        total = total + value.astype(F32)
    return total


def together(*values):
    return lax.optimization_barrier(values)


def from_plane(values):
    return [values[0]] + [swap_along(values[j], "seq", j) for j in range(1, len(values))]


def from_line(values):
    return [values[0]] + [swap_along(values[j], "dp", 2 * j) for j in range(1, len(values))]


def other_core(value):
    return swap_along(value, "dp", 1)


def add_split(left, right):
    return [add_up((left[j], right[j])).astype(BF16) for j in range(left.shape[0])]


def both_cores(value):
    return [value, other_core(value)]


def split_first(value):
    return [value[j] for j in range(value.shape[0])]


def halve_line(value):
    half = value.shape[0] // 2
    while half:
        came = swap_along(value[half:], "dp", 2 * half)
        value = add_up((value[:half], came))
        half //= 2
        if half:
            value = value.astype(BF16)
    return value[0]


def gather_line(value):
    return jnp.stack(from_line([value] * (lax.axis_size("dp") // 2)))


def gather_plane(value):
    return jnp.stack(from_plane([value] * lax.axis_size("seq")))


def own_columns(weight):
    cols = weight.shape[1] // lax.axis_size("seq")
    return lax.dynamic_slice_in_dim(weight, lax.axis_index("seq") * cols, cols, 1)


def pieces_of(whole, own, seq_count, dp_count, flipped):
    row_blocks, col_blocks = (seq_count, dp_count) if flipped else (dp_count, seq_count)
    rows, cols = whole.shape[0] // row_blocks, whole.shape[1] // col_blocks
    whole = whole.reshape(row_blocks, rows, col_blocks, cols)
    whole = jnp.transpose(whole, (0, 2, 1, 3) if flipped else (2, 0, 1, 3))
    whole = whole.reshape(seq_count, dp_count // 2, 2, rows, cols)
    whole = jnp.take(whole, jnp.arange(seq_count) ^ own[0], axis=0)
    whole = jnp.take(whole, jnp.arange(dp_count // 2) ^ own[1], axis=1)
    whole = jnp.take(whole, jnp.arange(2) ^ own[2], axis=2)
    return jnp.transpose(whole, (2, 0, 1, 3, 4))


def per_device(
    inputs,
    cotangent,
    timestep,
    unmask_order,
    mask_embed,
    ln1_gain,
    weight_qkv,
    weight_out,
    ln2_gain,
    weight_up,
    weight_down,
):
    rows, segment, width = inputs.shape
    raised = weight_up.shape[1]
    seq_count, dp_count = lax.axis_size("seq"), lax.axis_size("dp")
    outer = seq_count // rows
    split = outer == 1 and (seq_count, dp_count) == (4, 8)
    place = lax.axis_index("seq")
    dp_place = lax.axis_index("dp")
    row = place % rows
    own = jnp.stack([place, dp_place // 2, dp_place % 2]).astype(jnp.int32)

    def by_partner(value):
        return [lax.dynamic_index_in_dim(value, row ^ j, 0, keepdims=False) for j in range(rows)]

    def to_rows(value):
        return jnp.concatenate(from_plane(by_partner(value)))

    def to_partners(value):
        return from_plane([value[j * segment : (j + 1) * segment] for j in range(rows)])

    def by_row(parts):
        out = jnp.zeros((rows,) + parts[0].shape, parts[0].dtype)
        for j in (0, 3, 2, 1) if rows == 4 else range(rows):
            out = lax.dynamic_update_index_in_dim(out, parts[j], row ^ j, 0)
        return out

    masked = (unmask_order <= timestep[:, None]).astype(BF16)
    masked = jnp.pad(masked[:, None, :], ((0, 0), (0, 15), (0, width - segment)))
    came = by_partner(jnp.concatenate((inputs, masked), axis=1))
    up_and_out = jnp.concatenate((weight_out, weight_up), axis=1)
    if split:
        down_rows = weight_down.shape[0] // seq_count
        own_down = lax.dynamic_slice_in_dim(weight_down, place * down_rows, down_rows, 0)
        line = gather_line(jnp.concatenate((own_columns(weight_qkv), own_down), axis=1))
        came = from_plane(came)
        line, up_and_out = together(line, up_and_out)
        line_up = jnp.stack((up_and_out, swap_along(up_and_out, "dp", 4)))
        line_up = [line_up, swap_along(line_up, "dp", 2)]
        plane_qkv = gather_plane(line[..., :-width])
        line_down = line[..., -width:].reshape(-1, width)
        cot = cotangent
        parts_qkv = both_cores(plane_qkv)
        cot = from_plane([jnp.concatenate((part, line_down)) for part in by_partner(cot)])
    else:
        came, cot = from_plane(came), from_plane(by_partner(cotangent))
        parts_qkv, parts_up, parts_down = (
            [lax.all_gather(weight, "dp", axis=0, tiled=True)]
            for weight in (weight_qkv, up_and_out, weight_down)
        )

    block = jnp.concatenate([part[:segment] for part in came]).astype(F32)
    mask_row = jnp.concatenate([part[segment, :segment] for part in came])
    hidden = block + mask_row.astype(F32)[:, None] * mask_embed
    normed_one, projected, whole_qkv = project(
        own, hidden, ln1_gain[None, :], parts_qkv, 3 * width
    )
    if outer > 1:
        groups = [[j * rows + i for j in range(outer)] for i in range(rows)]
        far = lax.all_gather(
            projected[:, width:], "seq", axis=0, tiled=True, axis_index_groups=groups
        )
        attended, denominators = attend(projected, far, 0)
    else:
        attended, denominators = attend_row(projected)
    if split:
        line_up, attended = together(line_up, attended)
        parts_up = both_cores(jnp.stack(line_up, axis=1).reshape((-1,) + up_and_out.shape))
        cot, parts_up[0] = together(cot, parts_up[0])
        plane_down = jnp.stack([part[segment:] for part in cot])
        plane_down = plane_down.reshape(seq_count, dp_count // 2, -1, width)
        parts_down = both_cores(plane_down)
    cot = jnp.concatenate([part[:segment] for part in cot])
    outputs, normed, scale, slope, whole_up, whole_down, *grad_down = rise(
        own,
        hidden,
        attended,
        cot,
        ln2_gain[None, :],
        parts_up,
        parts_down,
        raised,
        seq_count,
        dp_count,
        split,
    )
    result = to_partners(outputs)
    grad_first, scaled, extra, sum_gain_two, *grad_up = fall(
        own,
        cot,
        slope,
        normed,
        scale,
        attended,
        denominators,
        ln2_gain[None, :],
        whole_up,
        whole_down,
        seq_count,
        dp_count,
        split,
    )
    mask_rows = jnp.broadcast_to(mask_row[None, :], (8, mask_row.shape[0]))
    if split:
        grad_down[1] = other_core(grad_down[1])
        grad_down, scaled, grad_up, result = together(grad_down, scaled, grad_up, result)
        line_down = from_line(add_split(*grad_down))
        grad_up[1] = other_core(grad_up[1])
        half = attend_back_half(projected, scaled, extra)
        grad_up, half, line_down[1] = together(grad_up, half, line_down[1])
        plane_up = from_plane(add_split(*grad_up))
        *rest, mine_qkv, other_qkv = attend_back_sum(
            own, projected, scaled, extra, normed_one, half, seq_count, dp_count
        )
        plane_up, line_down, rest, mine_qkv, other_qkv = together(
            plane_up, line_down, rest, mine_qkv, other_qkv
        )
        grads = [part for pair in zip(half, rest) for part in pair]
        both_qkv = (mine_qkv, other_core(other_qkv))
        line_up = add_up(plane_up).astype(BF16)
        z_half = line_up.shape[0] // 2
        line_came = swap_along(line_up[z_half:], "dp", 2 * z_half)
        tall = width // dp_count
        down = add_up(line_down).astype(BF16).reshape(seq_count, -1, tall, 128)
        both_qkv, mask_rows = together(both_qkv, mask_rows)
        mine_qkv = [part.reshape(-1, tall, 128) for part in add_split(*both_qkv)]
        plane_last = from_plane([jnp.concatenate((mine_qkv[j], down[j])) for j in range(seq_count)])
    else:
        dq, dk, dv = attend_back(projected, far, scaled, extra)
        both = jnp.concatenate((dk, dv), axis=1)
        both = lax.psum_scatter(
            both, "seq", scatter_dimension=0, tiled=True, axis_index_groups=groups
        )
        grads = [dq, both]
        grad_qkv = lax.dot_general(
            normed_one,
            jnp.concatenate(grads, axis=1),
            (((0,), (0,)), ((), ())),
            preferred_element_type=F32,
        ).astype(BF16)
        cut = functools.partial(pieces_of, own=own, seq_count=seq_count, dp_count=dp_count)
        (grad_up,), (grad_down,) = grad_up, grad_down
        grad_out, grad_up = (
            cut(part, flipped=False) for part in (grad_up[:, :width], grad_up[:, width:])
        )
        grad_up = jnp.concatenate((grad_out, grad_up), axis=-1)
        grad_qkv = cut(grad_qkv, flipped=False)
        grad_down = cut(grad_down, flipped=True)
        sums = []
        for pieces in (grad_qkv, grad_up, grad_down):
            mine = add_up((pieces[0], other_core(pieces[1]))).astype(BF16)
            plane = add_up(from_plane(split_first(mine))).astype(BF16)
            sums.append(add_up(from_line(split_first(plane))))
        sum_qkv, sum_up, sum_down = sums
        sum_down = sum_down.T
    grad_hidden, sums = last(
        hidden, grad_first, ln1_gain[None, :], mask_rows, whole_qkv, grads
    )
    vectors = jnp.concatenate((sums[0:2], sum_gain_two, jnp.zeros((5, width), F32)), axis=0)
    vectors = vectors + other_core(vectors)
    bit = 2
    while bit < dp_count:
        vectors = vectors + swap_along(vectors, "dp", bit)
        bit *= 2
    if split:
        grad_hidden, vectors, line_came, plane_last = together(
            grad_hidden, vectors, line_came, plane_last
        )
        sum_up = add_up((line_up[:z_half], line_came)).astype(BF16)
        kinds = mine_qkv[0].shape[0]
        sum_qkv = add_up([part[:kinds] for part in plane_last]).astype(BF16)
        sum_qkv = sum_qkv.reshape((dp_count // 2, -1) + sum_qkv.shape[1:])
        line_came = swap_along(sum_qkv[z_half:], "dp", 2 * z_half)
        line_came, plane_last, sum_up = together(line_came, plane_last, sum_up)
        sum_qkv = halve_line(add_up((sum_qkv[:z_half], line_came)).astype(BF16))
        sum_up = halve_line(sum_up)
        sum_down = add_up([part[kinds:] for part in plane_last])
        sum_down = sum_down.reshape(-1, width // seq_count, 128)
        sum_down = jnp.transpose(sum_down, (0, 2, 1)).reshape(-1, width // seq_count)
        sum_qkv = jnp.transpose(sum_qkv, (1, 0, 2)).reshape(tall, -1)
    grad_inputs = [grad_hidden[j * segment : (j + 1) * segment] for j in range(rows)]
    if split:
        coarse = vectors.astype(BF16)
        terms = jnp.concatenate((coarse, (vectors - coarse.astype(F32)).astype(BF16)))
        grad_inputs = [jnp.concatenate((part, terms)) for part in grad_inputs]
    grad_inputs = from_plane(grad_inputs)
    if split:
        vectors = add_up([part[segment:] for part in grad_inputs])
        vectors = vectors[:8] + vectors[8:]
        grad_inputs = [part[:segment] for part in grad_inputs]
    else:
        vectors = add_up(from_plane([vectors] * seq_count))
    block_width = width // dp_count
    vectors = lax.dynamic_slice_in_dim(vectors, dp_place * block_width, block_width, 1)
    out_cols = width // seq_count
    return (
        by_row(result),
        by_row(grad_inputs),
        vectors[0],
        vectors[1],
        sum_qkv,
        sum_up[:, :out_cols],
        vectors[2],
        sum_up[:, out_cols:],
        sum_down,
    )


def solution(mesh):
    in_specs = (
        P("dp", "seq", None),
        P("dp", "seq", None),
        P("dp"),
        P("dp", "seq"),
        P(),
        P(),
        P("dp", None),
        P("dp", None),
        P(),
        P("dp", None),
        P("dp", None),
    )
    out_specs = (
        P("dp", "seq", None),
        P("dp", "seq", None),
        P("dp"),
        P("dp"),
        P("dp", "seq"),
        P("dp", "seq"),
        P("dp"),
        P("dp", "seq"),
        P("dp", "seq"),
    )
    return jax.shard_map(
        per_device, mesh=mesh, in_specs=in_specs, out_specs=out_specs, check_vma=False
    )
```
